32 devices in a mesh: sec: 2 (over y), gx: 2 (over x), gy: 8 (over z, core).
Axes of the slice: x: 2, y: 2, z: 4, core: 2. Of those that a mesh axis runs over, the one named last changes fastest.
Arguments:
- state: float32 [2, 3, 2, 8, 102400], P('sec', None, 'gx', 'gy'), may hold values from -6 to 6
- previous: float32 [2, 3, 2, 8, 102400], P('sec', None, 'gx', 'gy'), may hold values from -6 to 6
- coeff: float32 [2, 2, 2, 8, 102400], P('sec', None, 'gx', 'gy'), may hold values from 0.04 to 0.16
- wet_mask: int32 [2, 8, 102400], P('gx', 'gy'), may hold values 0 or 1
- link_dest: int32 [2, 2, 8, 32, 1], P('sec', 'gx', 'gy'), may hold values from 0 to 15; in each aligned block of 32 rows (0 to 31, 32 to 63, ..., all dimensions but the last counted through in order) at most 4 rows name the same one
- link_rows: int32 [2, 2, 8, 32, 2], P('sec', 'gx', 'gy'), may hold values from 0 to 79, as said below
- link_weight: float32 [2, 2, 8, 32], P('sec', 'gx', 'gy'), may hold values from 0.5 to 2
Outputs:
- final_state: float32 [2, 3, 2, 8, 102400], P('sec', None, 'gx', 'gy')
The draws below stay inside these ranges and needn't reach their ends.
Inputs may be any that keep to these rules, and one draw needn't show every extreme that they name: `link_rows`: in section 0, [..., 0] lies below 8 and [..., 1] below 80; in section 1, [..., 0] lies below 80 and [..., 1] below 8. `link_dest`: among the 32 links of one device at most 4 name the same owner.
All inputs are finite; a program needn't handle non-finite values. No bound on the sum of `wet_mask` on one device may be relied on, other than what follows from the above.
Results may differ from the reference program's by a relative error of at most 0.0001.
Values sent between devices are 32-bit elements; how exact they have to be, the bound alone decides.
No kernel may reach another device: no remote copies, remote signals or barrier semaphores. Data moves between devices by JAX's collectives and lax.ppermute only.
A program may use at most 128 MiB of HBM per device.

```python
import math
import jax
import jax.numpy as jnp
import numpy as np
from jax import lax

CX = 8
CY = 128
REFINE = 10
NL = 100
STEPS = 4
CAP = 4
LINKS = 32
NXG = 16
NYG = 1024
N_GX = 2
N_GY = 8


def draw_link_rows(key, part):
    shape = (2, N_GX, N_GY, LINKS)
    first_key, second_key = jax.random.split(key)
    source_bound = jnp.array([CX, REFINE * CX], dtype=jnp.int32)[:, None, None, None]
    landing_bound = jnp.array([REFINE * CX, CX], dtype=jnp.int32)[:, None, None, None]
    source_rows = jax.random.randint(first_key, shape, 0, 1 << 30, dtype=jnp.int32) % source_bound
    landing = jax.random.randint(second_key, shape, 0, 1 << 30, dtype=jnp.int32) % landing_bound
    source_rows = source_rows.at[1, 0, 0, 0].set(REFINE * CX - 1)
    landing = landing.at[0, 0, 0, 0].set(REFINE * CX - 1)
    return jnp.stack([source_rows, landing], axis=-1)


def plant(drawn, rng, smallest, high):
    index_at = [jax.random.randint(jax.random.fold_in(rng, axis), (), 0, length) for axis, length in enumerate(drawn.shape)]
    widest = drawn.shape.index(max(drawn.shape))
    beside = index_at[:widest] + [(index_at[widest] + 1) % drawn.shape[widest]] + index_at[widest + 1:]
    return drawn.at[tuple(index_at)].set(smallest).at[tuple(beside)].set(high)


def block_levels(own_key, shape, shards, smallest, top_value):
    level, own = 1.0, jax.random.fold_in(own_key, 6)
    for dim, blocks in shards:
        steps = jnp.exp(jax.random.uniform(jax.random.fold_in(own, dim), (blocks,), jnp.float32, smallest / len(shards), top_value / len(shards)))
        level = level * jnp.repeat(steps, shape[dim] // blocks).reshape([-1 if axis == dim else 1 for axis in range(len(shape))])
    return level


def deal_out(own_key, own, number, rows, number_of, top, most, lean):
    sequence = jax.random.permutation(own_key, number_of)
    heavy_load, usual = portions_of(number_of, rows * top, most, lean, True), portions_of(number_of, rows * top, most, lean, False)
    places = jnp.arange(number_of)

    def named(lengths, rotation):
        used = int((lengths > 0).sum())
        fixed = max(1, used // 4)
        shifted = fixed + (places - fixed + rotation * (used - fixed)) % max(1, number_of - fixed)
        return jnp.zeros((number_of,), jnp.int32).at[sequence[jnp.where(places < fixed, places, shifted)]].set(jnp.asarray(lengths, jnp.int32))

    lengths = jnp.where(number % 4 == 0, named(heavy_load, number // 4), named(usual, number - number // 4 - 1))
    mixed = jax.random.permutation(jax.random.fold_in(own, 3), number_of)
    giver, taker = mixed[0:number_of // 2 * 2:2], mixed[1:number_of // 2 * 2:2]
    slack = jnp.minimum(lengths[giver] - 1, most - lengths[taker]) // 2
    slack = jnp.where((giver == sequence[0]) | (taker == sequence[0]) | (lengths[taker] == 0), 0, jnp.maximum(slack, 0))
    shifted = jax.random.randint(jax.random.fold_in(own, 4), (number_of // 2,), 0, 1 << 20) % (slack + 1)
    lengths = lengths.at[giver].add(-shifted).at[taker].add(shifted)
    items = jnp.searchsorted(jnp.cumsum(lengths), jnp.arange(rows * top), side="right").astype(jnp.int32)
    listing = items.reshape(top, rows).T
    listing = listing[jax.random.permutation(jax.random.fold_in(own, 1), rows)]
    rotation = jax.random.randint(jax.random.fold_in(own, 2), (rows, 1), 0, top)
    return jnp.take_along_axis(listing, (jnp.arange(top)[None, :] + rotation) % top, axis=1)


def portions_of(number_of, total, limit, skew, full):
    loads = [(1 << 20) // math.isqrt(rank ** skew) + 1 for rank in range(1, number_of + 1)]
    largest = limit if full else min(limit, max(-(-total // number_of), total * loads[0] // sum(loads)))
    least = 1 if total - largest >= number_of - 1 else 0
    holding, rest = [largest] + [least] * (number_of - 1), total - largest - least * (number_of - 1)
    while rest > 0:
        candidates = [i for i in range(1, number_of) if holding[i] < largest] or [i for i in range(1, number_of) if holding[i] < limit]
        mass, budget = sum([loads[i] for i in candidates]), rest
        for i in candidates:
            more = min(limit - holding[i], max(1, budget * loads[i] // mass), rest)
            holding[i] = holding[i] + more
            rest = rest - more
    return np.array(holding)


def centred(own_key, shape, deviation, limit, shards=(), kind=jnp.bfloat16):
    level = block_levels(own_key, shape, shards, -0.22, 0.18) if shards else 1.0
    drawn = jax.random.normal(own_key, shape, jnp.float32) * deviation * level
    return jnp.minimum(jnp.maximum(drawn, -limit), limit).astype(kind)


def setup_inputs(seed: int = 0) -> dict:
    splits = jax.random.split(jax.random.key(seed), 8)
    state = centred(splits[0], (2, 3, N_GX, N_GY, CX * NL * CY), 1.0, 6.0, ((0, 2), (2, 2), (3, 8)), jnp.float32)
    previous = centred(splits[1], (2, 3, N_GX, N_GY, CX * NL * CY), 1.0, 6.0, ((0, 2), (2, 2), (3, 8)), jnp.float32)
    coeff = jnp.clip(0.04 + 0.12 * jax.random.uniform(splits[2], (2, 2, N_GX, N_GY, CX * NL * CY), jnp.float32) ** block_levels(splits[2], (2, 2, N_GX, N_GY, CX * NL * CY), ((0, 2), (2, 2), (3, 8)), -0.2, 0.2), 0.04, 0.16)
    wet_mask = plant((jax.random.randint(splits[3], (N_GX, N_GY, REFINE * CX * REFINE * CY), 0, 4) < 3).astype(jnp.int32), jax.random.fold_in(splits[3], 1), 0, 1)
    link_dest_keys = jax.random.split(jax.random.fold_in(splits[4], 1), 2 * N_GX * N_GY * LINKS // LINKS)
    link_dest_turns = jax.random.permutation(jax.random.fold_in(splits[4], 3), 2 * N_GX * N_GY * LINKS // LINKS)
    link_dest = jax.vmap(lambda own, number: deal_out(jax.random.fold_in(splits[4], 2), own, number, LINKS, N_GX * N_GY, 1, CAP, 2))(link_dest_keys, link_dest_turns).reshape((2, N_GX, N_GY, LINKS, 1))
    link_rows = draw_link_rows(jax.random.fold_in(splits[7], 71), 0)
    link_weight = jnp.clip(jnp.exp(math.log(2.0) - 1.3862944 * jax.random.uniform(splits[6], (2, N_GX, N_GY, LINKS), jnp.float32) ** block_levels(splits[6], (2, N_GX, N_GY, LINKS), ((0, 2), (1, 2), (2, 8)), -0.2, 0.2)), 0.5, 2.0)
    return dict(state=state, previous=previous, coeff=coeff, wet_mask=wet_mask, link_dest=link_dest, link_rows=link_rows, link_weight=link_weight)


def second_along(values, axis_index):
    widths = [(1, 1) if dim_index == axis_index else (0, 0) for dim_index in range(values.ndim)]
    padded = jnp.pad(values, widths)
    extent = values.shape[axis_index]
    forward_part = lax.slice_in_dim(padded, 2, extent + 2, axis=axis_index)
    backward_part = lax.slice_in_dim(padded, 0, extent, axis=axis_index)
    return forward_part - 2.0 * values + backward_part


def difference_along(values, axis_index):
    widths = [(1, 1) if dim_index == axis_index else (0, 0) for dim_index in range(values.ndim)]
    padded = jnp.pad(values, widths)
    extent = values.shape[axis_index]
    forward_part = lax.slice_in_dim(padded, 2, extent + 2, axis=axis_index)
    backward_part = lax.slice_in_dim(padded, 0, extent, axis=axis_index)
    return forward_part - backward_part


def to_elastic(blocks, count):
    return blocks.reshape(count, N_GX, N_GY, CX, NL, CY).transpose(0, 1, 3, 4, 2, 5).reshape(count, NXG, NL, NYG)


def from_elastic(field, count):
    return field.reshape(count, N_GX, CX, NL, N_GY, CY).transpose(0, 1, 4, 2, 3, 5).reshape(count, N_GX, N_GY, CX * NL * CY)


def to_sheet(blocks, count):
    return blocks.reshape(count, N_GX, N_GY, REFINE * CX, REFINE * CY).transpose(0, 1, 3, 2, 4).reshape(count, NXG * REFINE, NYG * REFINE)


def from_sheet(sheet, count):
    return sheet.reshape(count, N_GX, REFINE * CX, N_GY, REFINE * CY).transpose(0, 1, 3, 2, 4).reshape(count, N_GX, N_GY, CX * NL * CY)


def couple(elastic_field, sheet, link_dest, link_rows, link_weight):
    fine_rows = REFINE * CX
    uplift = elastic_field[2, :, 0, :].reshape(N_GX, CX, N_GY, CY).transpose(0, 2, 1, 3)
    surface = sheet[0].reshape(N_GX, fine_rows, N_GY, REFINE * CY).transpose(0, 2, 1, 3)
    from_elastic_tiles = jnp.take_along_axis(uplift, link_rows[0, :, :, :, 0:1], axis=2) * link_weight[0][..., None]
    picked = jnp.take_along_axis(surface, link_rows[1, :, :, :, 0:1], axis=2)
    averaged = jnp.sum(picked.reshape(N_GX, N_GY, LINKS, CY, REFINE), axis=-1) / REFINE
    from_shallow_tiles = averaged * link_weight[1][..., None]
    target_shallow = (link_dest[0, :, :, :, 0] * fine_rows + link_rows[0, :, :, :, 1]).reshape(-1)
    target_elastic = (link_dest[1, :, :, :, 0] * CX + link_rows[1, :, :, :, 1]).reshape(-1)
    into_shallow = jnp.zeros((N_GX * N_GY * fine_rows, CY), jnp.float32).at[target_shallow].add(from_elastic_tiles.reshape(-1, CY))
    into_elastic = jnp.zeros((N_GX * N_GY * CX, CY), jnp.float32).at[target_elastic].add(from_shallow_tiles.reshape(-1, CY))
    into_shallow = into_shallow.reshape(N_GX, N_GY, fine_rows, CY).transpose(0, 2, 1, 3).reshape(NXG * REFINE, NYG)
    into_shallow = jnp.repeat(into_shallow, REFINE, axis=1)
    into_elastic = into_elastic.reshape(N_GX, N_GY, CX, CY).transpose(0, 2, 1, 3).reshape(NXG, NYG)
    return into_elastic, into_shallow


def elastic_step(current_field, previous_field, shear_modulus, lame_first, surface_force):
    own_axis = (0, 2, 1)
    stiffness = lame_first + 2.0 * shear_modulus
    updated_list = []
    for component in range(3):
        displaced = current_field[component]
        factors = [stiffness if own_axis[component] == axis_index else shear_modulus for axis_index in range(3)]
        acceleration = factors[0] * second_along(displaced, 0) + factors[1] * second_along(displaced, 1) + factors[2] * second_along(displaced, 2)
        updated = 2.0 * displaced - previous_field[component] + acceleration
        if component == 2:
            updated = updated.at[:, 0, :].add(surface_force)
        updated_list.append(updated)
    return jnp.stack(updated_list)


def shallow_step(current_sheet, previous_sheet, wave_factor, area_factor, wetness, source):
    flux_first = wetness * (previous_sheet[1] - wave_factor * difference_along(current_sheet[0], 0))
    flux_second = wetness * (previous_sheet[2] - wave_factor * difference_along(current_sheet[0], 1))
    divergence = difference_along(current_sheet[1], 0) + difference_along(current_sheet[2], 1)
    height = wetness * (previous_sheet[0] - area_factor * divergence + source)
    return jnp.stack([height, flux_first, flux_second])


def reference(state, previous, coeff, wet_mask, link_dest, link_rows, link_weight):
    elastic_now = to_elastic(state[0], 3)
    elastic_before = to_elastic(previous[0], 3)
    sheet_now = to_sheet(state[1], 3)
    sheet_before = to_sheet(previous[1], 3)
    moduli = to_elastic(coeff[0], 2)
    factors = to_sheet(coeff[1], 2)
    wetness = to_sheet(wet_mask[None], 1)[0].astype(jnp.float32)
    for step_index in range(STEPS):
        into_elastic, into_shallow = couple(elastic_now, sheet_now, link_dest, link_rows, link_weight)
        elastic_new = elastic_step(elastic_now, elastic_before, moduli[0], moduli[1], into_elastic)
        sheet_new = shallow_step(sheet_now, sheet_before, factors[0], factors[1], wetness, into_shallow)
        elastic_before, elastic_now = elastic_now, elastic_new
        sheet_before, sheet_now = sheet_now, sheet_new
    return jnp.stack([from_elastic(elastic_now, 3), from_sheet(sheet_now, 3)])
```

```python
import functools

import jax
import jax.numpy as jnp
from jax import lax
from jax.experimental import pallas as pl
from jax.experimental.pallas import tpu as pltpu
from jax.sharding import PartitionSpec as P

CX = 8
CY = 128
REFINE = 10
NL = 100
STEPS = 4
CAP = 4
FINE = REFINE * CX
ROWS = CX * NL
FIRST = 104
TOTAL = FIRST + ROWS + FIRST
SLOTS = 8
GROUP = 200
F32 = jnp.float32


def dot(a, b):
    return jnp.dot(a, b, precision=lax.Precision.HIGHEST, preferred_element_type=F32)


def iota(shape, dim):
    return lax.broadcasted_iota(jnp.int32, shape, dim)


def one(mask):
    return jnp.where(mask, 1.0, 0.0).astype(F32)


def place():
    return lax.axis_index("sec"), lax.axis_index("gx"), lax.axis_index("gy")


def coarse_of(offset, shape):
    return ((iota(shape, 1) + offset) * 6554) >> 16


def average(rows_of):
    total = jnp.zeros((FINE, CY), F32)
    for m in range(REFINE):
        fine = iota((CY, CY), 0) + m * CY
        first = iota((CY, CY), 1) * REFINE
        total = total + dot(rows_of(m), one((fine >= first) & (fine < first + REFINE)))
    return total / REFINE


def surface(section, elastic, sheet, start, surf):
    surf[...] = jnp.zeros_like(surf)

    @pl.when(section == 0)
    def _():
        surf[0:CX] = elastic[pl.ds(start, CX, stride=NL)]

    @pl.when(section != 0)
    def _():
        surf[0:FINE] = average(lambda m: sheet[pl.ds(start + m, FINE, stride=REFINE)])


def source_pick(cols):
    return one(cols[0] == iota((cols.shape[1], CY), 1).astype(F32))


def outgoing(section, tiles, cols, pcat, payload):
    half = payload.shape[0] // 2
    lanes = tiles.shape
    last = jnp.broadcast_to(tiles[:, CY - 1 : CY], lanes) * cols[1]
    first = jnp.broadcast_to(tiles[:, 0:1], lanes) * cols[1]
    packed = dot(pcat[...], jnp.concatenate([tiles, last, first, cols[3]], axis=0))
    payload[pl.ds(pl.multiple_of(section * half, 8), half)] = jnp.zeros((half, CY), F32)
    payload[pl.ds(pl.multiple_of((1 - section) * half, 8), half)] = packed


def first_kernel(n_gy, state, dest, rows, weight, payload, cols, pcat, field, surf, lines, sem):
    section, p, q = place()
    links = dest.shape[1]
    copy = pltpu.make_async_copy(state.at[2 * (1 - section)], field, sem)
    copy.start()
    lines[...] = jnp.zeros_like(lines)
    lines[0:1, 0:links] = dest[...].astype(F32)
    lines[1:3, 0:links] = rows[...].astype(F32)
    lines[3:4, 0:links] = weight[...]
    x = lines[...]
    eye = one(iota((links, CY), 0) == iota((links, CY), 1))

    def column(i):
        return jnp.sum(eye * x[i : i + 1], axis=1, keepdims=True)

    target, source, landing, weights = [column(i) for i in range(4)]
    same = one(target == x[0:1])
    at = iota((links, CY), 0)
    other = iota((links, CY), 1)
    inside = one(other < links)
    slot_row = jnp.sum(same * one(at < other) * inside, axis=0, keepdims=True)
    slot = jnp.sum(same * one(other < at) * inside, axis=1, keepdims=True)
    lane = other.astype(F32)
    cols[0] = jnp.broadcast_to(source, (links, CY))
    cols[1] = one(landing == lane)
    cols[2] = jnp.broadcast_to(weights, (links, CY))
    me = ((p * n_gy + q) * SLOTS).astype(F32)
    cols[3] = landing * one(lane == slot + me)
    y = jnp.concatenate([x[0:3], slot_row, jnp.zeros((4, CY), F32)], axis=0)
    y = y + pltpu.roll(y, links, 1) + pltpu.roll(y, 2 * links, 1) + pltpu.roll(y, 3 * links, 1)
    shape = (pcat.shape[0], CY)
    owner = iota(shape, 0) >> 3
    part = iota(shape, 0) & 7
    group = iota(shape, 1) >> (links.bit_length() - 1)
    to = y[0:1]
    row = y[2:3]
    order = y[3:4]
    beside = jnp.where(owner < n_gy, owner + n_gy, owner - n_gy).astype(F32)
    bottom = jnp.where(section == 0, FINE - 1, CX - 1).astype(F32)
    edge = jnp.where(owner < n_gy, 0.0, bottom)
    along = owner & (n_gy - 1)
    own = owner.astype(F32)
    chosen = one((group == 0) & (part == order.astype(jnp.int32)) & (part < CAP) & (to == own))
    chosen += one((group == 0) & (part == 4) & (to == beside) & (row == edge))
    chosen += one((group == 1) & (part == 6) & (to == own - 1.0) & (along > 0))
    chosen += one((group == 2) & (part == 7) & (to == own + 1.0) & (along < n_gy - 1))
    chosen += one((group == 3) & (part == 5) & (to == own))
    pcat[...] = chosen
    copy.wait()
    surface(section, field, field, 0, surf)
    tiles = cols[2] * dot(source_pick(cols), surf[...])
    outgoing(section, tiles, cols, pcat, payload)


def arrived_rows(section, received):
    half = received.shape[0] // 2
    return received[pl.ds(pl.multiple_of((1 - section) * half, 8), half)]


def arrived_sums(arrived):
    return jnp.sum(arrived.reshape(-1, SLOTS, CY), axis=0)


def route_kernel(received, base, scale, cols, pcat, payload):
    section, _, _ = place()
    arrived = arrived_rows(section, received)
    landing = arrived_sums(arrived)[5:6]
    lane = iota(cols.shape[1:], 1)
    gather = one((cols[0] == landing) & ((lane & 7) < CAP))
    tiles = base[...] + scale[...] * dot(gather, arrived)
    outgoing(section, tiles, cols, pcat, payload)


def take_edges(section, p, fields, extra, xs):
    for c in range(3):

        @pl.when(p == 0)
        def _():
            xs[c] = fields[c, ROWS : ROWS + FIRST]

        @pl.when(p != 0)
        def _():
            xs[c] = fields[c, FIRST : FIRST + FIRST]

    @pl.when((section != 0) & (p == 0))
    def _():
        xs[2] = extra[2, ROWS - FIRST : ROWS]

    @pl.when((section != 0) & (p != 0))
    def _():
        xs[2] = extra[2, 0:FIRST]


def send_sides(q, left, right, ya, yb):
    odd = (q & 1) == 1

    @pl.when(odd)
    def _():
        ya[...] = left[...]
        yb[...] = right[...]

    @pl.when(jnp.logical_not(odd))
    def _():
        ya[...] = right[...]
        yb[...] = left[...]


def collect(acc, value, j, lane):
    return (
        jnp.where(lane == j, pltpu.roll(value, j, 1) if j else value, acc[0]),
        jnp.where(lane == j, pltpu.roll(value, j + 1, 1), acc[1]),
    )


def merge(it, acc, left, right):
    shift = it * (GROUP // 8)
    for c in range(3):
        left[c] += pltpu.roll(acc[c][0], shift, 1)
        right[c] += pltpu.roll(acc[c][1], shift, 1)


def load_kernel(state, previous, coeff, wet, cols, cur, prev, co, xs, ya, yb, scale, wet_in, left, right, surf, sem):
    section, p, q = place()
    own = pl.ds(FIRST, ROWS)
    copies = [pltpu.make_async_copy(wet, wet_in, sem.at[0])]
    for c in range(3):
        copies.append(pltpu.make_async_copy(state.at[c], cur.at[c, own], sem.at[1 + c]))
    for c in range(3):
        copies.append(pltpu.make_async_copy(previous.at[c], prev.at[c, own], sem.at[4 + c]))
    for c in range(2):
        copies.append(pltpu.make_async_copy(coeff.at[c], co.at[c], sem.at[7 + c]))
    for copy in copies:
        copy.start()
    left[...] = jnp.zeros_like(left)
    right[...] = jnp.zeros_like(right)
    copies[0].wait()

    def widen(g, carry):
        at = pl.ds(pl.multiple_of(g * 40, 8), 40)
        co[2, at] = wet_in[at].astype(F32)
        return carry

    lax.fori_loop(0, ROWS // 40, widen, 0)
    for copy in copies[1:4]:
        copy.wait()
    lane = iota((8, CY), 1)
    zero = jnp.zeros((8, CY), F32)

    def pack(it, carry):
        acc = [(zero, zero)] * 3
        for j in range(GROUP // 8):
            at = pl.multiple_of(it * GROUP + 8 * j, 8)
            for c in range(3):
                value = cur[c, pl.ds(FIRST + at, 8)]
                if c == 1:
                    value = jnp.where(section == 0, value, co[2, pl.ds(at, 8)])
                acc[c] = collect(acc[c], value, j, lane)
        merge(it, acc, left, right)
        return carry

    lax.fori_loop(0, ROWS // GROUP, pack, 0)
    send_sides(q, left, right, ya, yb)
    take_edges(section, p, cur, co, xs)
    scale[...] = cols[2]

    @pl.when(section != 0)
    def _():
        surf[...] = jnp.zeros_like(surf)
        surf[0:FINE] = average(lambda m: co[2, pl.ds(m, FINE, stride=REFINE)])
        scale[...] = cols[2] * dot(source_pick(cols), surf[...])

    for copy in copies[4:]:
        copy.wait()


def edge_addend(values, period, offset):
    at = iota((CY, CY), 0) * period + offset - iota((CY, CY), 1) * 8
    sub = (iota((8, CY), 1) * period + offset) & 7
    spread = jnp.where(sub == iota((8, CY), 0), jnp.broadcast_to(values, (8, CY)), 0.0)
    return dot(spread, one((at >= 0) & (at < 8)))


def step_kernel(linked, last, *refs):
    cur_in, prev_in, co, cols, xr, yra, yrb, *refs = refs
    if linked:
        received, *refs = refs
    cur, prev, *refs = refs
    if last:
        out, yl, yr, sem = refs
    else:
        base, xs, ya, yb, yl, yr, left, right, surf = refs
    section, p, q = place()
    odd = (q & 1) == 1
    lane = iota((8, CY), 1)
    sub = iota((8, CY), 0)
    zero = jnp.zeros((8, CY), F32)
    blocks = GROUP // 8

    @pl.when(odd)
    def _():
        yl[...] = yra[...]
        yr[...] = yrb[...]

    @pl.when(jnp.logical_not(odd))
    def _():
        yl[...] = yrb[...]
        yr[...] = yra[...]

    for c in range(3):

        @pl.when(p == 0)
        def _():
            cur[c, 0:FIRST] = jnp.zeros((FIRST, CY), F32)
            cur[c, FIRST + ROWS : TOTAL] = xr[c]

        @pl.when(p != 0)
        def _():
            cur[c, 0:FIRST] = xr[c]
            cur[c, FIRST + ROWS : TOTAL] = jnp.zeros((FIRST, CY), F32)

    if linked:
        arrived = arrived_rows(section, received)
        sums = arrived_sums(arrived)
        mine = iota((CY, arrived.shape[0]), 1)
        land = one((iota(mine.shape, 0).astype(F32) == sums[5:6]) & ((mine & 7) < CAP))
        addend = dot(land, arrived)
    if not last:
        left[...] = jnp.zeros_like(left)
        right[...] = jnp.zeros_like(right)

    @pl.when(section == 0)
    def _():
        if linked:
            for x in range(CX):
                cur[2, FIRST + NL * x : FIRST + NL * x + 1] += addend[x : x + 1]

            @pl.when(p == 0)
            def _():
                cur[2, FIRST + ROWS : FIRST + ROWS + 1] += sums[4:5]

            @pl.when(p != 0)
            def _():
                cur[2, FIRST - NL : FIRST - NL + 1] += sums[4:5]

            yl[2] += edge_addend(sums[6:7], NL, 0)
            yr[2] += edge_addend(sums[7:8], NL, 0)

        def group(it, carry):
            turn = (CY - blocks * it) & (CY - 1)
            lows = [pltpu.roll(yl[c], turn, 1) for c in range(3)]
            highs = [pltpu.roll(yr[c], turn, 1) for c in range(3)]
            acc = [(zero, zero)] * 3
            for j in range(blocks):
                at = pl.multiple_of(it * GROUP + 8 * j, 8)
                here = FIRST + at
                mu = co[0, pl.ds(at, 8)]
                stiff = co[1, pl.ds(at, 8)] + 2.0 * mu
                for c in range(3):
                    v = cur[c, pl.ds(here, 8)]
                    twice = 2.0 * v
                    above = cur[c, pl.ds(here - 1, 8)]
                    below = cur[c, pl.ds(here + 1, 8)]
                    for row in (0, NL):
                        if 8 * j <= row < 8 * j + 8:
                            above = jnp.where(sub == row - 8 * j, 0.0, above)
                    for row in (NL - 1, GROUP - 1):
                        if 8 * j <= row < 8 * j + 8:
                            below = jnp.where(sub == row - 8 * j, 0.0, below)
                    low = jnp.where(lane == CY - 1, pltpu.roll(lows[c], CY - 1 - j, 1), v)
                    high = jnp.where(lane == 0, pltpu.roll(highs[c], (CY - j) % CY, 1) if j else highs[c], v)
                    along_first = cur[c, pl.ds(here - NL, 8)] + cur[c, pl.ds(here + NL, 8)] - twice
                    along_depth = above + below - twice
                    along_second = pltpu.roll(low, 1, 1) + pltpu.roll(high, CY - 1, 1) - twice
                    if c == 0:
                        force = stiff * along_first + mu * (along_depth + along_second)
                    elif c == 1:
                        force = stiff * along_second + mu * (along_first + along_depth)
                    else:
                        force = stiff * along_depth + mu * (along_first + along_second)
                    new = twice - prev_in[c, pl.ds(here, 8)] + force
                    prev[c, pl.ds(here, 8)] = new
                    if not last:
                        acc[c] = collect(acc[c], new, j, lane)
            if not last:
                merge(it, acc, left, right)
            return carry

        lax.fori_loop(0, ROWS // GROUP, group, 0)

    @pl.when(section != 0)
    def _():
        for c in (0, 1, 2):
            value = yl[c]
            once = pltpu.roll(pltpu.roll(value, CY - 1, 1), 7, 0)
            again = pltpu.roll(pltpu.roll(value, CY - 2, 1), 7, 0)
            yl[c] = jnp.where(sub == 7, again, once)
            value = yr[c]
            once = pltpu.roll(pltpu.roll(value, 1, 1), 1, 0)
            again = pltpu.roll(pltpu.roll(value, 2, 1), 1, 0)
            yr[c] = jnp.where(sub == 0, again, once)
        if linked:
            yl[0] += yl[1] * edge_addend(sums[6:7], REFINE, 0)
            yr[0] += yr[1] * edge_addend(sums[7:8], REFINE, REFINE - 1)
            spread_row = jnp.broadcast_to(sums[4:5], (8, CY))
            fine_row = jnp.concatenate(
                [
                    jnp.take_along_axis(spread_row, (((sub + m) * CY + lane) * 6554) >> 16, axis=1)
                    for m in (0, 2)
                ],
                axis=0,
            )

            def add_edge(first):
                for start, rows in ((0, fine_row[0:8]), (8, fine_row[14:16])):
                    at = slice(first + start, first + start + rows.shape[0])
                    cur[0, at] += cur[2, at] * rows

            @pl.when(p == 0)
            def _():
                add_edge(FIRST + ROWS)

            @pl.when(p != 0)
            def _():
                add_edge(FIRST - REFINE)

            add_sheet(addend, cur, co)

        def group(it, carry):
            turn = (CY - blocks * it) & (CY - 1)
            lows = [pltpu.roll(yl[c], turn, 1) for c in (0, 2)]
            highs = [pltpu.roll(yr[c], turn, 1) for c in (0, 2)]
            acc = [(zero, zero)] * 3
            for j in range(blocks):
                at = pl.multiple_of(it * GROUP + 8 * j, 8)
                here = FIRST + at
                a = co[0, pl.ds(at, 8)]
                b = co[1, pl.ds(at, 8)]
                w = co[2, pl.ds(at, 8)]

                def across(c, low_side, high_side):
                    v = cur[c, pl.ds(here, 8)]
                    low = jnp.where(lane == CY - 1, cur[c, pl.ds(here - 1, 8)], v)
                    high = jnp.where(lane == 0, cur[c, pl.ds(here + 1, 8)], v)
                    for s in range(8):
                        if (8 * j + s) % REFINE == 0:
                            side = pltpu.roll(low_side, CY - 1 - j, 1)
                            low = jnp.where((lane == CY - 1) & (sub == s), side, low)
                        if (8 * j + s) % REFINE == REFINE - 1:
                            side = pltpu.roll(high_side, CY - j, 1) if j else high_side
                            high = jnp.where((lane == 0) & (sub == s), side, high)
                    return pltpu.roll(high, CY - 1, 1) - pltpu.roll(low, 1, 1)

                def down(c):
                    return cur[c, pl.ds(here + REFINE, 8)] - cur[c, pl.ds(here - REFINE, 8)]

                def before(c):
                    return prev_in[c, pl.ds(here, 8)]

                first_flux = w * (before(1) - a * down(0))
                second_flux = w * (before(2) - a * across(0, lows[0], highs[0]))
                height = w * (before(0) - b * (down(1) + across(2, lows[1], highs[1])))
                prev[0, pl.ds(here, 8)] = height
                prev[1, pl.ds(here, 8)] = first_flux
                prev[2, pl.ds(here, 8)] = second_flux
                if not last:
                    for c, value in enumerate((height, w, second_flux)):
                        acc[c] = collect(acc[c], value, j, lane)
            if not last:
                merge(it, acc, left, right)
            return carry

        lax.fori_loop(0, ROWS // GROUP, group, 0)

    if last:
        own = pl.ds(FIRST, ROWS)
        copies = [pltpu.make_async_copy(prev.at[c, own], out.at[c], sem.at[c]) for c in range(3)]
        for copy in copies:
            copy.start()
        for copy in copies:
            copy.wait()
    else:
        send_sides(q, left, right, ya, yb)
        take_edges(section, p, prev, co, xs)
        surface(section, prev.at[2], prev.at[0], FIRST, surf)
        base[...] = cols[2] * dot(source_pick(cols), surf[...])


def add_sheet(addend, fields, co):
    lane = iota((8, CY), 1)
    for m in range(FINE // 8):
        rows = addend[8 * m : 8 * m + 8]
        for k in range(REFINE):
            fine = jnp.take_along_axis(rows, ((lane + k * CY) * 6554) >> 16, axis=1)
            start = 8 * REFINE * m + k
            at = pl.ds(FIRST + start, 8, stride=REFINE)
            fields[0, at] += co[2, pl.ds(start, 8, stride=REFINE)] * fine


def last_kernel(final_in, fields, co, received, final, height, sem):
    section, _, _ = place()
    arrived = arrived_rows(section, received)
    sums = arrived_sums(arrived)
    mine = iota((CY, arrived.shape[0]), 1)
    land = one((iota(mine.shape, 0).astype(F32) == sums[5:6]) & ((mine & 7) < CAP))
    addend = dot(land, arrived)

    @pl.when(section == 0)
    def _():
        copies = []
        for x in range(CX):
            row = NL * x
            first = row // 8 * 8
            height[8 * x : 8 * x + 8] = fields[2, FIRST + first : FIRST + first + 8]
            at = 8 * x + row - first
            height[at : at + 1] += addend[x : x + 1]
            copies.append(
                pltpu.make_async_copy(
                    height.at[8 * x : 8 * x + 8], final.at[2, pl.ds(first, 8)], sem.at[x]
                )
            )
        for copy in copies:
            copy.start()
        for copy in copies:
            copy.wait()

    @pl.when(section != 0)
    def _():
        lane = iota((8, CY), 1)
        for m in range(FINE // 8):
            rows = addend[8 * m : 8 * m + 8]
            for k in range(REFINE):
                fine = jnp.take_along_axis(rows, ((lane + k * CY) * 6554) >> 16, axis=1)
                start = 8 * REFINE * m + k
                at = pl.ds(start, 8, stride=REFINE)
                height[at] = (
                    fields[0, pl.ds(FIRST + start, 8, stride=REFINE)] + co[2, at] * fine
                )
        copy = pltpu.make_async_copy(height, final.at[0], sem.at[0])
        copy.start()
        copy.wait()


def call(kernel, operands, outs, scratch=(), aliases=None, flops=0, any_inputs=(), any_outs=()):
    vmem = pl.BlockSpec(memory_space=pltpu.VMEM)
    anywhere = pl.BlockSpec(memory_space=pl.ANY)
    return pl.pallas_call(
        kernel,
        out_shape=[
            pltpu.VMEM(shape, F32) if kept else jax.ShapeDtypeStruct(shape, F32)
            for shape, kept in outs
        ],
        in_specs=[anywhere if i in any_inputs else vmem for i in range(len(operands))],
        out_specs=[anywhere if i in any_outs else vmem for i in range(len(outs))],
        scratch_shapes=list(scratch),
        input_output_aliases=aliases or {},
        compiler_params=pltpu.CompilerParams(vmem_limit_bytes=40 * 1024 * 1024),
        cost_estimate=pl.CostEstimate(flops=flops, bytes_accessed=4 * 1024 * 1024, transcendentals=0),
    )(*operands)


def keep(value):
    return pltpu.with_memory_space_constraint(value, pltpu.VMEM)


def on_device(n_gy, owners, state, previous, coeff, wet_mask, link_dest, link_rows, link_weight):
    state = state.reshape(3, ROWS, CY)
    previous = previous.reshape(3, ROWS, CY)
    coeff = coeff.reshape(2, ROWS, CY)
    wet = wet_mask.reshape(ROWS, CY)
    links = link_weight.size
    dest = link_dest.reshape(1, links)
    rows = link_rows.reshape(links, 2).T
    weight = link_weight.reshape(1, links)
    pairs = 2 * owners * SLOTS
    vmem = pltpu.VMEM
    side = vmem((3, 8, CY), F32)
    surf = vmem((CY, CY), F32)
    table = ((4, links, CY), True)
    padded = ((3, TOTAL, CY), True)
    edges = ((3, FIRST, CY), False)
    sides = ((3, 8, CY), False)
    tiles = ((links, CY), True)

    def exchange(payload):
        payload = payload.reshape(2 * owners, SLOTS, CY)
        payload = lax.all_to_all(payload, ("sec", "gx", "gy"), 0, 0, tiled=True)
        return payload.reshape(pairs, CY)

    payload, cols, pcat = call(
        functools.partial(first_kernel, n_gy),
        (state, dest, rows, weight),
        [((pairs, CY), False), table, ((owners * SLOTS, CY), True)],
        [vmem((ROWS, CY), F32), surf, vmem((8, CY), F32), pltpu.SemaphoreType.DMA],
        any_inputs=(0,),
    )
    received = exchange(payload)
    cur, prev, co, xs, ya, yb, scale = call(
        load_kernel,
        (state, previous, coeff, wet, keep(cols)),
        [padded, padded, ((3, ROWS, CY), True), edges, sides, sides, tiles],
        [vmem((ROWS, CY), jnp.int32), side, side, surf, pltpu.SemaphoreType.DMA((9,))],
        any_inputs=(0, 1, 2, 3),
    )
    swap = [(0, 1), (1, 0)]
    inner = [(i, i ^ 1) for i in range(n_gy)]
    outer = [(i, j) for k in range(1, n_gy - 1, 2) for i, j in ((k, k + 1), (k + 1, k))]
    before = None
    for step in range(STEPS):
        last = step == STEPS - 1
        xr = lax.ppermute(xs, "gx", swap)
        yra = lax.ppermute(ya, "gy", inner)
        yrb = lax.ppermute(yb, "gy", outer)
        operands = [keep(cur), keep(prev), keep(co), keep(cols), xr, yra, yrb]
        if before is not None:
            operands.append(before)
        kernel = functools.partial(step_kernel, before is not None, last)
        if last:
            _, new, final = call(
                kernel, operands, [padded, padded, ((3, ROWS, CY), False)],
                [side, side, pltpu.SemaphoreType.DMA((3,))],
                aliases={0: 0, 1: 1}, flops=4_000_000, any_outs=(2,),
            )
        else:
            old, new, base, xs, ya, yb = call(
                kernel, operands, [padded, padded, tiles, edges, sides, sides],
                [side, side, side, side, surf],
                aliases={0: 0, 1: 1}, flops=4_000_000,
            )
            cur, prev = new, old
            payload = call(
                route_kernel, (received, keep(base), keep(scale), keep(cols), keep(pcat)),
                [((pairs, CY), False)],
            )[0]
            before = received
            received = exchange(payload)
    final = call(
        last_kernel,
        (final, keep(new), keep(co), received),
        [((3, ROWS, CY), False)],
        [vmem((ROWS, CY), F32), pltpu.SemaphoreType.DMA((CX,))],
        aliases={0: 0}, any_inputs=(0,), any_outs=(0,),
    )[0]
    return final.reshape(1, 3, 1, 1, -1)


def from_partner(value, axis, stride):
    return lax.ppermute(value, axis, [(i, i ^ 1 << stride) for i in range(lax.axis_size(axis))])


def with_halo(block, sides, width):
    for axis, dim in sides:
        count = lax.axis_size(axis)
        forward = [(i, i + 1) for i in range(count - 1)]
        backward = [(target, source) for source, target in forward]
        low = lax.ppermute(
            lax.slice_in_dim(block, block.shape[dim] - width, None, axis=dim), axis, forward
        )
        high = lax.ppermute(lax.slice_in_dim(block, 0, width, axis=dim), axis, backward)
        block = jnp.concatenate([low, block, high], axis=dim)
    return block


def elastic_update(padded, current, previous_field, shear_modulus, lame_first, surface_force):
    own_axis = (0, 2, 1)
    stiffness = lame_first + 2.0 * shear_modulus
    updated_list = []
    for component in range(3):
        displaced = current[component]
        extended = padded[component]
        along_first = extended[2:, :, 1:-1] - 2.0 * displaced + extended[:-2, :, 1:-1]
        deeper = jnp.pad(displaced, ((0, 0), (1, 1), (0, 0)))
        along_depth = deeper[:, 2:, :] - 2.0 * displaced + deeper[:, :-2, :]
        along_second = extended[1:-1, :, 2:] - 2.0 * displaced + extended[1:-1, :, :-2]
        factors = [
            stiffness if own_axis[component] == axis_index else shear_modulus
            for axis_index in range(3)
        ]
        acceleration = (
            factors[0] * along_first + factors[1] * along_depth + factors[2] * along_second
        )
        updated = 2.0 * displaced - previous_field[component] + acceleration
        if component == 2:
            updated = updated.at[:, 0, :].add(surface_force)
        updated_list.append(updated)
    return jnp.stack(updated_list)


def shallow_update(padded, current, previous_field, wave_factor, area_factor, wetness, source):
    fine_rows = REFINE * CX
    fine_cols = REFINE * CY
    sheet = current.reshape(3, fine_rows, fine_cols)
    earlier_sheet = previous_field.reshape(3, fine_rows, fine_cols)
    above = padded[:, 0, (REFINE - 1) * REFINE :, 1:-1].reshape(3, 1, fine_cols)
    below = padded[:, -1, :REFINE, 1:-1].reshape(3, 1, fine_cols)
    left_side = padded[:, 1:-1, REFINE - 1 :: REFINE, 0].reshape(3, fine_rows, 1)
    right_side = padded[:, 1:-1, 0::REFINE, -1].reshape(3, fine_rows, 1)
    by_rows = jnp.concatenate([above, sheet, below], axis=1)
    by_columns = jnp.concatenate([left_side, sheet, right_side], axis=2)

    def rows_diff(channel):
        return by_rows[channel, 2:, :] - by_rows[channel, :-2, :]

    def columns_diff(channel):
        return by_columns[channel, :, 2:] - by_columns[channel, :, :-2]

    flux_first = wetness * (earlier_sheet[1] - wave_factor * rows_diff(0))
    flux_second = wetness * (earlier_sheet[2] - wave_factor * columns_diff(0))
    height = wetness * (earlier_sheet[0] - area_factor * (rows_diff(1) + columns_diff(2)) + source)
    return jnp.stack([height, flux_first, flux_second]).reshape(3, CX, NL, CY)


def route(payload):
    tile_data, tile_rows = payload
    width = tile_data.shape[-1]
    received_data, received_rows = (
        lax.all_to_all(tile_data, ("gx", "gy"), split_axis=0, concat_axis=0, tiled=True),
        lax.all_to_all(tile_rows, ("gx", "gy"), split_axis=0, concat_axis=0, tiled=True),
    )
    return (received_data.reshape(-1, width), received_rows.reshape(-1))


def deliver(outgoing, send_rows):
    crossed = from_partner((outgoing, send_rows), "sec", 0)
    return route(crossed)


def general_on_device(state, previous, coeff, wet_mask, link_dest, link_rows, link_weight):
    section = lax.axis_index("sec")
    owners = lax.axis_size("gx") * lax.axis_size("gy")
    fine_rows = REFINE * CX
    fine_cols = REFINE * CY
    current = state[0, :, 0, 0].reshape(3, CX, NL, CY)
    earlier = previous[0, :, 0, 0].reshape(3, CX, NL, CY)
    first_factor = coeff[0, 0, 0, 0]
    second_factor = coeff[0, 1, 0, 0]
    wetness = wet_mask[0, 0].reshape(fine_rows, fine_cols).astype(jnp.float32)
    targets = link_dest.reshape(-1)
    pairs = link_rows.reshape(-1, 2)
    source_rows = pairs[:, 0]
    landing = pairs[:, 1]
    weights = link_weight.reshape(-1)
    one_hot = (targets[:, None] == jnp.arange(owners, dtype=jnp.int32)[None, :]).astype(jnp.int32)
    before = jnp.cumsum(one_hot, axis=0) - one_hot
    slot_index = jnp.sum(before * one_hot, axis=1)
    position = targets * CAP + slot_index
    send_rows = jnp.zeros((owners * CAP,), jnp.int32).at[position].set(landing).reshape(owners, CAP)
    for step_index in range(STEPS):
        padded = with_halo(current, (("gx", 1), ("gy", 3)), 1)

        def elastic_rows():
            return current[2, :, 0, :][source_rows]

        def shallow_rows():
            picked_fine = current[0].reshape(fine_rows, fine_cols)[source_rows]
            return jnp.sum(picked_fine.reshape(-1, CY, REFINE), axis=-1) / REFINE

        picked = lax.cond(section == 0, elastic_rows, shallow_rows)
        outgoing = (
            jnp.zeros((owners * CAP, CY), jnp.float32).at[position].set(picked * weights[:, None])
        )
        outgoing = outgoing.reshape(owners, CAP, CY)
        arrived, arrived_rows = deliver(outgoing, send_rows)

        def elastic_branch():
            surface_force = jnp.zeros((CX, CY), jnp.float32).at[arrived_rows].add(arrived)
            return elastic_update(
                padded,
                current,
                earlier,
                first_factor.reshape(CX, NL, CY),
                second_factor.reshape(CX, NL, CY),
                surface_force,
            )

        def shallow_branch():
            coarse_source = jnp.zeros((fine_rows, CY), jnp.float32).at[arrived_rows].add(arrived)
            source = jnp.repeat(coarse_source, REFINE, axis=1)
            return shallow_update(
                padded,
                current,
                earlier,
                first_factor.reshape(fine_rows, fine_cols),
                second_factor.reshape(fine_rows, fine_cols),
                wetness,
                source,
            )

        updated = lax.cond(section == 0, elastic_branch, shallow_branch)
        earlier, current = (current, updated)
    return current.reshape(1, 3, 1, 1, -1)


def solution(mesh):
    placed = (
        P("sec", None, "gx", "gy", None),
        P("sec", None, "gx", "gy", None),
        P("sec", None, "gx", "gy", None),
        P("gx", "gy", None),
        P("sec", "gx", "gy", None, None),
        P("sec", "gx", "gy", None, None),
        P("sec", "gx", "gy", None),
    )
    n_gx, n_gy = mesh.shape["gx"], mesh.shape["gy"]
    owners = n_gx * n_gy
    device_program = general_on_device
    if n_gx == 2 and n_gy & (n_gy - 1) == 0 and owners * SLOTS == CY:
        device_program = functools.partial(on_device, n_gy, owners)
    return jax.shard_map(
        device_program,
        mesh=mesh,
        in_specs=placed,
        out_specs=P("sec", None, "gx", "gy", None),
        check_vma=False,
    )
```

```python
import functools

import jax
import jax.numpy as jnp
from jax import lax
from jax.experimental import pallas as pl
from jax.experimental.pallas import tpu as pltpu
from jax.sharding import PartitionSpec as P

CX = 8
CY = 128
REFINE = 10
NL = 100
STEPS = 4
CAP = 4
FINE = REFINE * CX
ROWS = CX * NL
FIRST = 104
TOTAL = FIRST + ROWS + FIRST
SLOTS = 8
GROUP = 200
BLOCKS = GROUP // 8
F32 = jnp.float32


def split(x):
    high = x.astype(jnp.bfloat16)
    rest = x - high.astype(F32)
    middle = rest.astype(jnp.bfloat16)
    low = (rest - middle.astype(F32)).astype(jnp.bfloat16)
    return high, middle, low


def pick(mask, x):
    parts = jnp.concatenate(split(x), axis=1)
    wide = jnp.dot(mask.astype(jnp.bfloat16), parts, preferred_element_type=F32)
    width = x.shape[1]
    return wide[:, 0:width] + (wide[:, width : 2 * width] + wide[:, 2 * width :])


def spread(x, mask):
    rows = x.shape[0]
    tall = jnp.dot(jnp.concatenate(split(x), axis=0), mask, preferred_element_type=F32)
    return tall[0:rows] + (tall[rows : 2 * rows] + tall[2 * rows :])


def iota(shape, dim):
    return lax.broadcasted_iota(jnp.int32, shape, dim)


def one(mask):
    return jnp.where(mask, 1.0, 0.0).astype(F32)


def place():
    return lax.axis_index("sec"), lax.axis_index("gx"), lax.axis_index("gy")


def average(rows_of):
    total = jnp.zeros((FINE, CY), F32)
    for m in range(REFINE):
        fine = iota((CY, CY), 0) + m * CY
        first = iota((CY, CY), 1) * REFINE
        mask = one((fine >= first) & (fine < first + REFINE)).astype(jnp.bfloat16)
        total = total + spread(rows_of(m), mask)
    return total / REFINE


def surface(section, elastic, sheet, surf):
    surf[...] = jnp.zeros_like(surf)

    @pl.when(section == 0)
    def _():
        surf[0:CX] = elastic[pl.ds(0, CX, stride=NL)]

    @pl.when(section != 0)
    def _():
        surf[0:FINE] = average(lambda m: sheet[pl.ds(m, FINE, stride=REFINE)])


def source_pick(cols):
    return one(cols[0] == iota((cols.shape[1], CY), 1).astype(F32))


def outgoing(section, tiles, cols, pcat, payload):
    half = payload.shape[0] // 2
    lanes = tiles.shape
    last = jnp.broadcast_to(tiles[:, CY - 1 : CY], lanes) * cols[1]
    first = jnp.broadcast_to(tiles[:, 0:1], lanes) * cols[1]
    packed = pick(pcat[...], jnp.concatenate([tiles, last, first, cols[3]], axis=0))
    payload[pl.ds(pl.multiple_of(section * half, 8), half)] = jnp.zeros((half, CY), F32)
    payload[pl.ds(pl.multiple_of((1 - section) * half, 8), half)] = packed


def link_tables(section, me, n_gy, dest, rows, weight, lines, cols, pcat):
    links = dest.shape[1]
    lines[...] = jnp.zeros_like(lines)
    lines[0:1, 0:links] = dest[...].astype(F32)
    lines[1:3, 0:links] = rows[...].astype(F32)
    lines[3:4, 0:links] = weight[...]
    x = lines[...]
    eye = one(iota((links, CY), 0) == iota((links, CY), 1))

    def column(i):
        return jnp.sum(eye * x[i : i + 1], axis=1, keepdims=True)

    target, source, landing, weights = [column(i) for i in range(4)]
    same = one(target == x[0:1])
    at = iota((links, CY), 0)
    other = iota((links, CY), 1)
    inside = one(other < links)
    slot_row = jnp.sum(same * one(at < other) * inside, axis=0, keepdims=True)
    slot = jnp.sum(same * one(other < at) * inside, axis=1, keepdims=True)
    lane = other.astype(F32)
    cols[0] = jnp.broadcast_to(source, (links, CY))
    cols[1] = one(landing == lane)
    cols[2] = jnp.broadcast_to(weights, (links, CY))
    cols[3] = landing * one(lane == slot + (me * SLOTS).astype(F32))
    y = jnp.concatenate([x[0:3], slot_row, jnp.zeros((4, CY), F32)], axis=0)
    y = y + pltpu.roll(y, links, 1) + pltpu.roll(y, 2 * links, 1) + pltpu.roll(y, 3 * links, 1)
    shape = (pcat.shape[0], CY)
    owner = iota(shape, 0) >> 3
    part = iota(shape, 0) & 7
    group = iota(shape, 1) >> (links.bit_length() - 1)
    to = y[0:1]
    row = y[2:3]
    order = y[3:4]
    beside = jnp.where(owner < n_gy, owner + n_gy, owner - n_gy).astype(F32)
    bottom = jnp.where(section == 0, FINE - 1, CX - 1).astype(F32)
    edge = jnp.where(owner < n_gy, 0.0, bottom)
    along = owner & (n_gy - 1)
    own = owner.astype(F32)
    chosen = one((group == 0) & (part == order.astype(jnp.int32)) & (part < CAP) & (to == own))
    chosen += one((group == 0) & (part == 4) & (to == beside) & (row == edge))
    chosen += one((group == 1) & (part == 6) & (to == own - 1.0) & (along > 0))
    chosen += one((group == 2) & (part == 7) & (to == own + 1.0) & (along < n_gy - 1))
    chosen += one((group == 3) & (part == 5) & (to == own))
    pcat[...] = chosen


def collect(acc, value, j, lane):
    return jnp.where(lane >> 1 == j, pltpu.roll(value, 2 * j + 1, 1), acc)


def merge(it, acc, sides):
    for c, value in acc.items():
        sides[c, it >> 1] += pltpu.roll(value, (it & 1) * 2 * BLOCKS, 1)


def take_edges(section, p, fields, wet, xs):
    start = pl.multiple_of(jnp.where(p == 0, ROWS - FIRST, 0), 8)
    for c in range(3):
        xs[c] = fields[c, pl.ds(start, FIRST)]

    @pl.when(section != 0)
    def _():
        xs[2] = wet[pl.ds(start, FIRST)].astype(F32)


def load_kernel(n_gy, state, previous, wet, dest, rows, weight, payload, cols, pcat, cur, prev, xs, sides, scale, wet_in, dest_in, rows_in, weight_in, lines, surf, sem):
    section, p, q = place()
    pairs = [(dest, dest_in), (rows, rows_in), (weight, weight_in)]
    pairs += [(state.at[c], cur.at[c]) for c in (2, 0, 1)]
    pairs += [(wet, wet_in), (previous, prev)]
    copies = [pltpu.make_async_copy(a, b, sem.at[i]) for i, (a, b) in enumerate(pairs)]
    for copy in copies:
        copy.start()
    sides[...] = jnp.zeros_like(sides)
    for copy in copies[0:3]:
        copy.wait()
    link_tables(section, p * n_gy + q, n_gy, dest_in, rows_in, weight_in, lines, cols, pcat)
    for copy in copies[3:7]:
        copy.wait()
    surface(section, cur.at[2], cur.at[0], surf)
    tiles = cols[2] * pick(source_pick(cols), surf[...])
    outgoing(section, tiles, cols, pcat, payload)
    lane = iota((8, CY), 1)

    def pack(it, carry):
        acc = {c: jnp.zeros((8, CY), F32) for c in range(3)}
        views = [cur.at[c, group_rows(it, GROUP)] for c in range(3)]
        wets = wet_in.at[group_rows(it, GROUP)]
        for j in range(BLOCKS):
            at = slice(8 * j, 8 * j + 8)
            for c in range(3):
                value = views[c][at]
                if c == 1:
                    value = jnp.where(section == 0, value, wets[at].astype(F32))
                acc[c] = collect(acc[c], value, j, lane)
        merge(it, acc, sides)
        return carry

    lax.fori_loop(0, ROWS // GROUP, pack, 0)
    take_edges(section, p, cur, wet_in, xs)
    scale[...] = cols[2]

    @pl.when(section != 0)
    def _():
        surf[0:FINE] = average(lambda m: wet_in[pl.ds(m, FINE, stride=REFINE)].astype(F32))
        scale[...] = cols[2] * pick(source_pick(cols), surf[...])

    copies[7].wait()


def group_rows(it, rows):
    return pl.ds(pl.multiple_of(it * GROUP, 8), rows)


def arrived_rows(section, received):
    half = received.shape[0] // 2
    return received[pl.ds(pl.multiple_of((1 - section) * half, 8), half)]


def arrived_sums(arrived):
    return jnp.sum(arrived.reshape(-1, SLOTS, CY), axis=0)


def landed(arrived, sums):
    mine = iota((CY, arrived.shape[0]), 1)
    return pick(one((iota(mine.shape, 0).astype(F32) == sums[5:6]) & ((mine & 7) < CAP)), arrived)


def route_kernel(received, base, scale, cols, pcat, payload):
    section, _, _ = place()
    arrived = arrived_rows(section, received)
    landing = arrived_sums(arrived)[5:6]
    lane = iota(cols.shape[1:], 1)
    gather = one((cols[0] == landing) & ((lane & 7) < CAP))
    tiles = base[...] + scale[...] * pick(gather, arrived)
    outgoing(section, tiles, cols, pcat, payload)


def edge_addends(sums, period, offset):
    masks, values = [], []
    lane = iota((CY, 2 * CY), 1)
    block = ((lane & (CY - 1)) >> 1) + jnp.where(lane >= CY, 2 * BLOCKS, 0)
    inside = (lane & (CY - 1)) < 4 * BLOCKS
    for side, shift in ((0, 0), (1, offset)):
        at = iota(lane.shape, 0) * period + shift - block * 8
        masks.append(one((at >= 0) & (at < 8) & ((lane & 1) == side) & inside).astype(jnp.bfloat16))
        sub = (iota((16, CY), 1) * period + shift) & 7
        row = jnp.broadcast_to(sums[6 + side : 7 + side], (16, CY))
        values.append(jnp.where(sub == iota((16, CY), 0), row, 0.0))
    wide = spread(values[0], masks[0]) + spread(values[1], masks[1])
    return wide[0:8, 0:CY], wide[0:8, CY:]


def align_sides(zs, c, lane, sub):
    first, second = zs[c, 0], zs[c, 1]
    top = 4 * BLOCKS
    low_first = jnp.where(lane == top - 2, pltpu.roll(second, top - 2, 1), pltpu.roll(first, CY - 2, 1))
    low_second = pltpu.roll(second, CY - 2, 1)
    high_first = pltpu.roll(first, 2, 1)
    high_second = jnp.where(lane == 1, pltpu.roll(first, CY + 2 - top, 1), pltpu.roll(second, 2, 1))
    for h, (low, high) in enumerate(((low_first, high_first), (low_second, high_second))):
        zs[c, h] = jnp.where(lane & 1 == 0, pltpu.roll(low, 7, 0), pltpu.roll(high, 1, 0))


def step_kernel(linked, last, *refs):
    cur_in, prev_in, coeff, wet, cols, xr, yra, yrb, mine, *refs = refs
    if linked:
        received, *refs = refs
    cur, prev, *refs = refs
    if last:
        out, zs, full, co, wet_in, sem = refs
    else:
        base, xs, sides, zs, full, co, wet_in, sem, surf = refs
    section, p, q = place()
    lane = iota((8, CY), 1)
    sub = iota((8, CY), 0)
    zero = jnp.zeros((8, CY), F32)
    even_lane = lane & 1 == 0
    loads = [pltpu.make_async_copy(coeff, co, sem.at[0]), pltpu.make_async_copy(wet, wet_in, sem.at[1])]
    for load in loads:
        load.start()

    @pl.when((q & 1) == 1)
    def _():
        for c in range(3):
            for h in range(2):
                zs[c, h] = jnp.where(even_lane, yra[c, h], yrb[c, h])

    @pl.when((q & 1) == 0)
    def _():
        for c in range(3):
            for h in range(2):
                zs[c, h] = jnp.where(even_lane, yrb[c, h], yra[c, h])

    there = pl.multiple_of(jnp.where(p == 0, FIRST + ROWS, 0), 8)
    nowhere = pl.multiple_of(jnp.where(p == 0, 0, FIRST + ROWS), 8)
    for c in range(3):
        full[c, pl.ds(there, FIRST)] = xr[c]
        full[c, pl.ds(nowhere, FIRST)] = jnp.zeros((FIRST, CY), F32)

    if linked:
        arrived = arrived_rows(section, received)
        sums = arrived_sums(arrived)
        addend = landed(arrived, sums)
    if not last:
        sides[...] = jnp.zeros_like(sides)

    def widen(it, carry):
        for c in range(3):
            view = full.at[c, group_rows(it, FIRST + GROUP)]
            view[FIRST : FIRST + GROUP] = cur[c, group_rows(it, GROUP)]
        return carry

    def views_of(it, ref):
        return [ref.at[c, group_rows(it, GROUP)] for c in range(ref.shape[0])]

    def padded_of(it):
        return [full.at[c, group_rows(it, GROUP + 2 * FIRST)] for c in range(3)]

    @pl.when(section == 0)
    def _():
        if linked:
            for x in range(CX):
                cur[2, NL * x : NL * x + 1] += addend[x : x + 1]

            @pl.when(p == 0)
            def _():
                full[2, FIRST + ROWS : FIRST + ROWS + 1] += sums[4:5]

            @pl.when(p != 0)
            def _():
                full[2, FIRST - NL : FIRST - NL + 1] += sums[4:5]

            for h, value in enumerate(edge_addends(sums, NL, 0)):
                zs[2, h] += value

        lax.fori_loop(0, ROWS // GROUP, widen, 0)
        for load in loads:
            load.wait()

        def group(it, carry):
            turn = (CY - (it & 1) * 2 * BLOCKS) & (CY - 1)
            halos = [pltpu.roll(zs[c, it >> 1], turn, 1) for c in range(3)]
            acc = {c: zero for c in range(3)}
            fields, old, new_fields, factors = padded_of(it), views_of(it, prev_in), views_of(it, prev), views_of(it, co)
            for j in range(BLOCKS):
                at = slice(8 * j, 8 * j + 8)
                mu = factors[0][at]
                stiff = factors[1][at] + 2.0 * mu
                for c in range(3):

                    def near(rows):
                        return fields[c][FIRST + 8 * j + rows : FIRST + 8 * j + rows + 8]

                    v = near(0)
                    twice = 2.0 * v
                    above = near(-1)
                    below = near(1)
                    for row in (0, NL):
                        if 8 * j <= row < 8 * j + 8:
                            above = jnp.where(sub == row - 8 * j, 0.0, above)
                    for row in (NL - 1, GROUP - 1):
                        if 8 * j <= row < 8 * j + 8:
                            below = jnp.where(sub == row - 8 * j, 0.0, below)
                    halo = pltpu.roll(halos[c], CY - 1 - 2 * j, 1)
                    low = jnp.where(lane == CY - 1, halo, v)
                    high = jnp.where(lane == 0, halo, v)
                    along_first = near(-NL) + near(NL) - twice
                    along_depth = above + below - twice
                    along_second = pltpu.roll(low, 1, 1) + pltpu.roll(high, CY - 1, 1) - twice
                    if c == 0:
                        force = stiff * along_first + mu * (along_depth + along_second)
                    elif c == 1:
                        force = stiff * along_second + mu * (along_first + along_depth)
                    else:
                        force = stiff * along_depth + mu * (along_first + along_second)
                    new = twice - old[c][at] + force
                    new_fields[c][at] = new
                    if not last:
                        acc[c] = collect(acc[c], new, j, lane)
            if not last:
                merge(it, acc, sides)
            return carry

        lax.fori_loop(0, ROWS // GROUP, group, 0)

    @pl.when(section != 0)
    def _():
        for c in range(3):
            align_sides(zs, c, lane, sub)
        if linked:
            for h, value in enumerate(edge_addends(sums, REFINE, REFINE - 1)):
                zs[0, h] += zs[1, h] * value
            beside = jnp.broadcast_to(sums[4:5], (8, CY))
            fine_row = jnp.concatenate(
                [
                    jnp.take_along_axis(beside, (((sub + m) * CY + lane) * 6554) >> 16, axis=1)
                    for m in (0, 2)
                ],
                axis=0,
            )

            def add_edge(first):
                for start, rows in ((0, fine_row[0:8]), (8, fine_row[14:16])):
                    at = slice(first + start, first + start + rows.shape[0])
                    full[0, at] += full[2, at] * rows

            @pl.when(p == 0)
            def _():
                add_edge(FIRST + ROWS)

            @pl.when(p != 0)
            def _():
                add_edge(FIRST - REFINE)

        for load in loads:
            load.wait()
        if linked:
            for start, fine in fine_addend(addend):
                at = pl.ds(start, 8, stride=REFINE)
                cur[0, at] += wet_in[at].astype(F32) * fine
        lax.fori_loop(0, ROWS // GROUP, widen, 0)

        def group(it, carry):
            turn = (CY - (it & 1) * 2 * BLOCKS) & (CY - 1)
            halos = {c: pltpu.roll(zs[c, it >> 1], turn, 1) for c in (0, 2)}
            acc = {0: zero, 2: zero}
            fields, old, new_fields, factors = padded_of(it), views_of(it, prev_in), views_of(it, prev), views_of(it, co)
            wets = wet_in.at[group_rows(it, GROUP)]
            for j in range(BLOCKS):
                at = slice(8 * j, 8 * j + 8)
                a = factors[0][at]
                b = factors[1][at]
                w = wets[at].astype(F32)

                def near(c, rows):
                    return fields[c][FIRST + 8 * j + rows : FIRST + 8 * j + rows + 8]

                def across(c):
                    v = near(c, 0)
                    low = jnp.where(lane == CY - 1, near(c, -1), v)
                    high = jnp.where(lane == 0, near(c, 1), v)
                    halo = pltpu.roll(halos[c], CY - 1 - 2 * j, 1)
                    for s in range(8):
                        if (8 * j + s) % REFINE == 0:
                            low = jnp.where((lane == CY - 1) & (sub == s), halo, low)
                        if (8 * j + s) % REFINE == REFINE - 1:
                            high = jnp.where((lane == 0) & (sub == s), halo, high)
                    return pltpu.roll(high, CY - 1, 1) - pltpu.roll(low, 1, 1)

                def down(c):
                    return near(c, REFINE) - near(c, -REFINE)

                first_flux = w * (old[1][at] - a * down(0))
                second_flux = w * (old[2][at] - a * across(0))
                height = w * (old[0][at] - b * (down(1) + across(2)))
                new_fields[0][at] = height
                new_fields[1][at] = first_flux
                new_fields[2][at] = second_flux
                if not last:
                    acc[0] = collect(acc[0], height, j, lane)
                    acc[2] = collect(acc[2], second_flux, j, lane)
            if not last:
                merge(it, acc, sides)
            return carry

        lax.fori_loop(0, ROWS // GROUP, group, 0)
        if not last:
            sides[1] = mine[1]

    if last:
        copy = pltpu.make_async_copy(prev, out, sem.at[0])
        copy.start()
        copy.wait()
    else:
        take_edges(section, p, prev, wet_in, xs)
        surface(section, prev.at[2], prev.at[0], surf)
        base[...] = cols[2] * pick(source_pick(cols), surf[...])


def fine_addend(addend):
    lane = iota((8, CY), 1)
    for m in range(FINE // 8):
        rows = addend[8 * m : 8 * m + 8]
        for k in range(REFINE):
            fine = jnp.take_along_axis(rows, ((lane + k * CY) * 6554) >> 16, axis=1)
            yield 8 * REFINE * m + k, fine


def last_kernel(final_in, fields, wet, received, final, height, wet_in, load_sem, sem):
    section, _, _ = place()
    load = pltpu.make_async_copy(wet, wet_in, load_sem)
    load.start()
    arrived = arrived_rows(section, received)
    addend = landed(arrived, arrived_sums(arrived))
    load.wait()

    @pl.when(section == 0)
    def _():
        copies = []
        for x in range(CX):
            row = NL * x
            first = row // 8 * 8
            height[8 * x : 8 * x + 8] = fields[2, first : first + 8]
            at = 8 * x + row - first
            height[at : at + 1] += addend[x : x + 1]
            copies.append(
                pltpu.make_async_copy(
                    height.at[8 * x : 8 * x + 8], final.at[2, pl.ds(first, 8)], sem.at[x]
                )
            )
        for copy in copies:
            copy.start()
        for copy in copies:
            copy.wait()

    @pl.when(section != 0)
    def _():
        for start, fine in fine_addend(addend):
            at = pl.ds(start, 8, stride=REFINE)
            height[at] = fields[0, at] + wet_in[at].astype(F32) * fine
        copy = pltpu.make_async_copy(height, final.at[0], sem.at[0])
        copy.start()
        copy.wait()


def call(kernel, operands, outs, scratch=(), aliases=None, any_inputs=(), any_outs=(), limit=12, cost=4):
    vmem = pl.BlockSpec(memory_space=pltpu.VMEM)
    anywhere = pl.BlockSpec(memory_space=pl.ANY)
    return pl.pallas_call(
        kernel,
        out_shape=[
            (pltpu.VMEM if kept else jax.ShapeDtypeStruct)(shape, kind[0] if kind else F32)
            for shape, kept, *kind in outs
        ],
        in_specs=[anywhere if i in any_inputs else vmem for i in range(len(operands))],
        out_specs=[anywhere if i in any_outs else vmem for i in range(len(outs))],
        scratch_shapes=list(scratch),
        input_output_aliases=aliases or {},
        compiler_params=pltpu.CompilerParams(vmem_limit_bytes=limit * 1024 * 1024),
        cost_estimate=pl.CostEstimate(flops=cost * 10**9, bytes_accessed=cost * 1024 * 1024, transcendentals=0),
    )(*operands)


def keep(value):
    return pltpu.with_memory_space_constraint(value, pltpu.VMEM)


def outside(value):
    return pltpu.with_memory_space_constraint(value, pltpu.HBM)


def on_device(n_gy, owners, state, previous, coeff, wet_mask, link_dest, link_rows, link_weight):
    links = link_weight.size
    pairs = 2 * owners * SLOTS
    vmem = pltpu.VMEM
    dma = pltpu.SemaphoreType.DMA
    field_shape = (3, ROWS, CY)
    sides_shape = (3, 2, 8, CY)
    fields = (field_shape, True)
    edges = ((3, FIRST, CY), False)
    sides_out = (sides_shape, False)
    tiles = ((links, CY), True)
    surf = vmem((CY, CY), F32)
    wet_in = vmem((ROWS, CY), jnp.int32)
    state, previous = state.reshape(field_shape), previous.reshape(field_shape)
    coeff, wet = outside(coeff.reshape(2, ROWS, CY)), outside(wet_mask.reshape(ROWS, CY))

    def exchange(payload):
        payload = payload.reshape(2 * owners, SLOTS, CY)
        payload = lax.all_to_all(payload, ("sec", "gx", "gy"), 0, 0, tiled=True)
        return payload.reshape(pairs, CY)

    dest, rows, weight = link_dest.reshape(1, links), link_rows.reshape(links, 2).T, link_weight.reshape(1, links)
    payload, cols, pcat, cur, prev, xs, sides, scale = call(
        functools.partial(load_kernel, n_gy),
        [outside(x) for x in (state, previous, wet, dest, rows, weight)],
        [
            ((pairs, CY), False), ((4, links, CY), True), ((owners * SLOTS, CY), True), fields, fields,
            edges, sides_out, tiles,
        ],
        [
            wet_in, vmem((1, links), jnp.int32), vmem((2, links), jnp.int32),
            vmem((1, links), F32), vmem((8, CY), F32), surf, dma((8,)),
        ],
        any_inputs=range(6),
    )
    received = exchange(payload)
    swap = [(0, 1), (1, 0)]
    inner = [(i, i ^ 1) for i in range(n_gy)]
    outer = [(i, j) for k in range(1, n_gy - 1, 2) for i, j in ((k, k + 1), (k + 1, k))]
    before = None
    for step in range(STEPS):
        last = step == STEPS - 1
        xr = lax.ppermute(xs, "gx", swap)
        yra = lax.ppermute(sides, "gy", inner)
        yrb = lax.ppermute(sides, "gy", outer)
        operands = [keep(cur), keep(prev), coeff, wet, keep(cols), xr, yra, yrb, sides]
        if before is not None:
            operands.append(before)
        kernel = functools.partial(step_kernel, before is not None, last)
        scratch = [vmem(sides_shape, F32), vmem((3, TOTAL, CY), F32), vmem((2, ROWS, CY), F32), wet_in, dma((2,))]
        more = dict(aliases={0: 0, 1: 1}, any_inputs=(2, 3), cost=64)
        if last:
            _, new, final = call(
                kernel, operands, [fields, fields, (field_shape, False)], scratch, any_outs=(2,), **more
            )
        else:
            cur, prev, base, xs, sides = call(
                kernel, operands, [fields, fields, tiles, edges, sides_out], scratch + [surf], **more
            )
            cur, prev = prev, cur
            payload = call(
                route_kernel, (received, keep(base), keep(scale), keep(cols), keep(pcat)),
                [((pairs, CY), False)], limit=4,
            )[0]
            before = received
            received = exchange(payload)
    final = call(
        last_kernel,
        (outside(final), keep(new), wet, received),
        [(field_shape, False)],
        [vmem((ROWS, CY), F32), wet_in, dma, dma((CX,))],
        aliases={0: 0}, any_inputs=(0, 2), any_outs=(0,),
    )[0]
    return final.reshape(1, 3, 1, 1, -1)


def from_partner(value, axis, stride):
    return lax.ppermute(value, axis, [(i, i ^ 1 << stride) for i in range(lax.axis_size(axis))])


def with_halo(block, sides, width):
    for axis, dim in sides:
        count = lax.axis_size(axis)
        forward = [(i, i + 1) for i in range(count - 1)]
        backward = [(target, source) for source, target in forward]
        low = lax.ppermute(
            lax.slice_in_dim(block, block.shape[dim] - width, None, axis=dim), axis, forward
        )
        high = lax.ppermute(lax.slice_in_dim(block, 0, width, axis=dim), axis, backward)
        block = jnp.concatenate([low, block, high], axis=dim)
    return block


def elastic_update(padded, current, previous_field, shear_modulus, lame_first, surface_force):
    own_axis = (0, 2, 1)
    stiffness = lame_first + 2.0 * shear_modulus
    updated_list = []
    for component in range(3):
        displaced = current[component]
        extended = padded[component]
        along_first = extended[2:, :, 1:-1] - 2.0 * displaced + extended[:-2, :, 1:-1]
        deeper = jnp.pad(displaced, ((0, 0), (1, 1), (0, 0)))
        along_depth = deeper[:, 2:, :] - 2.0 * displaced + deeper[:, :-2, :]
        along_second = extended[1:-1, :, 2:] - 2.0 * displaced + extended[1:-1, :, :-2]
        factors = [
            stiffness if own_axis[component] == axis_index else shear_modulus
            for axis_index in range(3)
        ]
        acceleration = (
            factors[0] * along_first + factors[1] * along_depth + factors[2] * along_second
        )
        updated = 2.0 * displaced - previous_field[component] + acceleration
        if component == 2:
            updated = updated.at[:, 0, :].add(surface_force)
        updated_list.append(updated)
    return jnp.stack(updated_list)


def shallow_update(padded, current, previous_field, wave_factor, area_factor, wetness, source):
    fine_rows = REFINE * CX
    fine_cols = REFINE * CY
    sheet = current.reshape(3, fine_rows, fine_cols)
    earlier_sheet = previous_field.reshape(3, fine_rows, fine_cols)
    above = padded[:, 0, (REFINE - 1) * REFINE :, 1:-1].reshape(3, 1, fine_cols)
    below = padded[:, -1, :REFINE, 1:-1].reshape(3, 1, fine_cols)
    left_side = padded[:, 1:-1, REFINE - 1 :: REFINE, 0].reshape(3, fine_rows, 1)
    right_side = padded[:, 1:-1, 0::REFINE, -1].reshape(3, fine_rows, 1)
    by_rows = jnp.concatenate([above, sheet, below], axis=1)
    by_columns = jnp.concatenate([left_side, sheet, right_side], axis=2)

    def rows_diff(channel):
        return by_rows[channel, 2:, :] - by_rows[channel, :-2, :]

    def columns_diff(channel):
        return by_columns[channel, :, 2:] - by_columns[channel, :, :-2]

    flux_first = wetness * (earlier_sheet[1] - wave_factor * rows_diff(0))
    flux_second = wetness * (earlier_sheet[2] - wave_factor * columns_diff(0))
    height = wetness * (earlier_sheet[0] - area_factor * (rows_diff(1) + columns_diff(2)) + source)
    return jnp.stack([height, flux_first, flux_second]).reshape(3, CX, NL, CY)


def route(payload):
    tile_data, tile_rows = payload
    width = tile_data.shape[-1]
    received_data, received_rows = (
        lax.all_to_all(tile_data, ("gx", "gy"), split_axis=0, concat_axis=0, tiled=True),
        lax.all_to_all(tile_rows, ("gx", "gy"), split_axis=0, concat_axis=0, tiled=True),
    )
    return (received_data.reshape(-1, width), received_rows.reshape(-1))


def deliver(outgoing, send_rows):
    crossed = from_partner((outgoing, send_rows), "sec", 0)
    return route(crossed)


def general_on_device(state, previous, coeff, wet_mask, link_dest, link_rows, link_weight):
    section = lax.axis_index("sec")
    owners = lax.axis_size("gx") * lax.axis_size("gy")
    fine_rows = REFINE * CX
    fine_cols = REFINE * CY
    current = state[0, :, 0, 0].reshape(3, CX, NL, CY)
    earlier = previous[0, :, 0, 0].reshape(3, CX, NL, CY)
    first_factor = coeff[0, 0, 0, 0]
    second_factor = coeff[0, 1, 0, 0]
    wetness = wet_mask[0, 0].reshape(fine_rows, fine_cols).astype(jnp.float32)
    targets = link_dest.reshape(-1)
    pairs = link_rows.reshape(-1, 2)
    source_rows = pairs[:, 0]
    landing = pairs[:, 1]
    weights = link_weight.reshape(-1)
    one_hot = (targets[:, None] == jnp.arange(owners, dtype=jnp.int32)[None, :]).astype(jnp.int32)
    before = jnp.cumsum(one_hot, axis=0) - one_hot
    slot_index = jnp.sum(before * one_hot, axis=1)
    position = targets * CAP + slot_index
    send_rows = jnp.zeros((owners * CAP,), jnp.int32).at[position].set(landing).reshape(owners, CAP)
    for step_index in range(STEPS):
        padded = with_halo(current, (("gx", 1), ("gy", 3)), 1)

        def elastic_rows():
            return current[2, :, 0, :][source_rows]

        def shallow_rows():
            picked_fine = current[0].reshape(fine_rows, fine_cols)[source_rows]
            return jnp.sum(picked_fine.reshape(-1, CY, REFINE), axis=-1) / REFINE

        picked = lax.cond(section == 0, elastic_rows, shallow_rows)
        outgoing = (
            jnp.zeros((owners * CAP, CY), jnp.float32).at[position].set(picked * weights[:, None])
        )
        outgoing = outgoing.reshape(owners, CAP, CY)
        arrived, arrived_rows = deliver(outgoing, send_rows)

        def elastic_branch():
            surface_force = jnp.zeros((CX, CY), jnp.float32).at[arrived_rows].add(arrived)
            return elastic_update(
                padded,
                current,
                earlier,
                first_factor.reshape(CX, NL, CY),
                second_factor.reshape(CX, NL, CY),
                surface_force,
            )

        def shallow_branch():
            coarse_source = jnp.zeros((fine_rows, CY), jnp.float32).at[arrived_rows].add(arrived)
            source = jnp.repeat(coarse_source, REFINE, axis=1)
            return shallow_update(
                padded,
                current,
                earlier,
                first_factor.reshape(fine_rows, fine_cols),
                second_factor.reshape(fine_rows, fine_cols),
                wetness,
                source,
            )

        updated = lax.cond(section == 0, elastic_branch, shallow_branch)
        earlier, current = (current, updated)
    return current.reshape(1, 3, 1, 1, -1)


def solution(mesh):
    placed = (
        P("sec", None, "gx", "gy", None),
        P("sec", None, "gx", "gy", None),
        P("sec", None, "gx", "gy", None),
        P("gx", "gy", None),
        P("sec", "gx", "gy", None, None),
        P("sec", "gx", "gy", None, None),
        P("sec", "gx", "gy", None),
    )
    n_gx, n_gy = mesh.shape["gx"], mesh.shape["gy"]
    owners = n_gx * n_gy
    device_program = general_on_device
    if n_gx == 2 and n_gy & (n_gy - 1) == 0 and owners * SLOTS == CY:
        device_program = functools.partial(on_device, n_gy, owners)
    return jax.shard_map(
        device_program,
        mesh=mesh,
        in_specs=placed,
        out_specs=P("sec", None, "gx", "gy", None),
        check_vma=False,
    )
```

```python
import functools

import jax
import jax.numpy as jnp
from jax import lax
from jax.experimental import pallas as pl
from jax.experimental.pallas import tpu as pltpu
from jax.sharding import PartitionSpec as P

CX = 8
CY = 128
REFINE = 10
NL = 100
STEPS = 4
CAP = 4
FINE = REFINE * CX
ROWS = CX * NL
FIRST = 104
TOTAL = FIRST + ROWS + FIRST
SLOTS = 8
BLOCKS = 20
BATCH = 4
GROUP = 8 * BLOCKS
HALF = ROWS // 16
F32 = jnp.float32


def split(x):
    high = x.astype(jnp.bfloat16)
    return high, (x - high.astype(F32)).astype(jnp.bfloat16)


def pick(mask, x):
    parts = jnp.concatenate(split(x), axis=1)
    wide = jnp.dot(mask.astype(jnp.bfloat16), parts, preferred_element_type=F32)
    return wide[:, 0 : x.shape[1]] + wide[:, x.shape[1] :]


def spread(x, mask):
    tall = jnp.dot(jnp.concatenate(split(x), axis=0), mask, preferred_element_type=F32)
    return tall[0 : x.shape[0]] + tall[x.shape[0] :]


def iota(shape, dim):
    return lax.broadcasted_iota(jnp.int32, shape, dim)


def one(mask):
    return jnp.where(mask, 1.0, 0.0).astype(F32)


def place():
    return lax.axis_index("sec"), lax.axis_index("gx"), lax.axis_index("gy")


def average(rows_of):
    total = jnp.zeros((FINE, CY), F32)
    for m in range(REFINE):
        fine = iota((CY, CY), 0) + m * CY
        first = iota((CY, CY), 1) * REFINE
        mask = one((fine >= first) & (fine < first + REFINE)).astype(jnp.bfloat16)
        total = total + spread(rows_of(m), mask)
    return total / REFINE


def surface(section, elastic, sheet, surf):
    surf[...] = jnp.zeros_like(surf)

    @pl.when(section == 0)
    def _():
        surf[0:CX] = elastic[pl.ds(0, CX, stride=NL)]

    @pl.when(section != 0)
    def _():
        surf[0:FINE] = average(lambda m: sheet[pl.ds(m, FINE, stride=REFINE)])


def source_pick(cols):
    return one(cols[0] == iota((cols.shape[1], CY), 1).astype(F32))


def outgoing(section, tiles, cols, pcat, payload):
    half = payload.shape[0] // 2
    lanes = tiles.shape
    last = jnp.broadcast_to(tiles[:, CY - 1 : CY], lanes) * cols[1]
    first = jnp.broadcast_to(tiles[:, 0:1], lanes) * cols[1]
    packed = pick(pcat[...], jnp.concatenate([tiles, last, first, cols[3]], axis=0))
    payload[pl.ds(pl.multiple_of(section * half, 8), half)] = jnp.zeros((half, CY), F32)
    payload[pl.ds(pl.multiple_of((1 - section) * half, 8), half)] = packed


def link_tables(section, me, n_gy, dest, rows, weight, lines, cols, pcat):
    links = dest.shape[1]
    lines[...] = jnp.zeros_like(lines)
    lines[0:1, 0:links] = dest[...].astype(F32)
    lines[1:3, 0:links] = rows[...].astype(F32)
    lines[3:4, 0:links] = weight[...]
    x = lines[...]
    eye = one(iota((links, CY), 0) == iota((links, CY), 1))

    def column(i):
        return jnp.sum(eye * x[i : i + 1], axis=1, keepdims=True)

    target, source, landing, weights = [column(i) for i in range(4)]
    same = one(target == x[0:1])
    at = iota((links, CY), 0)
    other = iota((links, CY), 1)
    inside = one(other < links)
    slot_row = jnp.sum(same * one(at < other) * inside, axis=0, keepdims=True)
    slot = jnp.sum(same * one(other < at) * inside, axis=1, keepdims=True)
    lane = other.astype(F32)
    cols[0] = jnp.broadcast_to(source, (links, CY))
    cols[1] = one(landing == lane)
    cols[2] = jnp.broadcast_to(weights, (links, CY))
    cols[3] = landing * one(lane == slot + (me * SLOTS).astype(F32))
    y = jnp.concatenate([x[0:3], slot_row, jnp.zeros((4, CY), F32)], axis=0)
    y = y + pltpu.roll(y, links, 1) + pltpu.roll(y, 2 * links, 1) + pltpu.roll(y, 3 * links, 1)
    shape = (pcat.shape[0], CY)
    owner = iota(shape, 0) >> 3
    part = iota(shape, 0) & 7
    group = iota(shape, 1) >> (links.bit_length() - 1)
    to = y[0:1]
    row = y[2:3]
    order = y[3:4]
    beside = jnp.where(owner < n_gy, owner + n_gy, owner - n_gy).astype(F32)
    bottom = jnp.where(section == 0, FINE - 1, CX - 1).astype(F32)
    edge = jnp.where(owner < n_gy, 0.0, bottom)
    along = owner & (n_gy - 1)
    own = owner.astype(F32)
    chosen = one((group == 0) & (part == order.astype(jnp.int32)) & (part < CAP) & (to == own))
    chosen += one((group == 0) & (part == 4) & (to == beside) & (row == edge))
    chosen += one((group == 1) & (part == 6) & (to == own - 1.0) & (along > 0))
    chosen += one((group == 2) & (part == 7) & (to == own + 1.0) & (along < n_gy - 1))
    chosen += one((group == 3) & (part == 5) & (to == own))
    pcat[...] = chosen


def pack_sides(values_of, sides, channels):
    lane = iota((8, CY), 1)

    def half_of(h, carry):
        acc = {c: jnp.zeros((8, CY), F32) for c in channels}
        views = {c: values_of(c, pl.ds(pl.multiple_of(h * HALF * 8, 8), HALF * 8)) for c in channels}
        for b in range(HALF):
            for c in channels:
                value = views[c][8 * b : 8 * b + 8].astype(F32)
                acc[c] = jnp.where(lane >> 1 == b, pltpu.roll(value, 2 * b + 1, 1), acc[c])
        for c in channels:
            sides[c, h] = acc[c]
        return carry

    lax.fori_loop(0, 2, half_of, 0)


def unpack_sides(zs, halos, channels):
    def half_of(h, carry):
        for i, c in enumerate(channels):
            value = zs[c, h]
            view = halos.at[i, pl.ds(pl.multiple_of(h * HALF * 8, 8), HALF * 8)]
            for b in range(HALF):
                view[8 * b : 8 * b + 8] = pltpu.roll(value, CY - 1 - 2 * b, 1)
        return carry

    lax.fori_loop(0, 2, half_of, 0)


def take_edges(section, p, fields, wet, xs):
    start = pl.multiple_of(jnp.where(p == 0, ROWS - FIRST, 0), 8)
    for c in range(3):
        xs[c] = fields[c, pl.ds(start, FIRST)]

    @pl.when(section != 0)
    def _():
        xs[2] = wet[pl.ds(start, FIRST)].astype(F32)


def load_kernel(n_gy, state, previous, wet, dest, rows, weight, payload, cols, pcat, cur, prev, xs, sides, scale, wet_in, dest_in, rows_in, weight_in, lines, surf, sem):
    section, p, q = place()
    pairs = [(dest, dest_in), (rows, rows_in), (weight, weight_in)]
    pairs += [(state.at[c], cur.at[c]) for c in (2, 0, 1)]
    pairs += [(wet, wet_in), (previous, prev)]
    copies = [pltpu.make_async_copy(a, b, sem.at[i]) for i, (a, b) in enumerate(pairs)]
    for copy in copies:
        copy.start()
    for copy in copies[0:3]:
        copy.wait()
    link_tables(section, p * n_gy + q, n_gy, dest_in, rows_in, weight_in, lines, cols, pcat)
    for copy in copies[3:7]:
        copy.wait()
    surface(section, cur.at[2], cur.at[0], surf)
    tiles = cols[2] * pick(source_pick(cols), surf[...])
    outgoing(section, tiles, cols, pcat, payload)

    @pl.when(section == 0)
    def _():
        pack_sides(lambda c, at: cur.at[c, at], sides, (0, 1, 2))

    @pl.when(section != 0)
    def _():
        pack_sides(lambda c, at: wet_in.at[at] if c == 1 else cur.at[c, at], sides, (0, 1, 2))

    take_edges(section, p, cur, wet_in, xs)
    scale[...] = cols[2]

    @pl.when(section != 0)
    def _():
        surf[0:FINE] = average(lambda m: wet_in[pl.ds(m, FINE, stride=REFINE)].astype(F32))
        scale[...] = cols[2] * pick(source_pick(cols), surf[...])

    copies[7].wait()


def group_rows(it, rows):
    return pl.ds(pl.multiple_of(it * GROUP, 8), rows)


def arrived_rows(section, received):
    half = received.shape[0] // 2
    return received[pl.ds(pl.multiple_of((1 - section) * half, 8), half)]


def arrived_sums(arrived):
    return jnp.sum(arrived.reshape(-1, SLOTS, CY), axis=0)


def landed(arrived, sums):
    mine = iota((CY, arrived.shape[0]), 1)
    return pick(one((iota(mine.shape, 0).astype(F32) == sums[5:6]) & ((mine & 7) < CAP)), arrived)


def route_kernel(received, base, scale, cols, pcat, payload):
    section, _, _ = place()
    arrived = arrived_rows(section, received)
    landing = arrived_sums(arrived)[5:6]
    lane = iota(cols.shape[1:], 1)
    gather = one((cols[0] == landing) & ((lane & 7) < CAP))
    tiles = base[...] + scale[...] * pick(gather, arrived)
    outgoing(section, tiles, cols, pcat, payload)


def edge_addends(sums, period, offset):
    masks, values = [], []
    lane = iota((CY, 2 * CY), 1)
    block = ((lane & (CY - 1)) >> 1) + jnp.where(lane >= CY, HALF, 0)
    inside = (lane & (CY - 1)) < 2 * HALF
    for side, shift in ((0, 0), (1, offset)):
        at = iota(lane.shape, 0) * period + shift - block * 8
        masks.append(one((at >= 0) & (at < 8) & ((lane & 1) == side) & inside).astype(jnp.bfloat16))
        sub = (iota((16, CY), 1) * period + shift) & 7
        row = jnp.broadcast_to(sums[6 + side : 7 + side], (16, CY))
        values.append(jnp.where(sub == iota((16, CY), 0), row, 0.0))
    wide = spread(values[0], masks[0]) + spread(values[1], masks[1])
    return wide[0:8, 0:CY], wide[0:8, CY:]


def align_sides(zs, c, lane, sub):
    first, second = zs[c, 0], zs[c, 1]
    top = 2 * HALF
    low_first = jnp.where(lane == top - 2, pltpu.roll(second, top - 2, 1), pltpu.roll(first, CY - 2, 1))
    low_second = pltpu.roll(second, CY - 2, 1)
    high_first = pltpu.roll(first, 2, 1)
    high_second = jnp.where(lane == 1, pltpu.roll(first, CY + 2 - top, 1), pltpu.roll(second, 2, 1))
    for h, (low, high) in enumerate(((low_first, high_first), (low_second, high_second))):
        zs[c, h] = jnp.where(lane & 1 == 0, pltpu.roll(low, 7, 0), pltpu.roll(high, 1, 0))


def read_batch(fields, j):
    return [fields[c][8 * i : 8 * i + 8] for i in range(j, j + BATCH) for c in range(3)]


def write_batch(fields, j, values):
    for n, value in enumerate(values):
        i = j + 1 - BATCH + n // 3
        fields[n % 3][8 * i : 8 * i + 8] = value


def step_kernel(linked, last, *refs):
    cur_in, prev_in, coeff, wet, cols, xr, yra, yrb, mine, *refs = refs
    if linked:
        received, *refs = refs
    cur, prev, *refs = refs
    if last:
        out, zs, full, halos, co, wet_in, sem = refs
    else:
        base, xs, sides, zs, full, halos, co, wet_in, sem, surf = refs
    section, p, q = place()
    lane = iota((8, CY), 1)
    sub = iota((8, CY), 0)
    even_lane = lane & 1 == 0
    groups = ROWS // GROUP
    wet_load = pltpu.make_async_copy(wet, wet_in, sem.at[groups])

    def load(it):
        at = group_rows(it, GROUP)
        return pltpu.make_async_copy(coeff.at[:, at], co.at[:, at], sem.at[it])

    @pl.when(section != 0)
    def _():
        wet_load.start()

    for it in range(groups):
        load(it).start()

    @pl.when((q & 1) == 1)
    def _():
        for c in range(3):
            for h in range(2):
                zs[c, h] = jnp.where(even_lane, yra[c, h], yrb[c, h])

    @pl.when((q & 1) == 0)
    def _():
        for c in range(3):
            for h in range(2):
                zs[c, h] = jnp.where(even_lane, yrb[c, h], yra[c, h])

    there = pl.multiple_of(jnp.where(p == 0, FIRST + ROWS, 0), 8)
    nowhere = pl.multiple_of(jnp.where(p == 0, 0, FIRST + ROWS), 8)
    for c in range(3):
        full[c, pl.ds(there, FIRST)] = xr[c]
        full[c, pl.ds(nowhere, FIRST)] = jnp.zeros((FIRST, CY), F32)

    if linked:
        arrived = arrived_rows(section, received)
        sums = arrived_sums(arrived)
        addend = landed(arrived, sums)
    def widen(it, carry):
        for c in range(3):
            view = full.at[c, group_rows(it, FIRST + GROUP)]
            view[FIRST : FIRST + GROUP] = cur[c, group_rows(it, GROUP)]
        return carry

    def views_of(it, ref):
        return [ref.at[c, group_rows(it, GROUP)] for c in range(ref.shape[0])]

    def padded_of(it):
        return [full.at[c, group_rows(it, GROUP + 2 * FIRST)] for c in range(3)]

    @pl.when(section == 0)
    def _():
        if linked:
            for x in range(CX):
                cur[2, NL * x : NL * x + 1] += addend[x : x + 1]

            @pl.when(p == 0)
            def _():
                full[2, FIRST + ROWS : FIRST + ROWS + 1] += sums[4:5]

            @pl.when(p != 0)
            def _():
                full[2, FIRST - NL : FIRST - NL + 1] += sums[4:5]

            for h, value in enumerate(edge_addends(sums, NL, 0)):
                zs[2, h] += value

        lax.fori_loop(0, groups, widen, 0)
        unpack_sides(zs, halos, (0, 1, 2))

        def group(it, carry):
            load(it).wait()
            sides_of = views_of(it, halos)
            depth = it * GROUP - NL * ((it * GROUP * 656) >> 16) + sub
            fields, old, new_fields, factors = padded_of(it), views_of(it, prev_in), views_of(it, prev), views_of(it, co)
            for j in range(BLOCKS):
                if j % BATCH == 0:
                    olds, news = read_batch(old, j), []
                at = slice(8 * j, 8 * j + 8)
                mu = factors[0][at]
                stiff = factors[1][at] + 2.0 * mu
                layer = depth + 8 * j
                shallowest = (layer == 0) | (layer == NL) | (layer == 2 * NL)
                deepest = (layer == NL - 1) | (layer == 2 * NL - 1)
                for c in range(3):

                    def near(rows):
                        return fields[c][FIRST + 8 * j + rows : FIRST + 8 * j + rows + 8]

                    v = near(0)
                    twice = 2.0 * v
                    above = jnp.where(shallowest, 0.0, near(-1))
                    below = jnp.where(deepest, 0.0, near(1))
                    halo = sides_of[c][at]
                    low = jnp.where(lane == CY - 1, halo, v)
                    high = jnp.where(lane == 0, halo, v)
                    along_first = near(-NL) + near(NL) - twice
                    along_depth = above + below - twice
                    along_second = pltpu.roll(low, 1, 1) + pltpu.roll(high, CY - 1, 1) - twice
                    if c == 0:
                        force = stiff * along_first + mu * (along_depth + along_second)
                    elif c == 1:
                        force = stiff * along_second + mu * (along_first + along_depth)
                    else:
                        force = stiff * along_depth + mu * (along_first + along_second)
                    news.append(twice - olds.pop(0) + force)
                if j % BATCH == BATCH - 1:
                    write_batch(new_fields, j, news)
            return carry

        lax.fori_loop(0, groups, group, 0)
        if not last:
            pack_sides(lambda c, at: prev.at[c, at], sides, (0, 1, 2))

    @pl.when(section != 0)
    def _():
        for c in range(3):
            align_sides(zs, c, lane, sub)
        if linked:
            for h, value in enumerate(edge_addends(sums, REFINE, REFINE - 1)):
                zs[0, h] += zs[1, h] * value
            beside = jnp.broadcast_to(sums[4:5], (8, CY))
            fine_row = jnp.concatenate(
                [
                    jnp.take_along_axis(beside, (((sub + m) * CY + lane) * 6554) >> 16, axis=1)
                    for m in (0, 2)
                ],
                axis=0,
            )

            def add_edge(first):
                for start, rows in ((0, fine_row[0:8]), (8, fine_row[14:16])):
                    at = slice(first + start, first + start + rows.shape[0])
                    full[0, at] += full[2, at] * rows

            @pl.when(p == 0)
            def _():
                add_edge(FIRST + ROWS)

            @pl.when(p != 0)
            def _():
                add_edge(FIRST - REFINE)

        wet_load.wait()
        if linked:
            for start, fine in fine_addend(addend):
                at = pl.ds(start, 8, stride=REFINE)
                cur[0, at] += wet_in[at].astype(F32) * fine
        lax.fori_loop(0, groups, widen, 0)
        unpack_sides(zs, halos, (0, 2))

        def group(it, carry):
            load(it).wait()
            sides_of = views_of(it, halos)
            fields, old, new_fields, factors = padded_of(it), views_of(it, prev_in), views_of(it, prev), views_of(it, co)
            wets = wet_in.at[group_rows(it, GROUP)]
            for j in range(BLOCKS):
                if j % BATCH == 0:
                    olds, news = read_batch(old, j), []
                at = slice(8 * j, 8 * j + 8)
                a = factors[0][at]
                b = factors[1][at]
                w = wets[at].astype(F32)

                def near(c, rows):
                    return fields[c][FIRST + 8 * j + rows : FIRST + 8 * j + rows + 8]

                def across(c):
                    v = near(c, 0)
                    low = jnp.where(lane == CY - 1, near(c, -1), v)
                    high = jnp.where(lane == 0, near(c, 1), v)
                    halo = sides_of[c // 2][at]
                    for s in range(8):
                        if (8 * j + s) % REFINE == 0:
                            low = jnp.where((lane == CY - 1) & (sub == s), halo, low)
                        if (8 * j + s) % REFINE == REFINE - 1:
                            high = jnp.where((lane == 0) & (sub == s), halo, high)
                    return pltpu.roll(high, CY - 1, 1) - pltpu.roll(low, 1, 1)

                def down(c):
                    return near(c, REFINE) - near(c, -REFINE)

                news.append(w * (olds.pop(0) - b * (down(1) + across(2))))
                news.append(w * (olds.pop(0) - a * down(0)))
                news.append(w * (olds.pop(0) - a * across(0)))
                if j % BATCH == BATCH - 1:
                    write_batch(new_fields, j, news)
            return carry

        lax.fori_loop(0, groups, group, 0)
        if not last:
            pack_sides(lambda c, at: prev.at[c, at], sides, (0, 2))
            sides[1] = mine[1]

    if last:
        copy = pltpu.make_async_copy(prev, out, sem.at[0])
        copy.start()
        copy.wait()
    else:
        take_edges(section, p, prev, wet_in, xs)
        surface(section, prev.at[2], prev.at[0], surf)
        base[...] = cols[2] * pick(source_pick(cols), surf[...])


def fine_addend(addend):
    lane = iota((8, CY), 1)
    for m in range(FINE // 8):
        rows = addend[8 * m : 8 * m + 8]
        for k in range(REFINE):
            fine = jnp.take_along_axis(rows, ((lane + k * CY) * 6554) >> 16, axis=1)
            yield 8 * REFINE * m + k, fine


def last_kernel(final_in, fields, wet, received, final, height, wet_in, load_sem, sem):
    section, _, _ = place()
    load = pltpu.make_async_copy(wet, wet_in, load_sem)
    load.start()
    arrived = arrived_rows(section, received)
    addend = landed(arrived, arrived_sums(arrived))
    load.wait()

    @pl.when(section == 0)
    def _():
        copies = []
        for x in range(CX):
            row = NL * x
            first = row // 8 * 8
            height[8 * x : 8 * x + 8] = fields[2, first : first + 8]
            at = 8 * x + row - first
            height[at : at + 1] += addend[x : x + 1]
            copies.append(
                pltpu.make_async_copy(
                    height.at[8 * x : 8 * x + 8], final.at[2, pl.ds(first, 8)], sem.at[x]
                )
            )
        for copy in copies:
            copy.start()
        for copy in copies:
            copy.wait()

    @pl.when(section != 0)
    def _():
        for start, fine in fine_addend(addend):
            at = pl.ds(start, 8, stride=REFINE)
            height[at] = fields[0, at] + wet_in[at].astype(F32) * fine
        copy = pltpu.make_async_copy(height, final.at[0], sem.at[0])
        copy.start()
        copy.wait()


def call(kernel, operands, outs, scratch=(), aliases=None, any_inputs=(), any_outs=(), limit=12, cost=4):
    vmem = pl.BlockSpec(memory_space=pltpu.VMEM)
    anywhere = pl.BlockSpec(memory_space=pl.ANY)
    return pl.pallas_call(
        kernel,
        out_shape=[
            (pltpu.VMEM if kept else jax.ShapeDtypeStruct)(shape, kind[0] if kind else F32)
            for shape, kept, *kind in outs
        ],
        in_specs=[anywhere if i in any_inputs else vmem for i in range(len(operands))],
        out_specs=[anywhere if i in any_outs else vmem for i in range(len(outs))],
        scratch_shapes=list(scratch),
        input_output_aliases=aliases or {},
        compiler_params=pltpu.CompilerParams(vmem_limit_bytes=limit * 1024 * 1024),
        cost_estimate=pl.CostEstimate(flops=cost * 10**9, bytes_accessed=cost * 1024 * 1024, transcendentals=0),
    )(*operands)


def keep(value):
    return pltpu.with_memory_space_constraint(value, pltpu.VMEM)


def outside(value):
    return pltpu.with_memory_space_constraint(value, pltpu.HBM)


def on_device(n_gy, owners, state, previous, coeff, wet_mask, link_dest, link_rows, link_weight):
    links = link_weight.size
    pairs = 2 * owners * SLOTS
    vmem = pltpu.VMEM
    dma = pltpu.SemaphoreType.DMA
    field_shape = (3, ROWS, CY)
    sides_shape = (3, 2, 8, CY)
    fields = (field_shape, True)
    edges = ((3, FIRST, CY), False)
    sides_out = (sides_shape, False)
    tiles = ((links, CY), True)
    surf = vmem((CY, CY), F32)
    wet_in = vmem((ROWS, CY), jnp.int32)
    state, previous = state.reshape(field_shape), previous.reshape(field_shape)
    coeff, wet = outside(coeff.reshape(2, ROWS, CY)), outside(wet_mask.reshape(ROWS, CY))

    def exchange(payload):
        payload = payload.reshape(2 * owners, SLOTS, CY)
        payload = lax.all_to_all(payload, ("sec", "gx", "gy"), 0, 0, tiled=True)
        return payload.reshape(pairs, CY)

    dest, rows, weight = link_dest.reshape(1, links), link_rows.reshape(links, 2).T, link_weight.reshape(1, links)
    payload, cols, pcat, cur, prev, xs, sides, scale = call(
        functools.partial(load_kernel, n_gy),
        [outside(x) for x in (state, previous, wet, dest, rows, weight)],
        [
            ((pairs, CY), False), ((4, links, CY), True), ((owners * SLOTS, CY), True), fields, fields,
            edges, sides_out, tiles,
        ],
        [
            wet_in, vmem((1, links), jnp.int32), vmem((2, links), jnp.int32),
            vmem((1, links), F32), vmem((8, CY), F32), surf, dma((8,)),
        ],
        any_inputs=range(6),
    )
    received = exchange(payload)
    swap = [(0, 1), (1, 0)]
    inner = [(i, i ^ 1) for i in range(n_gy)]
    outer = [(i, j) for k in range(1, n_gy - 1, 2) for i, j in ((k, k + 1), (k + 1, k))]
    before = None
    for step in range(STEPS):
        last = step == STEPS - 1
        xr = lax.ppermute(xs, "gx", swap)
        yra = lax.ppermute(sides, "gy", inner)
        yrb = lax.ppermute(sides, "gy", outer)
        operands = [keep(cur), keep(prev), coeff, wet, keep(cols), xr, yra, yrb, sides]
        if before is not None:
            operands.append(before)
        kernel = functools.partial(step_kernel, before is not None, last)
        scratch = [
            vmem(sides_shape, F32), vmem((3, TOTAL, CY), F32), vmem(field_shape, F32), vmem((2, ROWS, CY), F32),
            wet_in, dma((ROWS // GROUP + 1,)),
        ]
        more = dict(aliases={0: 0, 1: 1}, any_inputs=(2, 3), cost=64)
        if last:
            _, new, final = call(
                kernel, operands, [fields, fields, (field_shape, False)], scratch, any_outs=(2,), **more
            )
        else:
            cur, prev, base, xs, sides = call(
                kernel, operands, [fields, fields, tiles, edges, sides_out], scratch + [surf], **more
            )
            cur, prev = prev, cur
            payload = call(
                route_kernel, (received, keep(base), keep(scale), keep(cols), keep(pcat)),
                [((pairs, CY), False)], limit=4,
            )[0]
            before = received
            received = exchange(payload)
    final = call(
        last_kernel,
        (outside(final), keep(new), wet, received),
        [(field_shape, False)],
        [vmem((ROWS, CY), F32), wet_in, dma, dma((CX,))],
        aliases={0: 0}, any_inputs=(0, 2), any_outs=(0,),
    )[0]
    return final.reshape(1, 3, 1, 1, -1)


def from_partner(value, axis, stride):
    return lax.ppermute(value, axis, [(i, i ^ 1 << stride) for i in range(lax.axis_size(axis))])


def with_halo(block, sides, width):
    for axis, dim in sides:
        count = lax.axis_size(axis)
        forward = [(i, i + 1) for i in range(count - 1)]
        backward = [(target, source) for source, target in forward]
        low = lax.ppermute(
            lax.slice_in_dim(block, block.shape[dim] - width, None, axis=dim), axis, forward
        )
        high = lax.ppermute(lax.slice_in_dim(block, 0, width, axis=dim), axis, backward)
        block = jnp.concatenate([low, block, high], axis=dim)
    return block


def elastic_update(padded, current, previous_field, shear_modulus, lame_first, surface_force):
    own_axis = (0, 2, 1)
    stiffness = lame_first + 2.0 * shear_modulus
    updated_list = []
    for component in range(3):
        displaced = current[component]
        extended = padded[component]
        along_first = extended[2:, :, 1:-1] - 2.0 * displaced + extended[:-2, :, 1:-1]
        deeper = jnp.pad(displaced, ((0, 0), (1, 1), (0, 0)))
        along_depth = deeper[:, 2:, :] - 2.0 * displaced + deeper[:, :-2, :]
        along_second = extended[1:-1, :, 2:] - 2.0 * displaced + extended[1:-1, :, :-2]
        factors = [
            stiffness if own_axis[component] == axis_index else shear_modulus
            for axis_index in range(3)
        ]
        acceleration = (
            factors[0] * along_first + factors[1] * along_depth + factors[2] * along_second
        )
        updated = 2.0 * displaced - previous_field[component] + acceleration
        if component == 2:
            updated = updated.at[:, 0, :].add(surface_force)
        updated_list.append(updated)
    return jnp.stack(updated_list)


def shallow_update(padded, current, previous_field, wave_factor, area_factor, wetness, source):
    fine_rows = REFINE * CX
    fine_cols = REFINE * CY
    sheet = current.reshape(3, fine_rows, fine_cols)
    earlier_sheet = previous_field.reshape(3, fine_rows, fine_cols)
    above = padded[:, 0, (REFINE - 1) * REFINE :, 1:-1].reshape(3, 1, fine_cols)
    below = padded[:, -1, :REFINE, 1:-1].reshape(3, 1, fine_cols)
    left_side = padded[:, 1:-1, REFINE - 1 :: REFINE, 0].reshape(3, fine_rows, 1)
    right_side = padded[:, 1:-1, 0::REFINE, -1].reshape(3, fine_rows, 1)
    by_rows = jnp.concatenate([above, sheet, below], axis=1)
    by_columns = jnp.concatenate([left_side, sheet, right_side], axis=2)

    def rows_diff(channel):
        return by_rows[channel, 2:, :] - by_rows[channel, :-2, :]

    def columns_diff(channel):
        return by_columns[channel, :, 2:] - by_columns[channel, :, :-2]

    flux_first = wetness * (earlier_sheet[1] - wave_factor * rows_diff(0))
    flux_second = wetness * (earlier_sheet[2] - wave_factor * columns_diff(0))
    height = wetness * (earlier_sheet[0] - area_factor * (rows_diff(1) + columns_diff(2)) + source)
    return jnp.stack([height, flux_first, flux_second]).reshape(3, CX, NL, CY)


def route(payload):
    tile_data, tile_rows = payload
    width = tile_data.shape[-1]
    received_data, received_rows = (
        lax.all_to_all(tile_data, ("gx", "gy"), split_axis=0, concat_axis=0, tiled=True),
        lax.all_to_all(tile_rows, ("gx", "gy"), split_axis=0, concat_axis=0, tiled=True),
    )
    return (received_data.reshape(-1, width), received_rows.reshape(-1))


def deliver(outgoing, send_rows):
    crossed = from_partner((outgoing, send_rows), "sec", 0)
    return route(crossed)


def general_on_device(state, previous, coeff, wet_mask, link_dest, link_rows, link_weight):
    section = lax.axis_index("sec")
    owners = lax.axis_size("gx") * lax.axis_size("gy")
    fine_rows = REFINE * CX
    fine_cols = REFINE * CY
    current = state[0, :, 0, 0].reshape(3, CX, NL, CY)
    earlier = previous[0, :, 0, 0].reshape(3, CX, NL, CY)
    first_factor = coeff[0, 0, 0, 0]
    second_factor = coeff[0, 1, 0, 0]
    wetness = wet_mask[0, 0].reshape(fine_rows, fine_cols).astype(jnp.float32)
    targets = link_dest.reshape(-1)
    pairs = link_rows.reshape(-1, 2)
    source_rows = pairs[:, 0]
    landing = pairs[:, 1]
    weights = link_weight.reshape(-1)
    one_hot = (targets[:, None] == jnp.arange(owners, dtype=jnp.int32)[None, :]).astype(jnp.int32)
    before = jnp.cumsum(one_hot, axis=0) - one_hot
    slot_index = jnp.sum(before * one_hot, axis=1)
    position = targets * CAP + slot_index
    send_rows = jnp.zeros((owners * CAP,), jnp.int32).at[position].set(landing).reshape(owners, CAP)
    for step_index in range(STEPS):
        padded = with_halo(current, (("gx", 1), ("gy", 3)), 1)

        def elastic_rows():
            return current[2, :, 0, :][source_rows]

        def shallow_rows():
            picked_fine = current[0].reshape(fine_rows, fine_cols)[source_rows]
            return jnp.sum(picked_fine.reshape(-1, CY, REFINE), axis=-1) / REFINE

        picked = lax.cond(section == 0, elastic_rows, shallow_rows)
        outgoing = (
            jnp.zeros((owners * CAP, CY), jnp.float32).at[position].set(picked * weights[:, None])
        )
        outgoing = outgoing.reshape(owners, CAP, CY)
        arrived, arrived_rows = deliver(outgoing, send_rows)

        def elastic_branch():
            surface_force = jnp.zeros((CX, CY), jnp.float32).at[arrived_rows].add(arrived)
            return elastic_update(
                padded,
                current,
                earlier,
                first_factor.reshape(CX, NL, CY),
                second_factor.reshape(CX, NL, CY),
                surface_force,
            )

        def shallow_branch():
            coarse_source = jnp.zeros((fine_rows, CY), jnp.float32).at[arrived_rows].add(arrived)
            source = jnp.repeat(coarse_source, REFINE, axis=1)
            return shallow_update(
                padded,
                current,
                earlier,
                first_factor.reshape(fine_rows, fine_cols),
                second_factor.reshape(fine_rows, fine_cols),
                wetness,
                source,
            )

        updated = lax.cond(section == 0, elastic_branch, shallow_branch)
        earlier, current = (current, updated)
    return current.reshape(1, 3, 1, 1, -1)


def solution(mesh):
    placed = (
        P("sec", None, "gx", "gy", None),
        P("sec", None, "gx", "gy", None),
        P("sec", None, "gx", "gy", None),
        P("gx", "gy", None),
        P("sec", "gx", "gy", None, None),
        P("sec", "gx", "gy", None, None),
        P("sec", "gx", "gy", None),
    )
    n_gx, n_gy = mesh.shape["gx"], mesh.shape["gy"]
    owners = n_gx * n_gy
    device_program = general_on_device
    if n_gx == 2 and n_gy & (n_gy - 1) == 0 and owners * SLOTS == CY:
        device_program = functools.partial(on_device, n_gy, owners)
    return jax.shard_map(
        device_program,
        mesh=mesh,
        in_specs=placed,
        out_specs=P("sec", None, "gx", "gy", None),
        check_vma=False,
    )
```

```python
import functools

import jax
import jax.numpy as jnp
from jax import lax
from jax.experimental import pallas as pl
from jax.experimental.pallas import tpu as pltpu
from jax.sharding import PartitionSpec as P

CX = 8
CY = 128
REFINE = 10
NL = 100
STEPS = 4
CAP = 4
FINE = REFINE * CX
ROWS = CX * NL
FIRST = 104
TOTAL = FIRST + ROWS + FIRST
SLOTS = 8
BLOCKS = 20
BATCH = 4
GROUP = 8 * BLOCKS
HALF = ROWS // 16
F32 = jnp.float32


def split(x):
    high = x.astype(jnp.bfloat16)
    return high, (x - high.astype(F32)).astype(jnp.bfloat16)


def pick(mask, x):
    parts = jnp.concatenate(split(x), axis=1)
    wide = jnp.dot(mask.astype(jnp.bfloat16), parts, preferred_element_type=F32)
    return wide[:, 0 : x.shape[1]] + wide[:, x.shape[1] :]


def spread(x, mask):
    tall = jnp.dot(jnp.concatenate(split(x), axis=0), mask, preferred_element_type=F32)
    return tall[0 : x.shape[0]] + tall[x.shape[0] :]


def iota(shape, dim):
    return lax.broadcasted_iota(jnp.int32, shape, dim)


def one(mask):
    return jnp.where(mask, 1.0, 0.0).astype(F32)


def place():
    return lax.axis_index("sec"), lax.axis_index("gx"), lax.axis_index("gy")


def average(rows_of):
    total = jnp.zeros((FINE, CY), F32)
    for m in range(REFINE):
        fine = iota((CY, CY), 0) + m * CY
        first = iota((CY, CY), 1) * REFINE
        mask = one((fine >= first) & (fine < first + REFINE)).astype(jnp.bfloat16)
        total = total + spread(rows_of(m), mask)
    return total / REFINE


def surface(section, elastic, sheet, surf):
    surf[...] = jnp.zeros_like(surf)

    @pl.when(section == 0)
    def _():
        surf[0:CX] = elastic[pl.ds(0, CX, stride=NL)]

    @pl.when(section != 0)
    def _():
        surf[0:FINE] = average(lambda m: sheet[pl.ds(m, FINE, stride=REFINE)])


def source_pick(cols):
    return one(cols[0] == iota((cols.shape[1], CY), 1).astype(F32))


def outgoing(section, tiles, cols, pcat, packed, payload, sem):
    half = packed.shape[0]
    lanes = tiles.shape
    last = jnp.broadcast_to(tiles[:, CY - 1 : CY], lanes) * cols[1]
    first = jnp.broadcast_to(tiles[:, 0:1], lanes) * cols[1]
    packed[...] = pick(pcat[...], jnp.concatenate([tiles, last, first, cols[3]], axis=0))
    there = payload.at[pl.ds(pl.multiple_of((1 - section) * half, 8), half)]
    copy = pltpu.make_async_copy(packed, there, sem)
    copy.start()
    return copy


def link_tables(section, me, n_gy, dest, rows, weight, lines, cols, pcat):
    links = dest.shape[1]
    lines[...] = jnp.zeros_like(lines)
    lines[0:1, 0:links] = dest[...].astype(F32)
    lines[1:3, 0:links] = rows[...].astype(F32)
    lines[3:4, 0:links] = weight[...]
    x = lines[...]
    eye = one(iota((links, CY), 0) == iota((links, CY), 1))

    def column(i):
        return jnp.sum(eye * x[i : i + 1], axis=1, keepdims=True)

    target, source, landing, weights = [column(i) for i in range(4)]
    same = one(target == x[0:1])
    at = iota((links, CY), 0)
    other = iota((links, CY), 1)
    inside = one(other < links)
    slot_row = jnp.sum(same * one(at < other) * inside, axis=0, keepdims=True)
    slot = jnp.sum(same * one(other < at) * inside, axis=1, keepdims=True)
    lane = other.astype(F32)
    cols[0] = jnp.broadcast_to(source, (links, CY))
    cols[1] = one(landing == lane)
    cols[2] = jnp.broadcast_to(weights, (links, CY))
    cols[3] = landing * one(lane == slot + (me * SLOTS).astype(F32))
    y = jnp.concatenate([x[0:3], slot_row, jnp.zeros((4, CY), F32)], axis=0)
    y = y + pltpu.roll(y, links, 1) + pltpu.roll(y, 2 * links, 1) + pltpu.roll(y, 3 * links, 1)
    shape = (pcat.shape[0], CY)
    owner = iota(shape, 0) >> 3
    part = iota(shape, 0) & 7
    group = iota(shape, 1) >> (links.bit_length() - 1)
    to = y[0:1]
    row = y[2:3]
    order = y[3:4]
    beside = jnp.where(owner < n_gy, owner + n_gy, owner - n_gy).astype(F32)
    bottom = jnp.where(section == 0, FINE - 1, CX - 1).astype(F32)
    edge = jnp.where(owner < n_gy, 0.0, bottom)
    along = owner & (n_gy - 1)
    own = owner.astype(F32)
    chosen = one((group == 0) & (part == order.astype(jnp.int32)) & (part < CAP) & (to == own))
    chosen += one((group == 0) & (part == 4) & (to == beside) & (row == edge))
    chosen += one((group == 1) & (part == 6) & (to == own - 1.0) & (along > 0))
    chosen += one((group == 2) & (part == 7) & (to == own + 1.0) & (along < n_gy - 1))
    chosen += one((group == 3) & (part == 5) & (to == own))
    pcat[...] = chosen


def pack_sides(values_of, sides, channels):
    lane = iota((8, CY), 1)

    def half_of(h, carry):
        acc = {c: jnp.zeros((8, CY), F32) for c in channels}
        views = {c: values_of(c, pl.ds(pl.multiple_of(h * HALF * 8, 8), HALF * 8)) for c in channels}
        for b in range(HALF):
            for c in channels:
                value = views[c][8 * b : 8 * b + 8].astype(F32)
                acc[c] = jnp.where(lane >> 1 == b, pltpu.roll(value, 2 * b + 1, 1), acc[c])
        for c in channels:
            sides[c, h] = acc[c]
        return carry

    lax.fori_loop(0, 2, half_of, 0)


def unpack_sides(zs, halos, channels):
    def half_of(h, carry):
        for i, c in enumerate(channels):
            value = zs[c, h]
            view = halos.at[i, pl.ds(pl.multiple_of(h * HALF * 8, 8), HALF * 8)]
            for b in range(HALF):
                view[8 * b : 8 * b + 8] = pltpu.roll(value, CY - 1 - 2 * b, 1)
        return carry

    lax.fori_loop(0, 2, half_of, 0)


def take_edges(section, p, fields, wet, xs):
    start = pl.multiple_of(jnp.where(p == 0, ROWS - FIRST, 0), 8)
    for c in range(3):
        xs[c] = fields[c, pl.ds(start, FIRST)]

    @pl.when(section != 0)
    def _():
        xs[2] = wet[pl.ds(start, FIRST)].astype(F32)


def load_kernel(n_gy, state, previous, wet, dest, rows, weight, payload, cols, pcat, cur, prev, xs, sides, wet_in, dest_in, rows_in, weight_in, lines, surf, packed, sem):
    section, p, q = place()
    pairs = [(dest, dest_in), (rows, rows_in), (weight, weight_in)]
    pairs += [(state.at[c], cur.at[c]) for c in (2, 0, 1)]
    pairs += [(wet, wet_in), (previous, prev)]
    copies = [pltpu.make_async_copy(a, b, sem.at[i]) for i, (a, b) in enumerate(pairs)]
    for copy in copies:
        copy.start()
    for copy in copies[0:3]:
        copy.wait()
    link_tables(section, p * n_gy + q, n_gy, dest_in, rows_in, weight_in, lines, cols, pcat)
    for copy in copies[3:7]:
        copy.wait()
    surface(section, cur.at[2], cur.at[0], surf)
    tiles = cols[2] * pick(source_pick(cols), surf[...])
    copies.append(outgoing(section, tiles, cols, pcat, packed, payload, sem.at[8]))

    @pl.when(section == 0)
    def _():
        pack_sides(lambda c, at: cur.at[c, at], sides, (0, 1, 2))

    @pl.when(section != 0)
    def _():
        pack_sides(lambda c, at: wet_in.at[at] if c == 1 else cur.at[c, at], sides, (0, 1, 2))

    take_edges(section, p, cur, wet_in, xs)
    for copy in copies[7:]:
        copy.wait()


def group_rows(it, rows):
    return pl.ds(pl.multiple_of(it * GROUP, 8), rows)


def arrived_rows(section, received):
    half = received.shape[0] // 2
    return received[pl.ds(pl.multiple_of((1 - section) * half, 8), half)]


def arrived_sums(arrived):
    return jnp.sum(arrived.reshape(-1, SLOTS, CY), axis=0)


def landed(arrived, sums):
    mine = iota((CY, arrived.shape[0]), 1)
    return pick(one((iota(mine.shape, 0).astype(F32) == sums[5:6]) & ((mine & 7) < CAP)), arrived)


def route_kernel(received, base, scale, cols, pcat, payload, packed, sem):
    section, _, _ = place()
    arrived = arrived_rows(section, received)
    landing = arrived_sums(arrived)[5:6]
    lane = iota(cols.shape[1:], 1)
    gather = one((cols[0] == landing) & ((lane & 7) < CAP))
    tiles = base[...] + scale[...] * pick(gather, arrived)
    outgoing(section, tiles, cols, pcat, packed, payload, sem).wait()


def edge_addends(sums, period, offset):
    masks, values = [], []
    lane = iota((CY, 2 * CY), 1)
    block = ((lane & (CY - 1)) >> 1) + jnp.where(lane >= CY, HALF, 0)
    inside = (lane & (CY - 1)) < 2 * HALF
    for side, shift in ((0, 0), (1, offset)):
        at = iota(lane.shape, 0) * period + shift - block * 8
        masks.append(one((at >= 0) & (at < 8) & ((lane & 1) == side) & inside).astype(jnp.bfloat16))
        sub = (iota((16, CY), 1) * period + shift) & 7
        row = jnp.broadcast_to(sums[6 + side : 7 + side], (16, CY))
        values.append(jnp.where(sub == iota((16, CY), 0), row, 0.0))
    wide = spread(values[0], masks[0]) + spread(values[1], masks[1])
    return wide[0:8, 0:CY], wide[0:8, CY:]


def align_sides(zs, c, lane, sub):
    first, second = zs[c, 0], zs[c, 1]
    top = 2 * HALF
    low_first = jnp.where(lane == top - 2, pltpu.roll(second, top - 2, 1), pltpu.roll(first, CY - 2, 1))
    low_second = pltpu.roll(second, CY - 2, 1)
    high_first = pltpu.roll(first, 2, 1)
    high_second = jnp.where(lane == 1, pltpu.roll(first, CY + 2 - top, 1), pltpu.roll(second, 2, 1))
    for h, (low, high) in enumerate(((low_first, high_first), (low_second, high_second))):
        zs[c, h] = jnp.where(lane & 1 == 0, pltpu.roll(low, 7, 0), pltpu.roll(high, 1, 0))


def read_batch(fields, j):
    return [fields[c][8 * i : 8 * i + 8] for i in range(j, j + BATCH) for c in range(3)]


def write_batch(fields, j, values):
    for n, value in enumerate(values):
        i = j + 1 - BATCH + n // 3
        fields[n % 3][8 * i : 8 * i + 8] = value


def step_kernel(linked, last, *refs):
    cur_in, prev_in, coeff, wet, cols, xr, yra, yrb, mine, *refs = refs
    if linked:
        received, *refs = refs
    cur, prev, *refs = refs
    if last:
        out, wet_out, zs, full, halos, co, wet_in, sem = refs
    else:
        base, xs, sides, *refs = refs
        if not linked:
            scale, *refs = refs
        zs, full, halos, co, wet_in, sem, surf = refs
    section, p, q = place()
    lane = iota((8, CY), 1)
    sub = iota((8, CY), 0)
    even_lane = lane & 1 == 0
    groups = ROWS // GROUP
    wet_load = pltpu.make_async_copy(wet, wet_in, sem.at[groups])

    def load(it):
        at = group_rows(it, GROUP)
        return pltpu.make_async_copy(coeff.at[:, at], co.at[:, at], sem.at[it])

    @pl.when(section != 0)
    def _():
        wet_load.start()

    for it in range(groups):
        load(it).start()

    @pl.when((q & 1) == 1)
    def _():
        for c in range(3):
            for h in range(2):
                zs[c, h] = jnp.where(even_lane, yra[c, h], yrb[c, h])

    @pl.when((q & 1) == 0)
    def _():
        for c in range(3):
            for h in range(2):
                zs[c, h] = jnp.where(even_lane, yrb[c, h], yra[c, h])

    there = pl.multiple_of(jnp.where(p == 0, FIRST + ROWS, 0), 8)
    nowhere = pl.multiple_of(jnp.where(p == 0, 0, FIRST + ROWS), 8)
    for c in range(3):
        full[c, pl.ds(there, FIRST)] = xr[c]
        full[c, pl.ds(nowhere, FIRST)] = jnp.zeros((FIRST, CY), F32)

    if linked:
        arrived = arrived_rows(section, received)
        sums = arrived_sums(arrived)
        addend = landed(arrived, sums)
    def widen(it, carry):
        for c in range(3):
            view = full.at[c, group_rows(it, FIRST + GROUP)]
            view[FIRST : FIRST + GROUP] = cur[c, group_rows(it, GROUP)]
        return carry

    if last:

        @pl.when(section == 0)
        def _():
            wet_out[...] = jnp.zeros_like(wet_out)

    def views_of(it, ref):
        return [ref.at[c, group_rows(it, GROUP)] for c in range(ref.shape[0])]

    def padded_of(it):
        return [full.at[c, group_rows(it, GROUP + 2 * FIRST)] for c in range(3)]

    @pl.when(section == 0)
    def _():
        if linked:
            for x in range(CX):
                cur[2, NL * x : NL * x + 1] += addend[x : x + 1]

            @pl.when(p == 0)
            def _():
                full[2, FIRST + ROWS : FIRST + ROWS + 1] += sums[4:5]

            @pl.when(p != 0)
            def _():
                full[2, FIRST - NL : FIRST - NL + 1] += sums[4:5]

            for h, value in enumerate(edge_addends(sums, NL, 0)):
                zs[2, h] += value

        lax.fori_loop(0, groups, widen, 0)
        unpack_sides(zs, halos, (0, 1, 2))

        def group(it, carry):
            load(it).wait()
            sides_of = views_of(it, halos)
            depth = it * GROUP - NL * ((it * GROUP * 656) >> 16) + sub
            fields, old, new_fields, factors = padded_of(it), views_of(it, prev_in), views_of(it, prev), views_of(it, co)
            for j in range(BLOCKS):
                if j % BATCH == 0:
                    olds, news = read_batch(old, j), []
                at = slice(8 * j, 8 * j + 8)
                mu = factors[0][at]
                stiff = factors[1][at] + 2.0 * mu
                layer = depth + 8 * j
                shallowest = (layer == 0) | (layer == NL) | (layer == 2 * NL)
                deepest = (layer == NL - 1) | (layer == 2 * NL - 1)
                for c in range(3):

                    def near(rows):
                        return fields[c][FIRST + 8 * j + rows : FIRST + 8 * j + rows + 8]

                    v = near(0)
                    twice = 2.0 * v
                    above = jnp.where(shallowest, 0.0, near(-1))
                    below = jnp.where(deepest, 0.0, near(1))
                    halo = sides_of[c][at]
                    low = jnp.where(lane == CY - 1, halo, v)
                    high = jnp.where(lane == 0, halo, v)
                    along_first = near(-NL) + near(NL) - twice
                    along_depth = above + below - twice
                    along_second = pltpu.roll(low, 1, 1) + pltpu.roll(high, CY - 1, 1) - twice
                    if c == 0:
                        force = stiff * along_first + mu * (along_depth + along_second)
                    elif c == 1:
                        force = stiff * along_second + mu * (along_first + along_depth)
                    else:
                        force = stiff * along_depth + mu * (along_first + along_second)
                    news.append(twice - olds.pop(0) + force)
                if j % BATCH == BATCH - 1:
                    write_batch(new_fields, j, news)
            return carry

        lax.fori_loop(0, groups, group, 0)
        if not last:
            pack_sides(lambda c, at: prev.at[c, at], sides, (0, 1, 2))

    @pl.when(section != 0)
    def _():
        for c in range(3):
            align_sides(zs, c, lane, sub)
        if linked:
            for h, value in enumerate(edge_addends(sums, REFINE, REFINE - 1)):
                zs[0, h] += zs[1, h] * value
            beside = jnp.broadcast_to(sums[4:5], (8, CY))
            fine_row = jnp.concatenate(
                [
                    jnp.take_along_axis(beside, (((sub + m) * CY + lane) * 6554) >> 16, axis=1)
                    for m in (0, 2)
                ],
                axis=0,
            )

            def add_edge(first):
                for start, rows in ((0, fine_row[0:8]), (8, fine_row[14:16])):
                    at = slice(first + start, first + start + rows.shape[0])
                    full[0, at] += full[2, at] * rows

            @pl.when(p == 0)
            def _():
                add_edge(FIRST + ROWS)

            @pl.when(p != 0)
            def _():
                add_edge(FIRST - REFINE)

        unpack_sides(zs, halos, (0, 2))
        lax.fori_loop(0, groups, widen, 0)
        wet_load.wait()
        if linked:
            for start, fine in fine_addend(addend):
                at = pl.ds(start, 8, stride=REFINE)
                value = cur[0, at] + wet_in[at].astype(F32) * fine
                cur[0, at] = value
                full[0, pl.ds(FIRST + start, 8, stride=REFINE)] = value
        if last:
            wet_out[...] = wet_in[...]

        def group(it, carry):
            load(it).wait()
            sides_of = views_of(it, halos)
            fields, old, new_fields, factors = padded_of(it), views_of(it, prev_in), views_of(it, prev), views_of(it, co)
            wets = wet_in.at[group_rows(it, GROUP)]
            for j in range(BLOCKS):
                if j % BATCH == 0:
                    olds, news = read_batch(old, j), []
                at = slice(8 * j, 8 * j + 8)
                a = factors[0][at]
                b = factors[1][at]
                w = wets[at].astype(F32)

                def near(c, rows):
                    return fields[c][FIRST + 8 * j + rows : FIRST + 8 * j + rows + 8]

                def across(c):
                    v = near(c, 0)
                    low = jnp.where(lane == CY - 1, near(c, -1), v)
                    high = jnp.where(lane == 0, near(c, 1), v)
                    halo = sides_of[c // 2][at]
                    for s in range(8):
                        if (8 * j + s) % REFINE == 0:
                            low = jnp.where((lane == CY - 1) & (sub == s), halo, low)
                        if (8 * j + s) % REFINE == REFINE - 1:
                            high = jnp.where((lane == 0) & (sub == s), halo, high)
                    return pltpu.roll(high, CY - 1, 1) - pltpu.roll(low, 1, 1)

                def down(c):
                    return near(c, REFINE) - near(c, -REFINE)

                news.append(w * (olds.pop(0) - b * (down(1) + across(2))))
                news.append(w * (olds.pop(0) - a * down(0)))
                news.append(w * (olds.pop(0) - a * across(0)))
                if j % BATCH == BATCH - 1:
                    write_batch(new_fields, j, news)
            return carry

        lax.fori_loop(0, groups, group, 0)
        if not last:
            pack_sides(lambda c, at: prev.at[c, at], sides, (0, 2))
            sides[1] = mine[1]

    if last:
        copy = pltpu.make_async_copy(prev, out, sem.at[0])
        copy.start()
        copy.wait()
    else:
        take_edges(section, p, prev, wet_in, xs)
        surface(section, prev.at[2], prev.at[0], surf)
        base[...] = cols[2] * pick(source_pick(cols), surf[...])
    if not linked:
        scale[...] = cols[2]

        @pl.when(section != 0)
        def _():
            surf[0:FINE] = average(lambda m: wet_in[pl.ds(m, FINE, stride=REFINE)].astype(F32))
            scale[...] = cols[2] * pick(source_pick(cols), surf[...])


def fine_addend(addend):
    lane = iota((8, CY), 1)
    for m in range(FINE // 8):
        rows = addend[8 * m : 8 * m + 8]
        for k in range(REFINE):
            fine = jnp.take_along_axis(rows, ((lane + k * CY) * 6554) >> 16, axis=1)
            yield 8 * REFINE * m + k, fine


def last_kernel(final_in, fields, wet, received, final, height, sem):
    section, _, _ = place()
    arrived = arrived_rows(section, received)
    addend = landed(arrived, arrived_sums(arrived))

    @pl.when(section == 0)
    def _():
        copies = []
        for x in range(CX):
            row = NL * x
            first = row // 8 * 8
            height[8 * x : 8 * x + 8] = fields[2, first : first + 8]
            at = 8 * x + row - first
            height[at : at + 1] += addend[x : x + 1]
            copies.append(
                pltpu.make_async_copy(
                    height.at[8 * x : 8 * x + 8], final.at[2, pl.ds(first, 8)], sem.at[x]
                )
            )
        for copy in copies:
            copy.start()
        for copy in copies:
            copy.wait()

    @pl.when(section != 0)
    def _():
        part = 8 * REFINE
        copies = []
        for start, fine in fine_addend(addend):
            at = pl.ds(start, 8, stride=REFINE)
            height[at] = fields[0, at] + wet[at].astype(F32) * fine
            if start % part == REFINE - 1:
                rows = pl.ds(start // part * part, part)
                copies.append(pltpu.make_async_copy(height.at[rows], final.at[0, rows], sem.at[len(copies)]))
                copies[-1].start()
        for copy in copies:
            copy.wait()


def call(kernel, operands, outs, scratch=(), aliases=None, any_inputs=(), any_outs=(), limit=12, cost=4):
    vmem = pl.BlockSpec(memory_space=pltpu.VMEM)
    anywhere = pl.BlockSpec(memory_space=pl.ANY)
    return pl.pallas_call(
        kernel,
        out_shape=[
            (pltpu.VMEM if kept else jax.ShapeDtypeStruct)(shape, kind[0] if kind else F32)
            for shape, kept, *kind in outs
        ],
        in_specs=[anywhere if i in any_inputs else vmem for i in range(len(operands))],
        out_specs=[anywhere if i in any_outs else vmem for i in range(len(outs))],
        scratch_shapes=list(scratch),
        input_output_aliases=aliases or {},
        compiler_params=pltpu.CompilerParams(vmem_limit_bytes=limit * 1024 * 1024),
        cost_estimate=pl.CostEstimate(flops=cost * 10**9, bytes_accessed=cost * 1024 * 1024, transcendentals=0),
    )(*operands)


def keep(value):
    return pltpu.with_memory_space_constraint(value, pltpu.VMEM)


def outside(value):
    return pltpu.with_memory_space_constraint(value, pltpu.HBM)


def on_device(n_gy, owners, state, previous, coeff, wet_mask, link_dest, link_rows, link_weight):
    links = link_weight.size
    pairs = 2 * owners * SLOTS
    vmem = pltpu.VMEM
    dma = pltpu.SemaphoreType.DMA
    field_shape = (3, ROWS, CY)
    sides_shape = (3, 2, 8, CY)
    fields = (field_shape, True)
    edges = ((3, FIRST, CY), False)
    sides_out = (sides_shape, False)
    tiles = ((links, CY), True)
    surf = vmem((CY, CY), F32)
    wet_in = vmem((ROWS, CY), jnp.int32)
    state, previous = state.reshape(field_shape), previous.reshape(field_shape)
    coeff, wet = outside(coeff.reshape(2, ROWS, CY)), outside(wet_mask.reshape(ROWS, CY))

    def exchange(payload):
        payload = payload.reshape(2 * owners, SLOTS, CY)
        payload = lax.all_to_all(payload, ("sec", "gx", "gy"), 0, 0, tiled=True)
        return payload.reshape(pairs, CY)

    dest, rows, weight = link_dest.reshape(1, links), link_rows.reshape(links, 2).T, link_weight.reshape(1, links)
    payload, cols, pcat, cur, prev, xs, sides = call(
        functools.partial(load_kernel, n_gy),
        [outside(x) for x in (state, previous, wet, dest, rows, weight)],
        [
            ((pairs, CY), False), ((4, links, CY), True), ((owners * SLOTS, CY), True), fields, fields,
            edges, sides_out,
        ],
        [
            wet_in, vmem((1, links), jnp.int32), vmem((2, links), jnp.int32),
            vmem((1, links), F32), vmem((8, CY), F32), surf, vmem((owners * SLOTS, CY), F32), dma((9,)),
        ],
        any_inputs=range(6), any_outs=(0,),
    )
    received = exchange(payload)
    swap = [(0, 1), (1, 0)]
    inner = [(i, i ^ 1) for i in range(n_gy)]
    outer = [(i, j) for k in range(1, n_gy - 1, 2) for i, j in ((k, k + 1), (k + 1, k))]
    before = None
    for step in range(STEPS):
        last = step == STEPS - 1
        xr = lax.ppermute(xs, "gx", swap)
        yra = lax.ppermute(sides, "gy", inner)
        yrb = lax.ppermute(sides, "gy", outer)
        operands = [keep(cur), keep(prev), coeff, wet, keep(cols), xr, yra, yrb, sides]
        if before is not None:
            operands.append(before)
        kernel = functools.partial(step_kernel, before is not None, last)
        scratch = [
            vmem(sides_shape, F32), vmem((3, TOTAL, CY), F32), vmem(field_shape, F32), vmem((2, ROWS, CY), F32),
            wet_in, dma((ROWS // GROUP + 1,)),
        ]
        more = dict(aliases={0: 0, 1: 1}, any_inputs=(2, 3), cost=64)
        if last:
            _, new, final, wet_kept = call(
                kernel, operands, [fields, fields, (field_shape, False), ((ROWS, CY), True, jnp.int32)], scratch,
                any_outs=(2,), **more
            )
        else:
            outs = [fields, fields, tiles, edges, sides_out] + [tiles] * (before is None)
            prev, cur, base, xs, sides, *first = call(kernel, operands, outs, scratch + [surf], **more)
            if first:
                scale = first[0]
            payload = call(
                route_kernel, (received, keep(base), keep(scale), keep(cols), keep(pcat)),
                [((pairs, CY), False)], [vmem((owners * SLOTS, CY), F32), dma], any_outs=(0,), limit=4,
            )[0]
            before = received
            received = exchange(payload)
    final = call(
        last_kernel,
        (outside(final), keep(new), keep(wet_kept), received),
        [(field_shape, False)],
        [vmem((ROWS, CY), F32), dma((FINE // 8,))],
        aliases={0: 0}, any_inputs=(0,), any_outs=(0,),
    )[0]
    return final.reshape(1, 3, 1, 1, -1)


def from_partner(value, axis, stride):
    return lax.ppermute(value, axis, [(i, i ^ 1 << stride) for i in range(lax.axis_size(axis))])


def with_halo(block, sides, width):
    for axis, dim in sides:
        count = lax.axis_size(axis)
        forward = [(i, i + 1) for i in range(count - 1)]
        backward = [(target, source) for source, target in forward]
        low = lax.ppermute(
            lax.slice_in_dim(block, block.shape[dim] - width, None, axis=dim), axis, forward
        )
        high = lax.ppermute(lax.slice_in_dim(block, 0, width, axis=dim), axis, backward)
        block = jnp.concatenate([low, block, high], axis=dim)
    return block


def elastic_update(padded, current, previous_field, shear_modulus, lame_first, surface_force):
    own_axis = (0, 2, 1)
    stiffness = lame_first + 2.0 * shear_modulus
    updated_list = []
    for component in range(3):
        displaced = current[component]
        extended = padded[component]
        along_first = extended[2:, :, 1:-1] - 2.0 * displaced + extended[:-2, :, 1:-1]
        deeper = jnp.pad(displaced, ((0, 0), (1, 1), (0, 0)))
        along_depth = deeper[:, 2:, :] - 2.0 * displaced + deeper[:, :-2, :]
        along_second = extended[1:-1, :, 2:] - 2.0 * displaced + extended[1:-1, :, :-2]
        factors = [
            stiffness if own_axis[component] == axis_index else shear_modulus
            for axis_index in range(3)
        ]
        acceleration = (
            factors[0] * along_first + factors[1] * along_depth + factors[2] * along_second
        )
        updated = 2.0 * displaced - previous_field[component] + acceleration
        if component == 2:
            updated = updated.at[:, 0, :].add(surface_force)
        updated_list.append(updated)
    return jnp.stack(updated_list)


def shallow_update(padded, current, previous_field, wave_factor, area_factor, wetness, source):
    fine_rows = REFINE * CX
    fine_cols = REFINE * CY
    sheet = current.reshape(3, fine_rows, fine_cols)
    earlier_sheet = previous_field.reshape(3, fine_rows, fine_cols)
    above = padded[:, 0, (REFINE - 1) * REFINE :, 1:-1].reshape(3, 1, fine_cols)
    below = padded[:, -1, :REFINE, 1:-1].reshape(3, 1, fine_cols)
    left_side = padded[:, 1:-1, REFINE - 1 :: REFINE, 0].reshape(3, fine_rows, 1)
    right_side = padded[:, 1:-1, 0::REFINE, -1].reshape(3, fine_rows, 1)
    by_rows = jnp.concatenate([above, sheet, below], axis=1)
    by_columns = jnp.concatenate([left_side, sheet, right_side], axis=2)

    def rows_diff(channel):
        return by_rows[channel, 2:, :] - by_rows[channel, :-2, :]

    def columns_diff(channel):
        return by_columns[channel, :, 2:] - by_columns[channel, :, :-2]

    flux_first = wetness * (earlier_sheet[1] - wave_factor * rows_diff(0))
    flux_second = wetness * (earlier_sheet[2] - wave_factor * columns_diff(0))
    height = wetness * (earlier_sheet[0] - area_factor * (rows_diff(1) + columns_diff(2)) + source)
    return jnp.stack([height, flux_first, flux_second]).reshape(3, CX, NL, CY)


def route(payload):
    tile_data, tile_rows = payload
    width = tile_data.shape[-1]
    received_data, received_rows = (
        lax.all_to_all(tile_data, ("gx", "gy"), split_axis=0, concat_axis=0, tiled=True),
        lax.all_to_all(tile_rows, ("gx", "gy"), split_axis=0, concat_axis=0, tiled=True),
    )
    return (received_data.reshape(-1, width), received_rows.reshape(-1))


def deliver(outgoing, send_rows):
    crossed = from_partner((outgoing, send_rows), "sec", 0)
    return route(crossed)


def general_on_device(state, previous, coeff, wet_mask, link_dest, link_rows, link_weight):
    section = lax.axis_index("sec")
    owners = lax.axis_size("gx") * lax.axis_size("gy")
    fine_rows = REFINE * CX
    fine_cols = REFINE * CY
    current = state[0, :, 0, 0].reshape(3, CX, NL, CY)
    earlier = previous[0, :, 0, 0].reshape(3, CX, NL, CY)
    first_factor = coeff[0, 0, 0, 0]
    second_factor = coeff[0, 1, 0, 0]
    wetness = wet_mask[0, 0].reshape(fine_rows, fine_cols).astype(jnp.float32)
    targets = link_dest.reshape(-1)
    pairs = link_rows.reshape(-1, 2)
    source_rows = pairs[:, 0]
    landing = pairs[:, 1]
    weights = link_weight.reshape(-1)
    one_hot = (targets[:, None] == jnp.arange(owners, dtype=jnp.int32)[None, :]).astype(jnp.int32)
    before = jnp.cumsum(one_hot, axis=0) - one_hot
    slot_index = jnp.sum(before * one_hot, axis=1)
    position = targets * CAP + slot_index
    send_rows = jnp.zeros((owners * CAP,), jnp.int32).at[position].set(landing).reshape(owners, CAP)
    for step_index in range(STEPS):
        padded = with_halo(current, (("gx", 1), ("gy", 3)), 1)

        def elastic_rows():
            return current[2, :, 0, :][source_rows]

        def shallow_rows():
            picked_fine = current[0].reshape(fine_rows, fine_cols)[source_rows]
            return jnp.sum(picked_fine.reshape(-1, CY, REFINE), axis=-1) / REFINE

        picked = lax.cond(section == 0, elastic_rows, shallow_rows)
        outgoing = (
            jnp.zeros((owners * CAP, CY), jnp.float32).at[position].set(picked * weights[:, None])
        )
        outgoing = outgoing.reshape(owners, CAP, CY)
        arrived, arrived_rows = deliver(outgoing, send_rows)

        def elastic_branch():
            surface_force = jnp.zeros((CX, CY), jnp.float32).at[arrived_rows].add(arrived)
            return elastic_update(
                padded,
                current,
                earlier,
                first_factor.reshape(CX, NL, CY),
                second_factor.reshape(CX, NL, CY),
                surface_force,
            )

        def shallow_branch():
            coarse_source = jnp.zeros((fine_rows, CY), jnp.float32).at[arrived_rows].add(arrived)
            source = jnp.repeat(coarse_source, REFINE, axis=1)
            return shallow_update(
                padded,
                current,
                earlier,
                first_factor.reshape(fine_rows, fine_cols),
                second_factor.reshape(fine_rows, fine_cols),
                wetness,
                source,
            )

        updated = lax.cond(section == 0, elastic_branch, shallow_branch)
        earlier, current = (current, updated)
    return current.reshape(1, 3, 1, 1, -1)


def solution(mesh):
    placed = (
        P("sec", None, "gx", "gy", None),
        P("sec", None, "gx", "gy", None),
        P("sec", None, "gx", "gy", None),
        P("gx", "gy", None),
        P("sec", "gx", "gy", None, None),
        P("sec", "gx", "gy", None, None),
        P("sec", "gx", "gy", None),
    )
    n_gx, n_gy = mesh.shape["gx"], mesh.shape["gy"]
    owners = n_gx * n_gy
    device_program = general_on_device
    if n_gx == 2 and n_gy & (n_gy - 1) == 0 and owners * SLOTS == CY:
        device_program = functools.partial(on_device, n_gy, owners)
    return jax.shard_map(
        device_program,
        mesh=mesh,
        in_specs=placed,
        out_specs=P("sec", None, "gx", "gy", None),
        check_vma=False,
    )
```

```python
import functools

import jax
import jax.numpy as jnp
from jax import lax
from jax.experimental import pallas as pl
from jax.experimental.pallas import tpu as pltpu
from jax.sharding import PartitionSpec as P

CX = 8
CY = 128
REFINE = 10
NL = 100
STEPS = 4
CAP = 4
FINE = REFINE * CX
ROWS = CX * NL
FIRST = 104
TOTAL = FIRST + ROWS + FIRST
SLOTS = 8
BLOCKS = 20
BATCH = 4
GROUP = 8 * BLOCKS
HALF = ROWS // 16
F32 = jnp.float32


def split(x):
    high = x.astype(jnp.bfloat16)
    return high, (x - high.astype(F32)).astype(jnp.bfloat16)


def pick(mask, x):
    parts = jnp.concatenate(split(x), axis=1)
    wide = jnp.dot(mask.astype(jnp.bfloat16), parts, preferred_element_type=F32)
    return wide[:, 0 : x.shape[1]] + wide[:, x.shape[1] :]


def spread(x, mask):
    tall = jnp.dot(jnp.concatenate(split(x), axis=0), mask, preferred_element_type=F32)
    return tall[0 : x.shape[0]] + tall[x.shape[0] :]


def iota(shape, dim):
    return lax.broadcasted_iota(jnp.int32, shape, dim)


def one(mask):
    return jnp.where(mask, 1.0, 0.0).astype(F32)


def place():
    return lax.axis_index("sec"), lax.axis_index("gx"), lax.axis_index("gy")


def average(rows_of):
    total = jnp.zeros((FINE, CY), F32)
    for m in range(REFINE):
        fine = iota((CY, CY), 0) + m * CY
        first = iota((CY, CY), 1) * REFINE
        mask = one((fine >= first) & (fine < first + REFINE)).astype(jnp.bfloat16)
        total = total + spread(rows_of(m), mask)
    return total / REFINE


def surface(section, elastic, sheet, surf):
    surf[...] = jnp.zeros_like(surf)

    @pl.when(section == 0)
    def _():
        surf[0:CX] = elastic[pl.ds(0, CX, stride=NL)]

    @pl.when(section != 0)
    def _():
        surf[0:FINE] = average(lambda m: sheet[pl.ds(m, FINE, stride=REFINE)])


def source_pick(cols):
    return one(cols[0] == iota((cols.shape[1], CY), 1).astype(F32))


def outgoing(section, tiles, cols, pcat, packed, payload, sem):
    half = packed.shape[0]
    lanes = tiles.shape
    last = jnp.broadcast_to(tiles[:, CY - 1 : CY], lanes) * cols[1]
    first = jnp.broadcast_to(tiles[:, 0:1], lanes) * cols[1]
    packed[...] = pick(pcat[...], jnp.concatenate([tiles, last, first, cols[3]], axis=0))
    there = payload.at[pl.ds(pl.multiple_of((1 - section) * half, 8), half)]
    copy = pltpu.make_async_copy(packed, there, sem)
    copy.start()
    return copy


def link_tables(section, me, n_gy, dest, rows, weight, lines, cols, pcat):
    links = dest.shape[1]
    lines[...] = jnp.zeros_like(lines)
    lines[0:1, 0:links] = dest[...].astype(F32)
    lines[1:3, 0:links] = rows[...].astype(F32)
    lines[3:4, 0:links] = weight[...]
    x = lines[...]
    eye = one(iota((links, CY), 0) == iota((links, CY), 1))

    def column(i):
        return jnp.sum(eye * x[i : i + 1], axis=1, keepdims=True)

    target, source, landing, weights = [column(i) for i in range(4)]
    same = one(target == x[0:1])
    at = iota((links, CY), 0)
    other = iota((links, CY), 1)
    inside = one(other < links)
    slot_row = jnp.sum(same * one(at < other) * inside, axis=0, keepdims=True)
    slot = jnp.sum(same * one(other < at) * inside, axis=1, keepdims=True)
    lane = other.astype(F32)
    cols[0] = jnp.broadcast_to(source, (links, CY))
    cols[1] = one(landing == lane)
    cols[2] = jnp.broadcast_to(weights, (links, CY))
    cols[3] = landing * one(lane == slot + (me * SLOTS).astype(F32))
    y = jnp.concatenate([x[0:3], slot_row, jnp.zeros((4, CY), F32)], axis=0)
    y = y + pltpu.roll(y, links, 1) + pltpu.roll(y, 2 * links, 1) + pltpu.roll(y, 3 * links, 1)
    shape = (pcat.shape[0], CY)
    owner = iota(shape, 0) >> 3
    part = iota(shape, 0) & 7
    group = iota(shape, 1) >> (links.bit_length() - 1)
    to = y[0:1]
    row = y[2:3]
    order = y[3:4]
    beside = jnp.where(owner < n_gy, owner + n_gy, owner - n_gy).astype(F32)
    bottom = jnp.where(section == 0, FINE - 1, CX - 1).astype(F32)
    edge = jnp.where(owner < n_gy, 0.0, bottom)
    along = owner & (n_gy - 1)
    own = owner.astype(F32)
    chosen = one((group == 0) & (part == order.astype(jnp.int32)) & (part < CAP) & (to == own))
    chosen += one((group == 0) & (part == 4) & (to == beside) & (row == edge))
    chosen += one((group == 1) & (part == 6) & (to == own - 1.0) & (along > 0))
    chosen += one((group == 2) & (part == 7) & (to == own + 1.0) & (along < n_gy - 1))
    chosen += one((group == 3) & (part == 5) & (to == own))
    pcat[...] = chosen


def pack_sides(values_of, sides, channels):
    lane = iota((8, CY), 1)

    def half_of(h, carry):
        acc = {c: jnp.zeros((8, CY), F32) for c in channels}
        views = {c: values_of(c, pl.ds(pl.multiple_of(h * HALF * 8, 8), HALF * 8)) for c in channels}
        for b in range(HALF):
            for c in channels:
                value = views[c][8 * b : 8 * b + 8].astype(F32)
                acc[c] = jnp.where(lane >> 1 == b, pltpu.roll(value, 2 * b + 1, 1), acc[c])
        for c in channels:
            sides[c, h] = acc[c]
        return carry

    lax.fori_loop(0, 2, half_of, 0)


def unpack_sides(zs, halos, channels):
    def half_of(h, carry):
        for i, c in enumerate(channels):
            value = zs[c, h]
            view = halos.at[i, pl.ds(pl.multiple_of(h * HALF * 8, 8), HALF * 8)]
            for b in range(HALF):
                view[8 * b : 8 * b + 8] = pltpu.roll(value, CY - 1 - 2 * b, 1)
        return carry

    lax.fori_loop(0, 2, half_of, 0)


def take_edges(section, p, fields, wet, xs):
    start = pl.multiple_of(jnp.where(p == 0, ROWS - FIRST, 0), 8)
    for c in range(3):
        xs[c] = fields[c, pl.ds(start, FIRST)]

    @pl.when(section != 0)
    def _():
        xs[2] = wet[pl.ds(start, FIRST)].astype(F32)


def load_kernel(n_gy, state, previous, wet, dest, rows, weight, payload, cols, pcat, cur, prev, xs, sides, wet_in, dest_in, rows_in, weight_in, lines, surf, packed, sem):
    section, p, q = place()
    linked = 2 * (1 - section)
    pairs = [(dest, dest_in), (rows, rows_in), (weight, weight_in)]
    pairs += [(state.at[c], cur.at[c]) for c in (linked, 1, 2 - linked)]
    pairs += [(wet, wet_in), (previous, prev)]
    copies = [pltpu.make_async_copy(a, b, sem.at[i]) for i, (a, b) in enumerate(pairs)]
    for copy in copies[0:7]:
        copy.start()
    for copy in copies[0:3]:
        copy.wait()
    link_tables(section, p * n_gy + q, n_gy, dest_in, rows_in, weight_in, lines, cols, pcat)
    copies[3].wait()
    copies[7].start()
    surface(section, cur.at[2], cur.at[0], surf)
    tiles = cols[2] * pick(source_pick(cols), surf[...])
    copies.append(outgoing(section, tiles, cols, pcat, packed, payload, sem.at[8]))
    for copy in copies[4:7]:
        copy.wait()

    @pl.when(section == 0)
    def _():
        pack_sides(lambda c, at: cur.at[c, at], sides, (0, 1, 2))

    @pl.when(section != 0)
    def _():
        pack_sides(lambda c, at: wet_in.at[at] if c == 1 else cur.at[c, at], sides, (0, 1, 2))

    take_edges(section, p, cur, wet_in, xs)
    for copy in copies[7:]:
        copy.wait()


def group_rows(it, rows):
    return pl.ds(pl.multiple_of(it * GROUP, 8), rows)


def arrived_rows(section, received):
    half = received.shape[0] // 2
    return received[pl.ds(pl.multiple_of((1 - section) * half, 8), half)]


def arrived_sums(arrived):
    return jnp.sum(arrived.reshape(-1, SLOTS, CY), axis=0)


def landed(arrived, sums):
    mine = iota((CY, arrived.shape[0]), 1)
    return pick(one((iota(mine.shape, 0).astype(F32) == sums[5:6]) & ((mine & 7) < CAP)), arrived)


def route_kernel(received, base, scale, cols, pcat, payload, packed, sem):
    section, _, _ = place()
    arrived = arrived_rows(section, received)
    landing = arrived_sums(arrived)[5:6]
    lane = iota(cols.shape[1:], 1)
    gather = one((cols[0] == landing) & ((lane & 7) < CAP))
    tiles = base[...] + scale[...] * pick(gather, arrived)
    outgoing(section, tiles, cols, pcat, packed, payload, sem).wait()


def edge_addends(sums, period, offset):
    masks, values = [], []
    lane = iota((CY, 2 * CY), 1)
    block = ((lane & (CY - 1)) >> 1) + jnp.where(lane >= CY, HALF, 0)
    inside = (lane & (CY - 1)) < 2 * HALF
    for side, shift in ((0, 0), (1, offset)):
        at = iota(lane.shape, 0) * period + shift - block * 8
        masks.append(one((at >= 0) & (at < 8) & ((lane & 1) == side) & inside).astype(jnp.bfloat16))
        sub = (iota((16, CY), 1) * period + shift) & 7
        row = jnp.broadcast_to(sums[6 + side : 7 + side], (16, CY))
        values.append(jnp.where(sub == iota((16, CY), 0), row, 0.0))
    wide = spread(values[0], masks[0]) + spread(values[1], masks[1])
    return wide[0:8, 0:CY], wide[0:8, CY:]


def align_sides(zs, c, lane, sub):
    first, second = zs[c, 0], zs[c, 1]
    top = 2 * HALF
    low_first = jnp.where(lane == top - 2, pltpu.roll(second, top - 2, 1), pltpu.roll(first, CY - 2, 1))
    low_second = pltpu.roll(second, CY - 2, 1)
    high_first = pltpu.roll(first, 2, 1)
    high_second = jnp.where(lane == 1, pltpu.roll(first, CY + 2 - top, 1), pltpu.roll(second, 2, 1))
    for h, (low, high) in enumerate(((low_first, high_first), (low_second, high_second))):
        zs[c, h] = jnp.where(lane & 1 == 0, pltpu.roll(low, 7, 0), pltpu.roll(high, 1, 0))


def read_batch(fields, j):
    return [fields[c][8 * i : 8 * i + 8] for i in range(j, j + BATCH) for c in range(3)]


def write_batch(fields, j, values):
    for n, value in enumerate(values):
        i = j + 1 - BATCH + n // 3
        fields[n % 3][8 * i : 8 * i + 8] = value


def step_kernel(linked, last, *refs):
    cur_in, prev_in, coeff, wet, cols, xr, yra, yrb, mine, *refs = refs
    if linked:
        received, *refs = refs
    cur, prev, *refs = refs
    if last:
        out, wet_out, zs, full, halos, co, wet_in, sem = refs
    else:
        base, xs, sides, *refs = refs
        if not linked:
            scale, *refs = refs
        zs, full, halos, co, wet_in, sem, surf = refs
    section, p, q = place()
    lane = iota((8, CY), 1)
    sub = iota((8, CY), 0)
    even_lane = lane & 1 == 0
    groups = ROWS // GROUP
    wet_load = pltpu.make_async_copy(wet, wet_in, sem.at[groups])

    def load(it):
        at = group_rows(it, GROUP)
        return pltpu.make_async_copy(coeff.at[:, at], co.at[:, at], sem.at[it])

    @pl.when(section != 0)
    def _():
        wet_load.start()

    for it in range(groups):
        load(it).start()

    @pl.when((q & 1) == 1)
    def _():
        for c in range(3):
            for h in range(2):
                zs[c, h] = jnp.where(even_lane, yra[c, h], yrb[c, h])

    @pl.when((q & 1) == 0)
    def _():
        for c in range(3):
            for h in range(2):
                zs[c, h] = jnp.where(even_lane, yrb[c, h], yra[c, h])

    there = pl.multiple_of(jnp.where(p == 0, FIRST + ROWS, 0), 8)
    nowhere = pl.multiple_of(jnp.where(p == 0, 0, FIRST + ROWS), 8)
    for c in range(3):
        full[c, pl.ds(there, FIRST)] = xr[c]
        full[c, pl.ds(nowhere, FIRST)] = jnp.zeros((FIRST, CY), F32)

    if linked:
        arrived = arrived_rows(section, received)
        sums = arrived_sums(arrived)
        addend = landed(arrived, sums)
    def widen(it, carry):
        for c in range(3):
            view = full.at[c, group_rows(it, FIRST + GROUP)]
            view[FIRST : FIRST + GROUP] = cur[c, group_rows(it, GROUP)]
        return carry

    if last:

        @pl.when(section == 0)
        def _():
            wet_out[...] = jnp.zeros_like(wet_out)

    def views_of(it, ref):
        return [ref.at[c, group_rows(it, GROUP)] for c in range(ref.shape[0])]

    def padded_of(it):
        return [full.at[c, group_rows(it, GROUP + 2 * FIRST)] for c in range(3)]

    @pl.when(section == 0)
    def _():
        if linked:
            for x in range(CX):
                cur[2, NL * x : NL * x + 1] += addend[x : x + 1]

            @pl.when(p == 0)
            def _():
                full[2, FIRST + ROWS : FIRST + ROWS + 1] += sums[4:5]

            @pl.when(p != 0)
            def _():
                full[2, FIRST - NL : FIRST - NL + 1] += sums[4:5]

            for h, value in enumerate(edge_addends(sums, NL, 0)):
                zs[2, h] += value

        lax.fori_loop(0, groups, widen, 0)
        unpack_sides(zs, halos, (0, 1, 2))

        def group(it, carry):
            load(it).wait()
            sides_of = views_of(it, halos)
            depth = it * GROUP - NL * ((it * GROUP * 656) >> 16) + sub
            fields, old, new_fields, factors = padded_of(it), views_of(it, prev_in), views_of(it, prev), views_of(it, co)
            for j in range(BLOCKS):
                if j % BATCH == 0:
                    olds, news = read_batch(old, j), []
                at = slice(8 * j, 8 * j + 8)
                mu = factors[0][at]
                stiff = factors[1][at] + 2.0 * mu
                layer = depth + 8 * j
                shallowest = (layer == 0) | (layer == NL) | (layer == 2 * NL)
                deepest = (layer == NL - 1) | (layer == 2 * NL - 1)
                for c in range(3):

                    def near(rows):
                        return fields[c][FIRST + 8 * j + rows : FIRST + 8 * j + rows + 8]

                    v = near(0)
                    twice = 2.0 * v
                    above = jnp.where(shallowest, 0.0, near(-1))
                    below = jnp.where(deepest, 0.0, near(1))
                    halo = sides_of[c][at]
                    low = jnp.where(lane == CY - 1, halo, v)
                    high = jnp.where(lane == 0, halo, v)
                    along_first = near(-NL) + near(NL) - twice
                    along_depth = above + below - twice
                    along_second = pltpu.roll(low, 1, 1) + pltpu.roll(high, CY - 1, 1) - twice
                    if c == 0:
                        force = stiff * along_first + mu * (along_depth + along_second)
                    elif c == 1:
                        force = stiff * along_second + mu * (along_first + along_depth)
                    else:
                        force = stiff * along_depth + mu * (along_first + along_second)
                    news.append(twice - olds.pop(0) + force)
                if j % BATCH == BATCH - 1:
                    write_batch(new_fields, j, news)
            return carry

        lax.fori_loop(0, groups, group, 0)
        if not last:
            pack_sides(lambda c, at: prev.at[c, at], sides, (0, 1, 2))

    @pl.when(section != 0)
    def _():
        for c in range(3):
            align_sides(zs, c, lane, sub)
        if linked:
            for h, value in enumerate(edge_addends(sums, REFINE, REFINE - 1)):
                zs[0, h] += zs[1, h] * value
            beside = jnp.broadcast_to(sums[4:5], (8, CY))
            fine_row = jnp.concatenate(
                [
                    jnp.take_along_axis(beside, (((sub + m) * CY + lane) * 6554) >> 16, axis=1)
                    for m in (0, 2)
                ],
                axis=0,
            )

            def add_edge(first):
                for start, rows in ((0, fine_row[0:8]), (8, fine_row[14:16])):
                    at = slice(first + start, first + start + rows.shape[0])
                    full[0, at] += full[2, at] * rows

            @pl.when(p == 0)
            def _():
                add_edge(FIRST + ROWS)

            @pl.when(p != 0)
            def _():
                add_edge(FIRST - REFINE)

        unpack_sides(zs, halos, (0, 2))
        lax.fori_loop(0, groups, widen, 0)
        wet_load.wait()
        if linked:
            for start, fine in fine_addend(addend):
                at = pl.ds(start, 8, stride=REFINE)
                value = cur[0, at] + wet_in[at].astype(F32) * fine
                cur[0, at] = value
                full[0, pl.ds(FIRST + start, 8, stride=REFINE)] = value
        if last:
            wet_out[...] = wet_in[...]

        def group(it, carry):
            load(it).wait()
            sides_of = views_of(it, halos)
            fields, old, new_fields, factors = padded_of(it), views_of(it, prev_in), views_of(it, prev), views_of(it, co)
            wets = wet_in.at[group_rows(it, GROUP)]
            for j in range(BLOCKS):
                if j % BATCH == 0:
                    olds, news = read_batch(old, j), []
                at = slice(8 * j, 8 * j + 8)
                a = factors[0][at]
                b = factors[1][at]
                w = wets[at].astype(F32)

                def near(c, rows):
                    return fields[c][FIRST + 8 * j + rows : FIRST + 8 * j + rows + 8]

                def across(c):
                    v = near(c, 0)
                    low = jnp.where(lane == CY - 1, near(c, -1), v)
                    high = jnp.where(lane == 0, near(c, 1), v)
                    halo = sides_of[c // 2][at]
                    for s in range(8):
                        if (8 * j + s) % REFINE == 0:
                            low = jnp.where((lane == CY - 1) & (sub == s), halo, low)
                        if (8 * j + s) % REFINE == REFINE - 1:
                            high = jnp.where((lane == 0) & (sub == s), halo, high)
                    return pltpu.roll(high, CY - 1, 1) - pltpu.roll(low, 1, 1)

                def down(c):
                    return near(c, REFINE) - near(c, -REFINE)

                news.append(w * (olds.pop(0) - b * (down(1) + across(2))))
                news.append(w * (olds.pop(0) - a * down(0)))
                news.append(w * (olds.pop(0) - a * across(0)))
                if j % BATCH == BATCH - 1:
                    write_batch(new_fields, j, news)
            return carry

        lax.fori_loop(0, groups, group, 0)
        if not last:
            pack_sides(lambda c, at: prev.at[c, at], sides, (0, 2))
            sides[1] = mine[1]

    if last:
        copy = pltpu.make_async_copy(prev, out, sem.at[0])
        copy.start()
        copy.wait()
    else:
        take_edges(section, p, prev, wet_in, xs)
        surface(section, prev.at[2], prev.at[0], surf)
        base[...] = cols[2] * pick(source_pick(cols), surf[...])
    if not linked:
        scale[...] = cols[2]

        @pl.when(section != 0)
        def _():
            surf[0:FINE] = average(lambda m: wet_in[pl.ds(m, FINE, stride=REFINE)].astype(F32))
            scale[...] = cols[2] * pick(source_pick(cols), surf[...])


def fine_addend(addend):
    lane = iota((8, CY), 1)
    for m in range(FINE // 8):
        rows = addend[8 * m : 8 * m + 8]
        for k in range(REFINE):
            fine = jnp.take_along_axis(rows, ((lane + k * CY) * 6554) >> 16, axis=1)
            yield 8 * REFINE * m + k, fine


def last_kernel(final_in, fields, wet, received, final, height, sem):
    section, _, _ = place()
    arrived = arrived_rows(section, received)
    addend = landed(arrived, arrived_sums(arrived))

    @pl.when(section == 0)
    def _():
        copies = []
        for x in range(CX):
            row = NL * x
            first = row // 8 * 8
            height[8 * x : 8 * x + 8] = fields[2, first : first + 8]
            at = 8 * x + row - first
            height[at : at + 1] += addend[x : x + 1]
            copies.append(
                pltpu.make_async_copy(
                    height.at[8 * x : 8 * x + 8], final.at[2, pl.ds(first, 8)], sem.at[x]
                )
            )
        for copy in copies:
            copy.start()
        for copy in copies:
            copy.wait()

    @pl.when(section != 0)
    def _():
        part = 8 * REFINE
        copies = []
        for start, fine in fine_addend(addend):
            at = pl.ds(start, 8, stride=REFINE)
            height[at] = fields[0, at] + wet[at].astype(F32) * fine
            if start % part == REFINE - 1:
                rows = pl.ds(start // part * part, part)
                copies.append(pltpu.make_async_copy(height.at[rows], final.at[0, rows], sem.at[len(copies)]))
                copies[-1].start()
        for copy in copies:
            copy.wait()


def call(kernel, operands, outs, scratch=(), aliases=None, any_inputs=(), any_outs=(), limit=12, cost=4):
    vmem = pl.BlockSpec(memory_space=pltpu.VMEM)
    anywhere = pl.BlockSpec(memory_space=pl.ANY)
    return pl.pallas_call(
        kernel,
        out_shape=[
            (pltpu.VMEM if kept else jax.ShapeDtypeStruct)(shape, kind[0] if kind else F32)
            for shape, kept, *kind in outs
        ],
        in_specs=[anywhere if i in any_inputs else vmem for i in range(len(operands))],
        out_specs=[anywhere if i in any_outs else vmem for i in range(len(outs))],
        scratch_shapes=list(scratch),
        input_output_aliases=aliases or {},
        compiler_params=pltpu.CompilerParams(vmem_limit_bytes=limit * 1024 * 1024),
        cost_estimate=pl.CostEstimate(flops=cost * 10**9, bytes_accessed=cost * 1024 * 1024, transcendentals=0),
    )(*operands)


def keep(value):
    return pltpu.with_memory_space_constraint(value, pltpu.VMEM)


def outside(value):
    return pltpu.with_memory_space_constraint(value, pltpu.HBM)


def on_device(n_gy, owners, state, previous, coeff, wet_mask, link_dest, link_rows, link_weight):
    links = link_weight.size
    pairs = 2 * owners * SLOTS
    vmem = pltpu.VMEM
    dma = pltpu.SemaphoreType.DMA
    field_shape = (3, ROWS, CY)
    sides_shape = (3, 2, 8, CY)
    fields = (field_shape, True)
    edges = ((3, FIRST, CY), False)
    sides_out = (sides_shape, False)
    tiles = ((links, CY), True)
    surf = vmem((CY, CY), F32)
    wet_in = vmem((ROWS, CY), jnp.int32)
    state, previous = state.reshape(field_shape), previous.reshape(field_shape)
    coeff, wet = outside(coeff.reshape(2, ROWS, CY)), outside(wet_mask.reshape(ROWS, CY))

    def exchange(payload):
        payload = payload.reshape(2 * owners, SLOTS, CY)
        payload = lax.all_to_all(payload, ("sec", "gx", "gy"), 0, 0, tiled=True)
        return payload.reshape(pairs, CY)

    dest, rows, weight = link_dest.reshape(1, links), link_rows.reshape(links, 2).T, link_weight.reshape(1, links)
    payload, cols, pcat, cur, prev, xs, sides = call(
        functools.partial(load_kernel, n_gy),
        [outside(x) for x in (state, previous, wet, dest, rows, weight)],
        [
            ((pairs, CY), False), ((4, links, CY), True), ((owners * SLOTS, CY), True), fields, fields,
            edges, sides_out,
        ],
        [
            wet_in, vmem((1, links), jnp.int32), vmem((2, links), jnp.int32),
            vmem((1, links), F32), vmem((8, CY), F32), surf, vmem((owners * SLOTS, CY), F32), dma((9,)),
        ],
        any_inputs=range(6), any_outs=(0,),
    )
    received = exchange(payload)
    swap = [(0, 1), (1, 0)]
    inner = [(i, i ^ 1) for i in range(n_gy)]
    outer = [(i, j) for k in range(1, n_gy - 1, 2) for i, j in ((k, k + 1), (k + 1, k))]
    before = None
    for step in range(STEPS):
        last = step == STEPS - 1
        xr = lax.ppermute(xs, "gx", swap)
        yra = lax.ppermute(sides, "gy", inner)
        yrb = lax.ppermute(sides, "gy", outer)
        operands = [keep(cur), keep(prev), coeff, wet, keep(cols), xr, yra, yrb, sides]
        if before is not None:
            operands.append(before)
        kernel = functools.partial(step_kernel, before is not None, last)
        scratch = [
            vmem(sides_shape, F32), vmem((3, TOTAL, CY), F32), vmem(field_shape, F32), vmem((2, ROWS, CY), F32),
            wet_in, dma((ROWS // GROUP + 1,)),
        ]
        more = dict(aliases={0: 0, 1: 1}, any_inputs=(2, 3), cost=64)
        if last:
            _, new, final, wet_kept = call(
                kernel, operands, [fields, fields, (field_shape, False), ((ROWS, CY), True, jnp.int32)], scratch,
                any_outs=(2,), **more
            )
        else:
            outs = [fields, fields, tiles, edges, sides_out] + [tiles] * (before is None)
            prev, cur, base, xs, sides, *first = call(kernel, operands, outs, scratch + [surf], **more)
            if first:
                scale = first[0]
            payload = call(
                route_kernel, (received, keep(base), keep(scale), keep(cols), keep(pcat)),
                [((pairs, CY), False)], [vmem((owners * SLOTS, CY), F32), dma], any_outs=(0,), limit=4,
            )[0]
            before = received
            received = exchange(payload)
    final = call(
        last_kernel,
        (outside(final), keep(new), keep(wet_kept), received),
        [(field_shape, False)],
        [vmem((ROWS, CY), F32), dma((FINE // 8,))],
        aliases={0: 0}, any_inputs=(0,), any_outs=(0,),
    )[0]
    return final.reshape(1, 3, 1, 1, -1)


def from_partner(value, axis, stride):
    return lax.ppermute(value, axis, [(i, i ^ 1 << stride) for i in range(lax.axis_size(axis))])


def with_halo(block, sides, width):
    for axis, dim in sides:
        count = lax.axis_size(axis)
        forward = [(i, i + 1) for i in range(count - 1)]
        backward = [(target, source) for source, target in forward]
        low = lax.ppermute(
            lax.slice_in_dim(block, block.shape[dim] - width, None, axis=dim), axis, forward
        )
        high = lax.ppermute(lax.slice_in_dim(block, 0, width, axis=dim), axis, backward)
        block = jnp.concatenate([low, block, high], axis=dim)
    return block


def elastic_update(padded, current, previous_field, shear_modulus, lame_first, surface_force):
    own_axis = (0, 2, 1)
    stiffness = lame_first + 2.0 * shear_modulus
    updated_list = []
    for component in range(3):
        displaced = current[component]
        extended = padded[component]
        along_first = extended[2:, :, 1:-1] - 2.0 * displaced + extended[:-2, :, 1:-1]
        deeper = jnp.pad(displaced, ((0, 0), (1, 1), (0, 0)))
        along_depth = deeper[:, 2:, :] - 2.0 * displaced + deeper[:, :-2, :]
        along_second = extended[1:-1, :, 2:] - 2.0 * displaced + extended[1:-1, :, :-2]
        factors = [
            stiffness if own_axis[component] == axis_index else shear_modulus
            for axis_index in range(3)
        ]
        acceleration = (
            factors[0] * along_first + factors[1] * along_depth + factors[2] * along_second
        )
        updated = 2.0 * displaced - previous_field[component] + acceleration
        if component == 2:
            updated = updated.at[:, 0, :].add(surface_force)
        updated_list.append(updated)
    return jnp.stack(updated_list)


def shallow_update(padded, current, previous_field, wave_factor, area_factor, wetness, source):
    fine_rows = REFINE * CX
    fine_cols = REFINE * CY
    sheet = current.reshape(3, fine_rows, fine_cols)
    earlier_sheet = previous_field.reshape(3, fine_rows, fine_cols)
    above = padded[:, 0, (REFINE - 1) * REFINE :, 1:-1].reshape(3, 1, fine_cols)
    below = padded[:, -1, :REFINE, 1:-1].reshape(3, 1, fine_cols)
    left_side = padded[:, 1:-1, REFINE - 1 :: REFINE, 0].reshape(3, fine_rows, 1)
    right_side = padded[:, 1:-1, 0::REFINE, -1].reshape(3, fine_rows, 1)
    by_rows = jnp.concatenate([above, sheet, below], axis=1)
    by_columns = jnp.concatenate([left_side, sheet, right_side], axis=2)

    def rows_diff(channel):
        return by_rows[channel, 2:, :] - by_rows[channel, :-2, :]

    def columns_diff(channel):
        return by_columns[channel, :, 2:] - by_columns[channel, :, :-2]

    flux_first = wetness * (earlier_sheet[1] - wave_factor * rows_diff(0))
    flux_second = wetness * (earlier_sheet[2] - wave_factor * columns_diff(0))
    height = wetness * (earlier_sheet[0] - area_factor * (rows_diff(1) + columns_diff(2)) + source)
    return jnp.stack([height, flux_first, flux_second]).reshape(3, CX, NL, CY)


def route(payload):
    tile_data, tile_rows = payload
    width = tile_data.shape[-1]
    received_data, received_rows = (
        lax.all_to_all(tile_data, ("gx", "gy"), split_axis=0, concat_axis=0, tiled=True),
        lax.all_to_all(tile_rows, ("gx", "gy"), split_axis=0, concat_axis=0, tiled=True),
    )
    return (received_data.reshape(-1, width), received_rows.reshape(-1))


def deliver(outgoing, send_rows):
    crossed = from_partner((outgoing, send_rows), "sec", 0)
    return route(crossed)


def general_on_device(state, previous, coeff, wet_mask, link_dest, link_rows, link_weight):
    section = lax.axis_index("sec")
    owners = lax.axis_size("gx") * lax.axis_size("gy")
    fine_rows = REFINE * CX
    fine_cols = REFINE * CY
    current = state[0, :, 0, 0].reshape(3, CX, NL, CY)
    earlier = previous[0, :, 0, 0].reshape(3, CX, NL, CY)
    first_factor = coeff[0, 0, 0, 0]
    second_factor = coeff[0, 1, 0, 0]
    wetness = wet_mask[0, 0].reshape(fine_rows, fine_cols).astype(jnp.float32)
    targets = link_dest.reshape(-1)
    pairs = link_rows.reshape(-1, 2)
    source_rows = pairs[:, 0]
    landing = pairs[:, 1]
    weights = link_weight.reshape(-1)
    one_hot = (targets[:, None] == jnp.arange(owners, dtype=jnp.int32)[None, :]).astype(jnp.int32)
    before = jnp.cumsum(one_hot, axis=0) - one_hot
    slot_index = jnp.sum(before * one_hot, axis=1)
    position = targets * CAP + slot_index
    send_rows = jnp.zeros((owners * CAP,), jnp.int32).at[position].set(landing).reshape(owners, CAP)
    for step_index in range(STEPS):
        padded = with_halo(current, (("gx", 1), ("gy", 3)), 1)

        def elastic_rows():
            return current[2, :, 0, :][source_rows]

        def shallow_rows():
            picked_fine = current[0].reshape(fine_rows, fine_cols)[source_rows]
            return jnp.sum(picked_fine.reshape(-1, CY, REFINE), axis=-1) / REFINE

        picked = lax.cond(section == 0, elastic_rows, shallow_rows)
        outgoing = (
            jnp.zeros((owners * CAP, CY), jnp.float32).at[position].set(picked * weights[:, None])
        )
        outgoing = outgoing.reshape(owners, CAP, CY)
        arrived, arrived_rows = deliver(outgoing, send_rows)

        def elastic_branch():
            surface_force = jnp.zeros((CX, CY), jnp.float32).at[arrived_rows].add(arrived)
            return elastic_update(
                padded,
                current,
                earlier,
                first_factor.reshape(CX, NL, CY),
                second_factor.reshape(CX, NL, CY),
                surface_force,
            )

        def shallow_branch():
            coarse_source = jnp.zeros((fine_rows, CY), jnp.float32).at[arrived_rows].add(arrived)
            source = jnp.repeat(coarse_source, REFINE, axis=1)
            return shallow_update(
                padded,
                current,
                earlier,
                first_factor.reshape(fine_rows, fine_cols),
                second_factor.reshape(fine_rows, fine_cols),
                wetness,
                source,
            )

        updated = lax.cond(section == 0, elastic_branch, shallow_branch)
        earlier, current = (current, updated)
    return current.reshape(1, 3, 1, 1, -1)


def solution(mesh):
    placed = (
        P("sec", None, "gx", "gy", None),
        P("sec", None, "gx", "gy", None),
        P("sec", None, "gx", "gy", None),
        P("gx", "gy", None),
        P("sec", "gx", "gy", None, None),
        P("sec", "gx", "gy", None, None),
        P("sec", "gx", "gy", None),
    )
    n_gx, n_gy = mesh.shape["gx"], mesh.shape["gy"]
    owners = n_gx * n_gy
    device_program = general_on_device
    if n_gx == 2 and n_gy & (n_gy - 1) == 0 and owners * SLOTS == CY:
        device_program = functools.partial(on_device, n_gy, owners)
    return jax.shard_map(
        device_program,
        mesh=mesh,
        in_specs=placed,
        out_specs=P("sec", None, "gx", "gy", None),
        check_vma=False,
    )
```

```python
import functools

import jax
import jax.numpy as jnp
from jax import lax
from jax.experimental import pallas as pl
from jax.experimental.pallas import tpu as pltpu
from jax.sharding import PartitionSpec as P

CX = 8
CY = 128
REFINE = 10
NL = 100
STEPS = 4
CAP = 4
FINE = REFINE * CX
ROWS = CX * NL
FIRST = 104
TOTAL = FIRST + ROWS + FIRST
SLOTS = 8
BLOCKS = 20
BATCH = 4
GROUP = 8 * BLOCKS
HALF = ROWS // 16
F32 = jnp.float32


def split(x):
    high = x.astype(jnp.bfloat16)
    return high, (x - high.astype(F32)).astype(jnp.bfloat16)


def pick(mask, x):
    parts = jnp.concatenate(split(x), axis=1)
    wide = jnp.dot(mask.astype(jnp.bfloat16), parts, preferred_element_type=F32)
    return wide[:, 0 : x.shape[1]] + wide[:, x.shape[1] :]


def spread(x, mask):
    tall = jnp.dot(jnp.concatenate(split(x), axis=0), mask, preferred_element_type=F32)
    return tall[0 : x.shape[0]] + tall[x.shape[0] :]


def iota(shape, dim):
    return lax.broadcasted_iota(jnp.int32, shape, dim)


def one(mask):
    return jnp.where(mask, 1.0, 0.0).astype(F32)


def place():
    return lax.axis_index("sec"), lax.axis_index("gx"), lax.axis_index("gy")


def average(rows_of):
    total = jnp.zeros((FINE, CY), F32)
    for m in range(REFINE):
        fine = iota((CY, CY), 0) + m * CY
        first = iota((CY, CY), 1) * REFINE
        mask = one((fine >= first) & (fine < first + REFINE)).astype(jnp.bfloat16)
        total = total + spread(rows_of(m), mask)
    return total / REFINE


def surface(section, elastic, sheet, surf):
    surf[...] = jnp.zeros_like(surf)

    @pl.when(section == 0)
    def _():
        surf[0:CX] = elastic[pl.ds(0, CX, stride=NL)]

    @pl.when(section != 0)
    def _():
        surf[0:FINE] = average(lambda m: sheet[pl.ds(m, FINE, stride=REFINE)])


def source_pick(cols):
    return one(cols[0] == iota((cols.shape[1], CY), 1).astype(F32))


def outgoing(section, tiles, cols, pcat, packed, payload, sem):
    half = packed.shape[0]
    lanes = tiles.shape
    last = jnp.broadcast_to(tiles[:, CY - 1 : CY], lanes) * cols[1]
    first = jnp.broadcast_to(tiles[:, 0:1], lanes) * cols[1]
    packed[...] = pick(pcat[...], jnp.concatenate([tiles, last, first, cols[3]], axis=0))
    there = payload.at[pl.ds(pl.multiple_of((1 - section) * half, 8), half)]
    copy = pltpu.make_async_copy(packed, there, sem)
    copy.start()
    return copy


def link_tables(section, me, n_gy, dest, rows, weight, lines, cols, pcat):
    links = dest.shape[1]
    lines[...] = jnp.zeros_like(lines)
    lines[0:1, 0:links] = dest[...].astype(F32)
    lines[1:3, 0:links] = rows[...].astype(F32)
    lines[3:4, 0:links] = weight[...]
    x = lines[...]
    eye = one(iota((links, CY), 0) == iota((links, CY), 1))

    def column(i):
        return jnp.sum(eye * x[i : i + 1], axis=1, keepdims=True)

    target, source, landing, weights = [column(i) for i in range(4)]
    same = one(target == x[0:1])
    at = iota((links, CY), 0)
    other = iota((links, CY), 1)
    inside = one(other < links)
    slot_row = jnp.sum(same * one(at < other) * inside, axis=0, keepdims=True)
    slot = jnp.sum(same * one(other < at) * inside, axis=1, keepdims=True)
    lane = other.astype(F32)
    cols[0] = jnp.broadcast_to(source, (links, CY))
    cols[1] = one(landing == lane)
    cols[2] = jnp.broadcast_to(weights, (links, CY))
    cols[3] = landing * one(lane == slot + (me * SLOTS).astype(F32))
    y = jnp.concatenate([x[0:3], slot_row, jnp.zeros((4, CY), F32)], axis=0)
    y = y + pltpu.roll(y, links, 1) + pltpu.roll(y, 2 * links, 1) + pltpu.roll(y, 3 * links, 1)
    shape = (pcat.shape[0], CY)
    owner = iota(shape, 0) >> 3
    part = iota(shape, 0) & 7
    group = iota(shape, 1) >> (links.bit_length() - 1)
    to = y[0:1]
    row = y[2:3]
    order = y[3:4]
    beside = jnp.where(owner < n_gy, owner + n_gy, owner - n_gy).astype(F32)
    bottom = jnp.where(section == 0, FINE - 1, CX - 1).astype(F32)
    edge = jnp.where(owner < n_gy, 0.0, bottom)
    along = owner & (n_gy - 1)
    own = owner.astype(F32)
    chosen = one((group == 0) & (part == order.astype(jnp.int32)) & (part < CAP) & (to == own))
    chosen += one((group == 0) & (part == 4) & (to == beside) & (row == edge))
    chosen += one((group == 1) & (part == 6) & (to == own - 1.0) & (along > 0))
    chosen += one((group == 2) & (part == 7) & (to == own + 1.0) & (along < n_gy - 1))
    chosen += one((group == 3) & (part == 5) & (to == own))
    pcat[...] = chosen


def pack_sides(values_of, sides, channels):
    lane = iota((8, CY), 1)

    def half_of(h, carry):
        acc = {c: jnp.zeros((8, CY), F32) for c in channels}
        views = {c: values_of(c, pl.ds(pl.multiple_of(h * HALF * 8, 8), HALF * 8)) for c in channels}
        for b in range(HALF):
            for c in channels:
                value = views[c][8 * b : 8 * b + 8].astype(F32)
                acc[c] = jnp.where(lane >> 1 == b, pltpu.roll(value, 2 * b + 1, 1), acc[c])
        for c in channels:
            sides[c, h] = acc[c]
        return carry

    lax.fori_loop(0, 2, half_of, 0)


def unpack_sides(zs, halos, channels):
    def half_of(h, carry):
        for i, c in enumerate(channels):
            value = zs[c, h]
            view = halos.at[i, pl.ds(pl.multiple_of(h * HALF * 8, 8), HALF * 8)]
            for b in range(HALF):
                view[8 * b : 8 * b + 8] = pltpu.roll(value, CY - 1 - 2 * b, 1)
        return carry

    lax.fori_loop(0, 2, half_of, 0)


def take_edges(section, p, fields, wet, xs):
    start = pl.multiple_of(jnp.where(p == 0, ROWS - FIRST, 0), 8)
    for c in range(3):
        xs[c] = fields[c, pl.ds(start, FIRST)]

    @pl.when(section != 0)
    def _():
        xs[2] = wet[pl.ds(start, FIRST)].astype(F32)


def load_kernel(n_gy, state, previous, wet, dest, rows, weight, payload, cols, pcat, cur, prev, xs, sides, wet_in, dest_in, rows_in, weight_in, lines, surf, packed, sem):
    section, p, q = place()
    linked = 2 * (1 - section)
    pairs = [(dest, dest_in), (rows, rows_in), (weight, weight_in)]
    pairs += [(state.at[c], cur.at[c]) for c in (linked, 1, 2 - linked)]
    pairs += [(wet, wet_in), (previous, prev)]
    copies = [pltpu.make_async_copy(a, b, sem.at[i]) for i, (a, b) in enumerate(pairs)]
    for copy in copies[0:7]:
        copy.start()
    for copy in copies[0:3]:
        copy.wait()
    link_tables(section, p * n_gy + q, n_gy, dest_in, rows_in, weight_in, lines, cols, pcat)
    copies[3].wait()
    copies[7].start()
    surface(section, cur.at[2], cur.at[0], surf)
    tiles = cols[2] * pick(source_pick(cols), surf[...])
    copies.append(outgoing(section, tiles, cols, pcat, packed, payload, sem.at[8]))
    for copy in copies[4:7]:
        copy.wait()

    @pl.when(section == 0)
    def _():
        pack_sides(lambda c, at: cur.at[c, at], sides, (0, 1, 2))

    @pl.when(section != 0)
    def _():
        pack_sides(lambda c, at: wet_in.at[at] if c == 1 else cur.at[c, at], sides, (0, 1, 2))

    take_edges(section, p, cur, wet_in, xs)
    for copy in copies[7:]:
        copy.wait()


def group_rows(it, rows):
    return pl.ds(pl.multiple_of(it * GROUP, 8), rows)


def arrived_rows(section, received):
    half = received.shape[0] // 2
    return received[pl.ds(pl.multiple_of((1 - section) * half, 8), half)]


def arrived_sums(arrived):
    return jnp.sum(arrived.reshape(-1, SLOTS, CY), axis=0)


def landed(arrived, sums):
    mine = iota((CY, arrived.shape[0]), 1)
    return pick(one((iota(mine.shape, 0).astype(F32) == sums[5:6]) & ((mine & 7) < CAP)), arrived)


def route_kernel(received, base, scale, cols, pcat, payload, packed, sem):
    section, _, _ = place()
    arrived = arrived_rows(section, received)
    landing = arrived_sums(arrived)[5:6]
    lane = iota(cols.shape[1:], 1)
    gather = one((cols[0] == landing) & ((lane & 7) < CAP))
    tiles = base[...] + scale[...] * pick(gather, arrived)
    outgoing(section, tiles, cols, pcat, packed, payload, sem).wait()


def edge_addends(sums, period, offset):
    masks, values = [], []
    lane = iota((CY, 2 * CY), 1)
    block = ((lane & (CY - 1)) >> 1) + jnp.where(lane >= CY, HALF, 0)
    inside = (lane & (CY - 1)) < 2 * HALF
    for side, shift in ((0, 0), (1, offset)):
        at = iota(lane.shape, 0) * period + shift - block * 8
        masks.append(one((at >= 0) & (at < 8) & ((lane & 1) == side) & inside).astype(jnp.bfloat16))
        sub = (iota((16, CY), 1) * period + shift) & 7
        row = jnp.broadcast_to(sums[6 + side : 7 + side], (16, CY))
        values.append(jnp.where(sub == iota((16, CY), 0), row, 0.0))
    wide = spread(values[0], masks[0]) + spread(values[1], masks[1])
    return wide[0:8, 0:CY], wide[0:8, CY:]


def align_sides(zs, c, lane, sub):
    first, second = zs[c, 0], zs[c, 1]
    top = 2 * HALF
    low_first = jnp.where(lane == top - 2, pltpu.roll(second, top - 2, 1), pltpu.roll(first, CY - 2, 1))
    low_second = pltpu.roll(second, CY - 2, 1)
    high_first = pltpu.roll(first, 2, 1)
    high_second = jnp.where(lane == 1, pltpu.roll(first, CY + 2 - top, 1), pltpu.roll(second, 2, 1))
    for h, (low, high) in enumerate(((low_first, high_first), (low_second, high_second))):
        zs[c, h] = jnp.where(lane & 1 == 0, pltpu.roll(low, 7, 0), pltpu.roll(high, 1, 0))


def read_batch(fields, j):
    return [fields[c][8 * i : 8 * i + 8] for i in range(j, j + BATCH) for c in range(3)]


def write_batch(fields, j, values):
    for n, value in enumerate(values):
        i = j + 1 - BATCH + n // 3
        fields[n % 3][8 * i : 8 * i + 8] = value


def step_kernel(n_gy, linked, last, *refs):
    cur_in, prev_in, coeff, wet, cols, xr, yra, yrb, mine, *refs = refs
    if linked:
        received, *refs = refs
    cur, prev, *refs = refs
    if last:
        out, wet_out, zs, full, halos, co, wet_in, sem = refs
    else:
        base, xs, sides, *refs = refs
        if not linked:
            scale, *refs = refs
        zs, full, halos, co, wet_in, sem, surf = refs
    section, p, q = place()
    lane = iota((8, CY), 1)
    sub = iota((8, CY), 0)
    even_lane = lane & 1 == 0
    groups = ROWS // GROUP
    wet_load = pltpu.make_async_copy(wet, wet_in, sem.at[groups])

    def load(it):
        at = group_rows(it, GROUP)
        return pltpu.make_async_copy(coeff.at[:, at], co.at[:, at], sem.at[it])

    @pl.when(section != 0)
    def _():
        wet_load.start()

    for it in range(groups):
        load(it).start()

    within = (q > 0) & (q < n_gy - 1)

    @pl.when((q & 1) == 1)
    def _():
        for c in range(3):
            for h in range(2):
                zs[c, h] = jnp.where(even_lane, yra[c, h], jnp.where(within, yrb[c, h], 0.0))

    @pl.when((q & 1) == 0)
    def _():
        for c in range(3):
            for h in range(2):
                zs[c, h] = jnp.where(even_lane, jnp.where(within, yrb[c, h], 0.0), yra[c, h])

    there = pl.multiple_of(jnp.where(p == 0, FIRST + ROWS, 0), 8)
    nowhere = pl.multiple_of(jnp.where(p == 0, 0, FIRST + ROWS), 8)
    for c in range(3):
        full[c, pl.ds(there, FIRST)] = xr[c]
        full[c, pl.ds(nowhere, FIRST)] = jnp.zeros((FIRST, CY), F32)

    if linked:
        arrived = arrived_rows(section, received)
        sums = arrived_sums(arrived)
        addend = landed(arrived, sums)
    def widen(it, carry):
        for c in range(3):
            view = full.at[c, group_rows(it, FIRST + GROUP)]
            view[FIRST : FIRST + GROUP] = cur[c, group_rows(it, GROUP)]
        return carry

    if last:

        @pl.when(section == 0)
        def _():
            wet_out[...] = jnp.zeros_like(wet_out)

    def views_of(it, ref):
        return [ref.at[c, group_rows(it, GROUP)] for c in range(ref.shape[0])]

    def padded_of(it):
        return [full.at[c, group_rows(it, GROUP + 2 * FIRST)] for c in range(3)]

    @pl.when(section == 0)
    def _():
        if linked:
            for x in range(CX):
                cur[2, NL * x : NL * x + 1] += addend[x : x + 1]

            @pl.when(p == 0)
            def _():
                full[2, FIRST + ROWS : FIRST + ROWS + 1] += sums[4:5]

            @pl.when(p != 0)
            def _():
                full[2, FIRST - NL : FIRST - NL + 1] += sums[4:5]

            for h, value in enumerate(edge_addends(sums, NL, 0)):
                zs[2, h] += value

        lax.fori_loop(0, groups, widen, 0)
        unpack_sides(zs, halos, (0, 1, 2))

        def group(it, carry):
            load(it).wait()
            sides_of = views_of(it, halos)
            depth = it * GROUP - NL * ((it * GROUP * 656) >> 16) + sub
            fields, old, new_fields, factors = padded_of(it), views_of(it, prev_in), views_of(it, prev), views_of(it, co)
            for j in range(BLOCKS):
                if j % BATCH == 0:
                    olds, news = read_batch(old, j), []
                at = slice(8 * j, 8 * j + 8)
                mu = factors[0][at]
                stiff = factors[1][at] + 2.0 * mu
                layer = depth + 8 * j
                shallowest = (layer == 0) | (layer == NL) | (layer == 2 * NL)
                deepest = (layer == NL - 1) | (layer == 2 * NL - 1)
                for c in range(3):

                    def near(rows):
                        return fields[c][FIRST + 8 * j + rows : FIRST + 8 * j + rows + 8]

                    v = near(0)
                    twice = 2.0 * v
                    above = jnp.where(shallowest, 0.0, near(-1))
                    below = jnp.where(deepest, 0.0, near(1))
                    halo = sides_of[c][at]
                    low = jnp.where(lane == CY - 1, halo, v)
                    high = jnp.where(lane == 0, halo, v)
                    along_first = near(-NL) + near(NL) - twice
                    along_depth = above + below - twice
                    along_second = pltpu.roll(low, 1, 1) + pltpu.roll(high, CY - 1, 1) - twice
                    if c == 0:
                        force = stiff * along_first + mu * (along_depth + along_second)
                    elif c == 1:
                        force = stiff * along_second + mu * (along_first + along_depth)
                    else:
                        force = stiff * along_depth + mu * (along_first + along_second)
                    news.append(twice - olds.pop(0) + force)
                if j % BATCH == BATCH - 1:
                    write_batch(new_fields, j, news)
            return carry

        lax.fori_loop(0, groups, group, 0)
        if not last:
            pack_sides(lambda c, at: prev.at[c, at], sides, (0, 1, 2))

    @pl.when(section != 0)
    def _():
        for c in range(3):
            align_sides(zs, c, lane, sub)
        if linked:
            for h, value in enumerate(edge_addends(sums, REFINE, REFINE - 1)):
                zs[0, h] += zs[1, h] * value
            beside = jnp.broadcast_to(sums[4:5], (8, CY))
            fine_row = jnp.concatenate(
                [
                    jnp.take_along_axis(beside, (((sub + m) * CY + lane) * 6554) >> 16, axis=1)
                    for m in (0, 2)
                ],
                axis=0,
            )

            def add_edge(first):
                for start, rows in ((0, fine_row[0:8]), (8, fine_row[14:16])):
                    at = slice(first + start, first + start + rows.shape[0])
                    full[0, at] += full[2, at] * rows

            @pl.when(p == 0)
            def _():
                add_edge(FIRST + ROWS)

            @pl.when(p != 0)
            def _():
                add_edge(FIRST - REFINE)

        unpack_sides(zs, halos, (0, 2))
        lax.fori_loop(0, groups, widen, 0)
        wet_load.wait()
        if linked:
            for start, fine in fine_addend(addend):
                at = pl.ds(start, 8, stride=REFINE)
                value = cur[0, at] + wet_in[at].astype(F32) * fine
                cur[0, at] = value
                full[0, pl.ds(FIRST + start, 8, stride=REFINE)] = value
        if last:
            wet_out[...] = wet_in[...]

        def group(it, carry):
            load(it).wait()
            sides_of = views_of(it, halos)
            fields, old, new_fields, factors = padded_of(it), views_of(it, prev_in), views_of(it, prev), views_of(it, co)
            wets = wet_in.at[group_rows(it, GROUP)]
            for j in range(BLOCKS):
                if j % BATCH == 0:
                    olds, news = read_batch(old, j), []
                at = slice(8 * j, 8 * j + 8)
                a = factors[0][at]
                b = factors[1][at]
                w = wets[at].astype(F32)

                def near(c, rows):
                    return fields[c][FIRST + 8 * j + rows : FIRST + 8 * j + rows + 8]

                def across(c):
                    v = near(c, 0)
                    low = jnp.where(lane == CY - 1, near(c, -1), v)
                    high = jnp.where(lane == 0, near(c, 1), v)
                    halo = sides_of[c // 2][at]
                    for s in range(8):
                        if (8 * j + s) % REFINE == 0:
                            low = jnp.where((lane == CY - 1) & (sub == s), halo, low)
                        if (8 * j + s) % REFINE == REFINE - 1:
                            high = jnp.where((lane == 0) & (sub == s), halo, high)
                    return pltpu.roll(high, CY - 1, 1) - pltpu.roll(low, 1, 1)

                def down(c):
                    return near(c, REFINE) - near(c, -REFINE)

                news.append(w * (olds.pop(0) - b * (down(1) + across(2))))
                news.append(w * (olds.pop(0) - a * down(0)))
                news.append(w * (olds.pop(0) - a * across(0)))
                if j % BATCH == BATCH - 1:
                    write_batch(new_fields, j, news)
            return carry

        lax.fori_loop(0, groups, group, 0)
        if not last:
            pack_sides(lambda c, at: prev.at[c, at], sides, (0, 2))
            sides[1] = mine[1]

    if last:
        copy = pltpu.make_async_copy(prev, out, sem.at[0])
        copy.start()
        copy.wait()
    else:
        take_edges(section, p, prev, wet_in, xs)
        surface(section, prev.at[2], prev.at[0], surf)
        base[...] = cols[2] * pick(source_pick(cols), surf[...])
    if not linked:
        scale[...] = cols[2]

        @pl.when(section != 0)
        def _():
            surf[0:FINE] = average(lambda m: wet_in[pl.ds(m, FINE, stride=REFINE)].astype(F32))
            scale[...] = cols[2] * pick(source_pick(cols), surf[...])


def fine_addend(addend):
    lane = iota((8, CY), 1)
    for m in range(FINE // 8):
        rows = addend[8 * m : 8 * m + 8]
        for k in range(REFINE):
            fine = jnp.take_along_axis(rows, ((lane + k * CY) * 6554) >> 16, axis=1)
            yield 8 * REFINE * m + k, fine


def last_kernel(final_in, fields, wet, received, final, height, sem):
    section, _, _ = place()
    arrived = arrived_rows(section, received)
    addend = landed(arrived, arrived_sums(arrived))

    @pl.when(section == 0)
    def _():
        copies = []
        for x in range(CX):
            row = NL * x
            first = row // 8 * 8
            height[8 * x : 8 * x + 8] = fields[2, first : first + 8]
            at = 8 * x + row - first
            height[at : at + 1] += addend[x : x + 1]
            copies.append(
                pltpu.make_async_copy(
                    height.at[8 * x : 8 * x + 8], final.at[2, pl.ds(first, 8)], sem.at[x]
                )
            )
        for copy in copies:
            copy.start()
        for copy in copies:
            copy.wait()

    @pl.when(section != 0)
    def _():
        part = 8 * REFINE
        copies = []
        for start, fine in fine_addend(addend):
            at = pl.ds(start, 8, stride=REFINE)
            height[at] = fields[0, at] + wet[at].astype(F32) * fine
            if start % part == REFINE - 1:
                rows = pl.ds(start // part * part, part)
                copies.append(pltpu.make_async_copy(height.at[rows], final.at[0, rows], sem.at[len(copies)]))
                copies[-1].start()
        for copy in copies:
            copy.wait()


def call(kernel, operands, outs, scratch=(), aliases=None, any_inputs=(), any_outs=(), limit=12, cost=4):
    vmem = pl.BlockSpec(memory_space=pltpu.VMEM)
    anywhere = pl.BlockSpec(memory_space=pl.ANY)
    return pl.pallas_call(
        kernel,
        out_shape=[
            (pltpu.VMEM if kept else jax.ShapeDtypeStruct)(shape, kind[0] if kind else F32)
            for shape, kept, *kind in outs
        ],
        in_specs=[anywhere if i in any_inputs else vmem for i in range(len(operands))],
        out_specs=[anywhere if i in any_outs else vmem for i in range(len(outs))],
        scratch_shapes=list(scratch),
        input_output_aliases=aliases or {},
        compiler_params=pltpu.CompilerParams(vmem_limit_bytes=limit * 1024 * 1024),
        cost_estimate=pl.CostEstimate(flops=cost * 10**9, bytes_accessed=cost * 1024 * 1024, transcendentals=0),
    )(*operands)


def keep(value):
    return pltpu.with_memory_space_constraint(value, pltpu.VMEM)


def outside(value):
    return pltpu.with_memory_space_constraint(value, pltpu.HBM)


def on_device(n_gy, owners, state, previous, coeff, wet_mask, link_dest, link_rows, link_weight):
    links = link_weight.size
    pairs = 2 * owners * SLOTS
    vmem = pltpu.VMEM
    dma = pltpu.SemaphoreType.DMA
    field_shape = (3, ROWS, CY)
    sides_shape = (3, 2, 8, CY)
    fields = (field_shape, True)
    edges = ((3, FIRST, CY), False)
    sides_out = (sides_shape, False)
    tiles = ((links, CY), True)
    surf = vmem((CY, CY), F32)
    wet_in = vmem((ROWS, CY), jnp.int32)
    state, previous = state.reshape(field_shape), previous.reshape(field_shape)
    coeff, wet = outside(coeff.reshape(2, ROWS, CY)), outside(wet_mask.reshape(ROWS, CY))

    def exchange(payload):
        payload = payload.reshape(2 * owners, SLOTS, CY)
        payload = lax.all_to_all(payload, ("sec", "gx", "gy"), 0, 0, tiled=True)
        return payload.reshape(pairs, CY)

    dest, rows, weight = link_dest.reshape(1, links), link_rows.reshape(links, 2).T, link_weight.reshape(1, links)
    payload, cols, pcat, cur, prev, xs, sides = call(
        functools.partial(load_kernel, n_gy),
        [outside(x) for x in (state, previous, wet, dest, rows, weight)],
        [
            ((pairs, CY), False), ((4, links, CY), True), ((owners * SLOTS, CY), True), fields, fields,
            edges, sides_out,
        ],
        [
            wet_in, vmem((1, links), jnp.int32), vmem((2, links), jnp.int32),
            vmem((1, links), F32), vmem((8, CY), F32), surf, vmem((owners * SLOTS, CY), F32), dma((9,)),
        ],
        any_inputs=range(6), any_outs=(0,),
    )
    received = exchange(payload)
    swap = [(0, 1), (1, 0)]
    inner = [(i, i ^ 1) for i in range(n_gy)]
    outer = [(i, (i + 1 if i % 2 else i - 1) % n_gy) for i in range(n_gy)]
    before = None
    for step in range(STEPS):
        last = step == STEPS - 1
        xr = lax.ppermute(xs, "gx", swap)
        yra = lax.ppermute(sides, "gy", inner)
        yrb = lax.ppermute(sides, "gy", outer)
        operands = [keep(cur), keep(prev), coeff, wet, keep(cols), xr, yra, yrb, sides]
        if before is not None:
            operands.append(before)
        kernel = functools.partial(step_kernel, n_gy, before is not None, last)
        scratch = [
            vmem(sides_shape, F32), vmem((3, TOTAL, CY), F32), vmem(field_shape, F32), vmem((2, ROWS, CY), F32),
            wet_in, dma((ROWS // GROUP + 1,)),
        ]
        more = dict(aliases={0: 0, 1: 1}, any_inputs=(2, 3), cost=64)
        if last:
            _, new, final, wet_kept = call(
                kernel, operands, [fields, fields, (field_shape, False), ((ROWS, CY), True, jnp.int32)], scratch,
                any_outs=(2,), **more
            )
        else:
            outs = [fields, fields, tiles, edges, sides_out] + [tiles] * (before is None)
            prev, cur, base, xs, sides, *first = call(kernel, operands, outs, scratch + [surf], **more)
            if first:
                scale = first[0]
            payload = call(
                route_kernel, (received, keep(base), keep(scale), keep(cols), keep(pcat)),
                [((pairs, CY), False)], [vmem((owners * SLOTS, CY), F32), dma], any_outs=(0,), limit=4,
            )[0]
            before = received
            received = exchange(payload)
    final = call(
        last_kernel,
        (outside(final), keep(new), keep(wet_kept), received),
        [(field_shape, False)],
        [vmem((ROWS, CY), F32), dma((FINE // 8,))],
        aliases={0: 0}, any_inputs=(0,), any_outs=(0,),
    )[0]
    return final.reshape(1, 3, 1, 1, -1)


def from_partner(value, axis, stride):
    return lax.ppermute(value, axis, [(i, i ^ 1 << stride) for i in range(lax.axis_size(axis))])


def with_halo(block, sides, width):
    for axis, dim in sides:
        count = lax.axis_size(axis)
        forward = [(i, i + 1) for i in range(count - 1)]
        backward = [(target, source) for source, target in forward]
        low = lax.ppermute(
            lax.slice_in_dim(block, block.shape[dim] - width, None, axis=dim), axis, forward
        )
        high = lax.ppermute(lax.slice_in_dim(block, 0, width, axis=dim), axis, backward)
        block = jnp.concatenate([low, block, high], axis=dim)
    return block


def elastic_update(padded, current, previous_field, shear_modulus, lame_first, surface_force):
    own_axis = (0, 2, 1)
    stiffness = lame_first + 2.0 * shear_modulus
    updated_list = []
    for component in range(3):
        displaced = current[component]
        extended = padded[component]
        along_first = extended[2:, :, 1:-1] - 2.0 * displaced + extended[:-2, :, 1:-1]
        deeper = jnp.pad(displaced, ((0, 0), (1, 1), (0, 0)))
        along_depth = deeper[:, 2:, :] - 2.0 * displaced + deeper[:, :-2, :]
        along_second = extended[1:-1, :, 2:] - 2.0 * displaced + extended[1:-1, :, :-2]
        factors = [
            stiffness if own_axis[component] == axis_index else shear_modulus
            for axis_index in range(3)
        ]
        acceleration = (
            factors[0] * along_first + factors[1] * along_depth + factors[2] * along_second
        )
        updated = 2.0 * displaced - previous_field[component] + acceleration
        if component == 2:
            updated = updated.at[:, 0, :].add(surface_force)
        updated_list.append(updated)
    return jnp.stack(updated_list)


def shallow_update(padded, current, previous_field, wave_factor, area_factor, wetness, source):
    fine_rows = REFINE * CX
    fine_cols = REFINE * CY
    sheet = current.reshape(3, fine_rows, fine_cols)
    earlier_sheet = previous_field.reshape(3, fine_rows, fine_cols)
    above = padded[:, 0, (REFINE - 1) * REFINE :, 1:-1].reshape(3, 1, fine_cols)
    below = padded[:, -1, :REFINE, 1:-1].reshape(3, 1, fine_cols)
    left_side = padded[:, 1:-1, REFINE - 1 :: REFINE, 0].reshape(3, fine_rows, 1)
    right_side = padded[:, 1:-1, 0::REFINE, -1].reshape(3, fine_rows, 1)
    by_rows = jnp.concatenate([above, sheet, below], axis=1)
    by_columns = jnp.concatenate([left_side, sheet, right_side], axis=2)

    def rows_diff(channel):
        return by_rows[channel, 2:, :] - by_rows[channel, :-2, :]

    def columns_diff(channel):
        return by_columns[channel, :, 2:] - by_columns[channel, :, :-2]

    flux_first = wetness * (earlier_sheet[1] - wave_factor * rows_diff(0))
    flux_second = wetness * (earlier_sheet[2] - wave_factor * columns_diff(0))
    height = wetness * (earlier_sheet[0] - area_factor * (rows_diff(1) + columns_diff(2)) + source)
    return jnp.stack([height, flux_first, flux_second]).reshape(3, CX, NL, CY)


def route(payload):
    tile_data, tile_rows = payload
    width = tile_data.shape[-1]
    received_data, received_rows = (
        lax.all_to_all(tile_data, ("gx", "gy"), split_axis=0, concat_axis=0, tiled=True),
        lax.all_to_all(tile_rows, ("gx", "gy"), split_axis=0, concat_axis=0, tiled=True),
    )
    return (received_data.reshape(-1, width), received_rows.reshape(-1))


def deliver(outgoing, send_rows):
    crossed = from_partner((outgoing, send_rows), "sec", 0)
    return route(crossed)


def general_on_device(state, previous, coeff, wet_mask, link_dest, link_rows, link_weight):
    section = lax.axis_index("sec")
    owners = lax.axis_size("gx") * lax.axis_size("gy")
    fine_rows = REFINE * CX
    fine_cols = REFINE * CY
    current = state[0, :, 0, 0].reshape(3, CX, NL, CY)
    earlier = previous[0, :, 0, 0].reshape(3, CX, NL, CY)
    first_factor = coeff[0, 0, 0, 0]
    second_factor = coeff[0, 1, 0, 0]
    wetness = wet_mask[0, 0].reshape(fine_rows, fine_cols).astype(jnp.float32)
    targets = link_dest.reshape(-1)
    pairs = link_rows.reshape(-1, 2)
    source_rows = pairs[:, 0]
    landing = pairs[:, 1]
    weights = link_weight.reshape(-1)
    one_hot = (targets[:, None] == jnp.arange(owners, dtype=jnp.int32)[None, :]).astype(jnp.int32)
    before = jnp.cumsum(one_hot, axis=0) - one_hot
    slot_index = jnp.sum(before * one_hot, axis=1)
    position = targets * CAP + slot_index
    send_rows = jnp.zeros((owners * CAP,), jnp.int32).at[position].set(landing).reshape(owners, CAP)
    for step_index in range(STEPS):
        padded = with_halo(current, (("gx", 1), ("gy", 3)), 1)

        def elastic_rows():
            return current[2, :, 0, :][source_rows]

        def shallow_rows():
            picked_fine = current[0].reshape(fine_rows, fine_cols)[source_rows]
            return jnp.sum(picked_fine.reshape(-1, CY, REFINE), axis=-1) / REFINE

        picked = lax.cond(section == 0, elastic_rows, shallow_rows)
        outgoing = (
            jnp.zeros((owners * CAP, CY), jnp.float32).at[position].set(picked * weights[:, None])
        )
        outgoing = outgoing.reshape(owners, CAP, CY)
        arrived, arrived_rows = deliver(outgoing, send_rows)

        def elastic_branch():
            surface_force = jnp.zeros((CX, CY), jnp.float32).at[arrived_rows].add(arrived)
            return elastic_update(
                padded,
                current,
                earlier,
                first_factor.reshape(CX, NL, CY),
                second_factor.reshape(CX, NL, CY),
                surface_force,
            )

        def shallow_branch():
            coarse_source = jnp.zeros((fine_rows, CY), jnp.float32).at[arrived_rows].add(arrived)
            source = jnp.repeat(coarse_source, REFINE, axis=1)
            return shallow_update(
                padded,
                current,
                earlier,
                first_factor.reshape(fine_rows, fine_cols),
                second_factor.reshape(fine_rows, fine_cols),
                wetness,
                source,
            )

        updated = lax.cond(section == 0, elastic_branch, shallow_branch)
        earlier, current = (current, updated)
    return current.reshape(1, 3, 1, 1, -1)


def solution(mesh):
    placed = (
        P("sec", None, "gx", "gy", None),
        P("sec", None, "gx", "gy", None),
        P("sec", None, "gx", "gy", None),
        P("gx", "gy", None),
        P("sec", "gx", "gy", None, None),
        P("sec", "gx", "gy", None, None),
        P("sec", "gx", "gy", None),
    )
    n_gx, n_gy = mesh.shape["gx"], mesh.shape["gy"]
    owners = n_gx * n_gy
    device_program = general_on_device
    if n_gx == 2 and n_gy & (n_gy - 1) == 0 and owners * SLOTS == CY:
        device_program = functools.partial(on_device, n_gy, owners)
    return jax.shard_map(
        device_program,
        mesh=mesh,
        in_specs=placed,
        out_specs=P("sec", None, "gx", "gy", None),
        check_vma=False,
    )
```

```python
import functools

import jax
import jax.numpy as jnp
from jax import lax
from jax.experimental import pallas as pl
from jax.experimental.pallas import tpu as pltpu
from jax.sharding import PartitionSpec as P

CX = 8
CY = 128
REFINE = 10
NL = 100
STEPS = 4
CAP = 4
FINE = REFINE * CX
ROWS = CX * NL
FIRST = 104
TOTAL = FIRST + ROWS + FIRST
SLOTS = 8
BLOCKS = 25
BATCH = 5
GROUP = 8 * BLOCKS
HALF = ROWS // 16
F32 = jnp.float32


def split(x):
    high = x.astype(jnp.bfloat16)
    return high, (x - high.astype(F32)).astype(jnp.bfloat16)


def pick(mask, x):
    parts = jnp.concatenate(split(x), axis=1)
    wide = jnp.dot(mask.astype(jnp.bfloat16), parts, preferred_element_type=F32)
    return wide[:, 0 : x.shape[1]] + wide[:, x.shape[1] :]


def spread(x, mask):
    tall = jnp.dot(jnp.concatenate(split(x), axis=0), mask, preferred_element_type=F32)
    return tall[0 : x.shape[0]] + tall[x.shape[0] :]


def iota(shape, dim):
    return lax.broadcasted_iota(jnp.int32, shape, dim)


def one(mask):
    return jnp.where(mask, 1.0, 0.0).astype(F32)


def place():
    return lax.axis_index("sec"), lax.axis_index("gx"), lax.axis_index("gy")


def average(rows_of):
    total = jnp.zeros((FINE, CY), F32)
    for m in range(REFINE):
        fine = iota((CY, CY), 0) + m * CY
        first = iota((CY, CY), 1) * REFINE
        mask = one((fine >= first) & (fine < first + REFINE)).astype(jnp.bfloat16)
        total = total + spread(rows_of(m), mask)
    return total / REFINE


def surface(section, elastic, sheet, surf):
    surf[...] = jnp.zeros_like(surf)

    @pl.when(section == 0)
    def _():
        surf[0:CX] = elastic[pl.ds(0, CX, stride=NL)]

    @pl.when(section != 0)
    def _():
        surf[0:FINE] = average(lambda m: sheet[pl.ds(m, FINE, stride=REFINE)])


def source_pick(cols):
    return one(cols[0] == iota((cols.shape[1], CY), 1).astype(F32))


def outgoing(section, tiles, cols, pcat, packed, payload, sem):
    half = packed.shape[0]
    lanes = tiles.shape
    last = jnp.broadcast_to(tiles[:, CY - 1 : CY], lanes) * cols[1]
    first = jnp.broadcast_to(tiles[:, 0:1], lanes) * cols[1]
    packed[...] = pick(pcat[...], jnp.concatenate([tiles, last, first, cols[3]], axis=0))
    there = payload.at[pl.ds(pl.multiple_of((1 - section) * half, 8), half)]
    copy = pltpu.make_async_copy(packed, there, sem)
    copy.start()
    return copy


def link_tables(section, me, n_gy, dest, rows, weight, lines, cols, pcat):
    links = dest.shape[1]
    lines[...] = jnp.zeros_like(lines)
    lines[0:1, 0:links] = dest[...].astype(F32)
    lines[1:3, 0:links] = rows[...].astype(F32)
    lines[3:4, 0:links] = weight[...]
    x = lines[...]
    eye = one(iota((links, CY), 0) == iota((links, CY), 1))

    def column(i):
        return jnp.sum(eye * x[i : i + 1], axis=1, keepdims=True)

    target, source, landing, weights = [column(i) for i in range(4)]
    same = one(target == x[0:1])
    at = iota((links, CY), 0)
    other = iota((links, CY), 1)
    inside = one(other < links)
    slot_row = jnp.sum(same * one(at < other) * inside, axis=0, keepdims=True)
    slot = jnp.sum(same * one(other < at) * inside, axis=1, keepdims=True)
    lane = other.astype(F32)
    cols[0] = jnp.broadcast_to(source, (links, CY))
    cols[1] = one(landing == lane)
    cols[2] = jnp.broadcast_to(weights, (links, CY))
    cols[3] = landing * one(lane == slot + (me * SLOTS).astype(F32))
    y = jnp.concatenate([x[0:3], slot_row, jnp.zeros((4, CY), F32)], axis=0)
    y = y + pltpu.roll(y, links, 1) + pltpu.roll(y, 2 * links, 1) + pltpu.roll(y, 3 * links, 1)
    shape = (pcat.shape[0], CY)
    owner = iota(shape, 0) >> 3
    part = iota(shape, 0) & 7
    group = iota(shape, 1) >> (links.bit_length() - 1)
    to = y[0:1]
    row = y[2:3]
    order = y[3:4]
    beside = jnp.where(owner < n_gy, owner + n_gy, owner - n_gy).astype(F32)
    bottom = jnp.where(section == 0, FINE - 1, CX - 1).astype(F32)
    edge = jnp.where(owner < n_gy, 0.0, bottom)
    along = owner & (n_gy - 1)
    own = owner.astype(F32)
    chosen = one((group == 0) & (part == order.astype(jnp.int32)) & (part < CAP) & (to == own))
    chosen += one((group == 0) & (part == 4) & (to == beside) & (row == edge))
    chosen += one((group == 1) & (part == 6) & (to == own - 1.0) & (along > 0))
    chosen += one((group == 2) & (part == 7) & (to == own + 1.0) & (along < n_gy - 1))
    chosen += one((group == 3) & (part == 5) & (to == own))
    pcat[...] = chosen


def pack_sides(values_of, sides, channels):
    lane = iota((8, CY), 1)

    def half_of(h, carry):
        acc = {c: jnp.zeros((8, CY), F32) for c in channels}
        views = {c: values_of(c, pl.ds(pl.multiple_of(h * HALF * 8, 8), HALF * 8)) for c in channels}
        for b in range(HALF):
            for c in channels:
                value = views[c][8 * b : 8 * b + 8].astype(F32)
                acc[c] = jnp.where(lane >> 1 == b, pltpu.roll(value, 2 * b + 1, 1), acc[c])
        for c in channels:
            sides[c, h] = acc[c]
        return carry

    lax.fori_loop(0, 2, half_of, 0)


def unpack_sides(zs, halos, channels):
    def half_of(h, carry):
        for i, c in enumerate(channels):
            value = zs[c, h]
            view = halos.at[i, pl.ds(pl.multiple_of(h * HALF * 8, 8), HALF * 8)]
            for b in range(HALF):
                view[8 * b : 8 * b + 8] = pltpu.roll(value, CY - 1 - 2 * b, 1)
        return carry

    lax.fori_loop(0, 2, half_of, 0)


def take_edges(section, p, fields, wet, xs):
    start = pl.multiple_of(jnp.where(p == 0, ROWS - FIRST, 0), 8)
    for c in range(3):
        xs[c] = fields[c, pl.ds(start, FIRST)]

    @pl.when(section != 0)
    def _():
        xs[2] = wet[pl.ds(start, FIRST)].astype(F32)


def load_kernel(n_gy, state, previous, wet, dest, rows, weight, payload, cols, pcat, cur, prev, xs, sides, wet_in, dest_in, rows_in, weight_in, lines, surf, packed, sem):
    section, p, q = place()
    linked = 2 * (1 - section)
    pairs = [(dest, dest_in), (rows, rows_in), (weight, weight_in)]
    pairs += [(state.at[c], cur.at[c]) for c in (linked, 1, 2 - linked)]
    pairs += [(wet, wet_in), (previous, prev)]
    copies = [pltpu.make_async_copy(a, b, sem.at[i]) for i, (a, b) in enumerate(pairs)]
    for copy in copies[0:7]:
        copy.start()
    for copy in copies[0:3]:
        copy.wait()
    link_tables(section, p * n_gy + q, n_gy, dest_in, rows_in, weight_in, lines, cols, pcat)
    copies[3].wait()
    copies[7].start()
    surface(section, cur.at[2], cur.at[0], surf)
    tiles = cols[2] * pick(source_pick(cols), surf[...])
    copies.append(outgoing(section, tiles, cols, pcat, packed, payload, sem.at[8]))
    for copy in copies[4:7]:
        copy.wait()

    @pl.when(section == 0)
    def _():
        pack_sides(lambda c, at: cur.at[c, at], sides, (0, 1, 2))

    @pl.when(section != 0)
    def _():
        pack_sides(lambda c, at: wet_in.at[at] if c == 1 else cur.at[c, at], sides, (0, 1, 2))

    take_edges(section, p, cur, wet_in, xs)
    for copy in copies[7:]:
        copy.wait()


def group_rows(it, rows):
    return pl.ds(pl.multiple_of(it * GROUP, 8), rows)


def arrived_rows(section, received):
    half = received.shape[0] // 2
    return received[pl.ds(pl.multiple_of((1 - section) * half, 8), half)]


def arrived_sums(arrived):
    return jnp.sum(arrived.reshape(-1, SLOTS, CY), axis=0)


def landed(arrived, sums):
    mine = iota((CY, arrived.shape[0]), 1)
    return pick(one((iota(mine.shape, 0).astype(F32) == sums[5:6]) & ((mine & 7) < CAP)), arrived)


def route_kernel(received, base, scale, cols, pcat, payload, packed, sem):
    section, _, _ = place()
    arrived = arrived_rows(section, received)
    landing = arrived_sums(arrived)[5:6]
    lane = iota(cols.shape[1:], 1)
    gather = one((cols[0] == landing) & ((lane & 7) < CAP))
    tiles = base[...] + scale[...] * pick(gather, arrived)
    outgoing(section, tiles, cols, pcat, packed, payload, sem).wait()


def edge_addends(sums, period, offset):
    masks, values = [], []
    lane = iota((CY, 2 * CY), 1)
    block = ((lane & (CY - 1)) >> 1) + jnp.where(lane >= CY, HALF, 0)
    inside = (lane & (CY - 1)) < 2 * HALF
    for side, shift in ((0, 0), (1, offset)):
        at = iota(lane.shape, 0) * period + shift - block * 8
        masks.append(one((at >= 0) & (at < 8) & ((lane & 1) == side) & inside).astype(jnp.bfloat16))
        sub = (iota((16, CY), 1) * period + shift) & 7
        row = jnp.broadcast_to(sums[6 + side : 7 + side], (16, CY))
        values.append(jnp.where(sub == iota((16, CY), 0), row, 0.0))
    wide = spread(values[0], masks[0]) + spread(values[1], masks[1])
    return wide[0:8, 0:CY], wide[0:8, CY:]


def align_sides(zs, c, lane, sub):
    first, second = zs[c, 0], zs[c, 1]
    top = 2 * HALF
    low_first = jnp.where(lane == top - 2, pltpu.roll(second, top - 2, 1), pltpu.roll(first, CY - 2, 1))
    low_second = pltpu.roll(second, CY - 2, 1)
    high_first = pltpu.roll(first, 2, 1)
    high_second = jnp.where(lane == 1, pltpu.roll(first, CY + 2 - top, 1), pltpu.roll(second, 2, 1))
    for h, (low, high) in enumerate(((low_first, high_first), (low_second, high_second))):
        zs[c, h] = jnp.where(lane & 1 == 0, pltpu.roll(low, 7, 0), pltpu.roll(high, 1, 0))


def read_batch(fields, j):
    return [fields[c][8 * i : 8 * i + 8] for i in range(j, j + BATCH) for c in range(3)]


def write_batch(fields, j, values):
    for n, value in enumerate(values):
        i = j + 1 - BATCH + n // 3
        fields[n % 3][8 * i : 8 * i + 8] = value


def step_kernel(n_gy, linked, last, *refs):
    cur_in, prev_in, coeff, wet, cols, xr, yra, yrb, mine, *refs = refs
    if linked:
        received, *refs = refs
    cur, prev, *refs = refs
    if last:
        out, wet_out, zs, full, halos, co, wet_in, sem = refs
    else:
        base, xs, sides, *refs = refs
        if not linked:
            scale, *refs = refs
        zs, full, halos, co, wet_in, sem, surf = refs
    section, p, q = place()
    lane = iota((8, CY), 1)
    sub = iota((8, CY), 0)
    even_lane = lane & 1 == 0
    groups = ROWS // GROUP
    wet_load = pltpu.make_async_copy(wet, wet_in, sem.at[groups])

    def load(it):
        at = group_rows(it, GROUP)
        return pltpu.make_async_copy(coeff.at[:, at], co.at[:, at], sem.at[it])

    @pl.when(section != 0)
    def _():
        wet_load.start()

    for it in range(groups):
        load(it).start()

    within = (q > 0) & (q < n_gy - 1)

    @pl.when((q & 1) == 1)
    def _():
        for c in range(3):
            for h in range(2):
                zs[c, h] = jnp.where(even_lane, yra[c, h], jnp.where(within, yrb[c, h], 0.0))

    @pl.when((q & 1) == 0)
    def _():
        for c in range(3):
            for h in range(2):
                zs[c, h] = jnp.where(even_lane, jnp.where(within, yrb[c, h], 0.0), yra[c, h])

    there = pl.multiple_of(jnp.where(p == 0, FIRST + ROWS, 0), 8)
    nowhere = pl.multiple_of(jnp.where(p == 0, 0, FIRST + ROWS), 8)
    for c in range(3):
        full[c, pl.ds(there, FIRST)] = xr[c]
        full[c, pl.ds(nowhere, FIRST)] = jnp.zeros((FIRST, CY), F32)

    if linked:
        arrived = arrived_rows(section, received)
        sums = arrived_sums(arrived)
        addend = landed(arrived, sums)
    def widen(it, carry):
        for c in range(3):
            view = full.at[c, group_rows(it, FIRST + GROUP)]
            view[FIRST : FIRST + GROUP] = cur[c, group_rows(it, GROUP)]
        return carry

    if last:

        @pl.when(section == 0)
        def _():
            wet_out[...] = jnp.zeros_like(wet_out)

    def views_of(it, ref):
        return [ref.at[c, group_rows(it, GROUP)] for c in range(ref.shape[0])]

    def padded_of(it):
        return [full.at[c, group_rows(it, GROUP + 2 * FIRST)] for c in range(3)]

    @pl.when(section == 0)
    def _():
        if linked:
            for x in range(CX):
                cur[2, NL * x : NL * x + 1] += addend[x : x + 1]

            @pl.when(p == 0)
            def _():
                full[2, FIRST + ROWS : FIRST + ROWS + 1] += sums[4:5]

            @pl.when(p != 0)
            def _():
                full[2, FIRST - NL : FIRST - NL + 1] += sums[4:5]

            for h, value in enumerate(edge_addends(sums, NL, 0)):
                zs[2, h] += value

        lax.fori_loop(0, groups, widen, 0)
        unpack_sides(zs, halos, (0, 1, 2))

        def group(it, carry):
            load(it).wait()
            sides_of = views_of(it, halos)
            depth = it * GROUP - NL * ((it * GROUP * 656) >> 16) + sub
            fields, old, new_fields, factors = padded_of(it), views_of(it, prev_in), views_of(it, prev), views_of(it, co)
            for j in range(BLOCKS):
                if j % BATCH == 0:
                    olds, news = read_batch(old, j), []
                at = slice(8 * j, 8 * j + 8)
                mu = factors[0][at]
                stiff = factors[1][at] + 2.0 * mu
                layer = depth + 8 * j
                shallowest = (layer == 0) | (layer == NL) | (layer == 2 * NL)
                deepest = (layer == NL - 1) | (layer == 2 * NL - 1)
                for c in range(3):

                    def near(rows):
                        return fields[c][FIRST + 8 * j + rows : FIRST + 8 * j + rows + 8]

                    v = near(0)
                    twice = 2.0 * v
                    above = jnp.where(shallowest, 0.0, near(-1))
                    below = jnp.where(deepest, 0.0, near(1))
                    halo = sides_of[c][at]
                    low = jnp.where(lane == CY - 1, halo, v)
                    high = jnp.where(lane == 0, halo, v)
                    along_first = near(-NL) + near(NL) - twice
                    along_depth = above + below - twice
                    along_second = pltpu.roll(low, 1, 1) + pltpu.roll(high, CY - 1, 1) - twice
                    if c == 0:
                        force = stiff * along_first + mu * (along_depth + along_second)
                    elif c == 1:
                        force = stiff * along_second + mu * (along_first + along_depth)
                    else:
                        force = stiff * along_depth + mu * (along_first + along_second)
                    news.append(twice - olds.pop(0) + force)
                if j % BATCH == BATCH - 1:
                    write_batch(new_fields, j, news)
            return carry

        lax.fori_loop(0, groups, group, 0)
        if not last:
            pack_sides(lambda c, at: prev.at[c, at], sides, (0, 1, 2))

    @pl.when(section != 0)
    def _():
        for c in range(3):
            align_sides(zs, c, lane, sub)
        if linked:
            for h, value in enumerate(edge_addends(sums, REFINE, REFINE - 1)):
                zs[0, h] += zs[1, h] * value
            beside = jnp.broadcast_to(sums[4:5], (8, CY))
            fine_row = jnp.concatenate(
                [
                    jnp.take_along_axis(beside, (((sub + m) * CY + lane) * 6554) >> 16, axis=1)
                    for m in (0, 2)
                ],
                axis=0,
            )

            def add_edge(first):
                for start, rows in ((0, fine_row[0:8]), (8, fine_row[14:16])):
                    at = slice(first + start, first + start + rows.shape[0])
                    full[0, at] += full[2, at] * rows

            @pl.when(p == 0)
            def _():
                add_edge(FIRST + ROWS)

            @pl.when(p != 0)
            def _():
                add_edge(FIRST - REFINE)

        unpack_sides(zs, halos, (0, 2))
        lax.fori_loop(0, groups, widen, 0)
        wet_load.wait()
        if linked:
            for start, fine in fine_addend(addend):
                at = pl.ds(start, 8, stride=REFINE)
                value = cur[0, at] + wet_in[at].astype(F32) * fine
                cur[0, at] = value
                full[0, pl.ds(FIRST + start, 8, stride=REFINE)] = value
        if last:
            wet_out[...] = wet_in[...]

        def group(it, carry):
            load(it).wait()
            sides_of = views_of(it, halos)
            fields, old, new_fields, factors = padded_of(it), views_of(it, prev_in), views_of(it, prev), views_of(it, co)
            wets = wet_in.at[group_rows(it, GROUP)]
            for j in range(BLOCKS):
                if j % BATCH == 0:
                    olds, news = read_batch(old, j), []
                at = slice(8 * j, 8 * j + 8)
                a = factors[0][at]
                b = factors[1][at]
                w = wets[at].astype(F32)

                def near(c, rows):
                    return fields[c][FIRST + 8 * j + rows : FIRST + 8 * j + rows + 8]

                def across(c):
                    v = near(c, 0)
                    low = jnp.where(lane == CY - 1, near(c, -1), v)
                    high = jnp.where(lane == 0, near(c, 1), v)
                    halo = sides_of[c // 2][at]
                    for s in range(8):
                        if (8 * j + s) % REFINE == 0:
                            low = jnp.where((lane == CY - 1) & (sub == s), halo, low)
                        if (8 * j + s) % REFINE == REFINE - 1:
                            high = jnp.where((lane == 0) & (sub == s), halo, high)
                    return pltpu.roll(high, CY - 1, 1) - pltpu.roll(low, 1, 1)

                def down(c):
                    return near(c, REFINE) - near(c, -REFINE)

                news.append(w * (olds.pop(0) - b * (down(1) + across(2))))
                news.append(w * (olds.pop(0) - a * down(0)))
                news.append(w * (olds.pop(0) - a * across(0)))
                if j % BATCH == BATCH - 1:
                    write_batch(new_fields, j, news)
            return carry

        lax.fori_loop(0, groups, group, 0)
        if not last:
            pack_sides(lambda c, at: prev.at[c, at], sides, (0, 2))
            sides[1] = mine[1]

    if last:
        copy = pltpu.make_async_copy(prev, out, sem.at[0])
        copy.start()
        copy.wait()
    else:
        take_edges(section, p, prev, wet_in, xs)
        surface(section, prev.at[2], prev.at[0], surf)
        base[...] = cols[2] * pick(source_pick(cols), surf[...])
    if not linked:
        scale[...] = cols[2]

        @pl.when(section != 0)
        def _():
            surf[0:FINE] = average(lambda m: wet_in[pl.ds(m, FINE, stride=REFINE)].astype(F32))
            scale[...] = cols[2] * pick(source_pick(cols), surf[...])


def fine_addend(addend):
    lane = iota((8, CY), 1)
    sources = [((lane + k * CY) * 6554) >> 16 for k in range(REFINE)]
    for m in range(FINE // 8):
        rows = addend[8 * m : 8 * m + 8]
        for k in range(REFINE):
            fine = jnp.take_along_axis(rows, sources[k], axis=1)
            yield 8 * REFINE * m + k, fine


def last_kernel(final_in, fields, wet, received, final, height, sem):
    section, _, _ = place()
    arrived = arrived_rows(section, received)
    addend = landed(arrived, arrived_sums(arrived))

    @pl.when(section == 0)
    def _():
        copies = []
        for x in range(CX):
            row = NL * x
            first = row // 8 * 8
            height[8 * x : 8 * x + 8] = fields[2, first : first + 8]
            at = 8 * x + row - first
            height[at : at + 1] += addend[x : x + 1]
            copies.append(
                pltpu.make_async_copy(
                    height.at[8 * x : 8 * x + 8], final.at[2, pl.ds(first, 8)], sem.at[x]
                )
            )
        for copy in copies:
            copy.start()
        for copy in copies:
            copy.wait()

    @pl.when(section != 0)
    def _():
        part = 8 * REFINE
        copies = []
        for start, fine in fine_addend(addend):
            at = pl.ds(start, 8, stride=REFINE)
            height[at] = fields[0, at] + wet[at].astype(F32) * fine
            if start % part == REFINE - 1:
                rows = pl.ds(start // part * part, part)
                copies.append(pltpu.make_async_copy(height.at[rows], final.at[0, rows], sem.at[len(copies)]))
                copies[-1].start()
        for copy in copies:
            copy.wait()


def call(kernel, operands, outs, scratch=(), aliases=None, any_inputs=(), any_outs=(), limit=12, cost=4):
    vmem = pl.BlockSpec(memory_space=pltpu.VMEM)
    anywhere = pl.BlockSpec(memory_space=pl.ANY)
    return pl.pallas_call(
        kernel,
        out_shape=[
            (pltpu.VMEM if kept else jax.ShapeDtypeStruct)(shape, kind[0] if kind else F32)
            for shape, kept, *kind in outs
        ],
        in_specs=[anywhere if i in any_inputs else vmem for i in range(len(operands))],
        out_specs=[anywhere if i in any_outs else vmem for i in range(len(outs))],
        scratch_shapes=list(scratch),
        input_output_aliases=aliases or {},
        compiler_params=pltpu.CompilerParams(vmem_limit_bytes=limit * 1024 * 1024),
        cost_estimate=pl.CostEstimate(flops=cost * 10**9, bytes_accessed=cost * 1024 * 1024, transcendentals=0),
    )(*operands)


def keep(value):
    return pltpu.with_memory_space_constraint(value, pltpu.VMEM)


def outside(value):
    return pltpu.with_memory_space_constraint(value, pltpu.HBM)


def on_device(n_gy, owners, state, previous, coeff, wet_mask, link_dest, link_rows, link_weight):
    links = link_weight.size
    pairs = 2 * owners * SLOTS
    vmem = pltpu.VMEM
    dma = pltpu.SemaphoreType.DMA
    field_shape = (3, ROWS, CY)
    sides_shape = (3, 2, 8, CY)
    fields = (field_shape, True)
    edges = ((3, FIRST, CY), False)
    sides_out = (sides_shape, False)
    tiles = ((links, CY), True)
    surf = vmem((CY, CY), F32)
    wet_in = vmem((ROWS, CY), jnp.int32)
    state, previous = state.reshape(field_shape), previous.reshape(field_shape)
    coeff, wet = outside(coeff.reshape(2, ROWS, CY)), outside(wet_mask.reshape(ROWS, CY))

    def exchange(payload):
        payload = payload.reshape(2 * owners, SLOTS, CY)
        payload = lax.all_to_all(payload, ("sec", "gx", "gy"), 0, 0, tiled=True)
        return payload.reshape(pairs, CY)

    dest, rows, weight = link_dest.reshape(1, links), link_rows.reshape(links, 2).T, link_weight.reshape(1, links)
    payload, cols, pcat, cur, prev, xs, sides = call(
        functools.partial(load_kernel, n_gy),
        [outside(x) for x in (state, previous, wet, dest, rows, weight)],
        [
            ((pairs, CY), False), ((4, links, CY), True), ((owners * SLOTS, CY), True), fields, fields,
            edges, sides_out,
        ],
        [
            wet_in, vmem((1, links), jnp.int32), vmem((2, links), jnp.int32),
            vmem((1, links), F32), vmem((8, CY), F32), surf, vmem((owners * SLOTS, CY), F32), dma((9,)),
        ],
        any_inputs=range(6), any_outs=(0,),
    )
    received = exchange(payload)
    swap = [(0, 1), (1, 0)]
    inner = [(i, i ^ 1) for i in range(n_gy)]
    outer = [(i, (i + 1 if i % 2 else i - 1) % n_gy) for i in range(n_gy)]
    before = None
    for step in range(STEPS):
        last = step == STEPS - 1
        xr = lax.ppermute(xs, "gx", swap)
        yra = lax.ppermute(sides, "gy", inner)
        yrb = lax.ppermute(sides, "gy", outer)
        operands = [keep(cur), keep(prev), coeff, wet, keep(cols), xr, yra, yrb, sides]
        if before is not None:
            operands.append(before)
        kernel = functools.partial(step_kernel, n_gy, before is not None, last)
        scratch = [
            vmem(sides_shape, F32), vmem((3, TOTAL, CY), F32), vmem(field_shape, F32), vmem((2, ROWS, CY), F32),
            wet_in, dma((ROWS // GROUP + 1,)),
        ]
        more = dict(aliases={0: 0, 1: 1}, any_inputs=(2, 3), cost=64)
        if last:
            _, new, final, wet_kept = call(
                kernel, operands, [fields, fields, (field_shape, False), ((ROWS, CY), True, jnp.int32)], scratch,
                any_outs=(2,), **more
            )
        else:
            outs = [fields, fields, tiles, edges, sides_out] + [tiles] * (before is None)
            prev, cur, base, xs, sides, *first = call(kernel, operands, outs, scratch + [surf], **more)
            if first:
                scale = first[0]
            payload = call(
                route_kernel, (received, keep(base), keep(scale), keep(cols), keep(pcat)),
                [((pairs, CY), False)], [vmem((owners * SLOTS, CY), F32), dma], any_outs=(0,), limit=4,
            )[0]
            before = received
            received = exchange(payload)
    final = call(
        last_kernel,
        (outside(final), keep(new), keep(wet_kept), received),
        [(field_shape, False)],
        [vmem((ROWS, CY), F32), dma((FINE // 8,))],
        aliases={0: 0}, any_inputs=(0,), any_outs=(0,),
    )[0]
    return final.reshape(1, 3, 1, 1, -1)


def from_partner(value, axis, stride):
    return lax.ppermute(value, axis, [(i, i ^ 1 << stride) for i in range(lax.axis_size(axis))])


def with_halo(block, sides, width):
    for axis, dim in sides:
        count = lax.axis_size(axis)
        forward = [(i, i + 1) for i in range(count - 1)]
        backward = [(target, source) for source, target in forward]
        low = lax.ppermute(
            lax.slice_in_dim(block, block.shape[dim] - width, None, axis=dim), axis, forward
        )
        high = lax.ppermute(lax.slice_in_dim(block, 0, width, axis=dim), axis, backward)
        block = jnp.concatenate([low, block, high], axis=dim)
    return block


def elastic_update(padded, current, previous_field, shear_modulus, lame_first, surface_force):
    own_axis = (0, 2, 1)
    stiffness = lame_first + 2.0 * shear_modulus
    updated_list = []
    for component in range(3):
        displaced = current[component]
        extended = padded[component]
        along_first = extended[2:, :, 1:-1] - 2.0 * displaced + extended[:-2, :, 1:-1]
        deeper = jnp.pad(displaced, ((0, 0), (1, 1), (0, 0)))
        along_depth = deeper[:, 2:, :] - 2.0 * displaced + deeper[:, :-2, :]
        along_second = extended[1:-1, :, 2:] - 2.0 * displaced + extended[1:-1, :, :-2]
        factors = [
            stiffness if own_axis[component] == axis_index else shear_modulus
            for axis_index in range(3)
        ]
        acceleration = (
            factors[0] * along_first + factors[1] * along_depth + factors[2] * along_second
        )
        updated = 2.0 * displaced - previous_field[component] + acceleration
        if component == 2:
            updated = updated.at[:, 0, :].add(surface_force)
        updated_list.append(updated)
    return jnp.stack(updated_list)


def shallow_update(padded, current, previous_field, wave_factor, area_factor, wetness, source):
    fine_rows = REFINE * CX
    fine_cols = REFINE * CY
    sheet = current.reshape(3, fine_rows, fine_cols)
    earlier_sheet = previous_field.reshape(3, fine_rows, fine_cols)
    above = padded[:, 0, (REFINE - 1) * REFINE :, 1:-1].reshape(3, 1, fine_cols)
    below = padded[:, -1, :REFINE, 1:-1].reshape(3, 1, fine_cols)
    left_side = padded[:, 1:-1, REFINE - 1 :: REFINE, 0].reshape(3, fine_rows, 1)
    right_side = padded[:, 1:-1, 0::REFINE, -1].reshape(3, fine_rows, 1)
    by_rows = jnp.concatenate([above, sheet, below], axis=1)
    by_columns = jnp.concatenate([left_side, sheet, right_side], axis=2)

    def rows_diff(channel):
        return by_rows[channel, 2:, :] - by_rows[channel, :-2, :]

    def columns_diff(channel):
        return by_columns[channel, :, 2:] - by_columns[channel, :, :-2]

    flux_first = wetness * (earlier_sheet[1] - wave_factor * rows_diff(0))
    flux_second = wetness * (earlier_sheet[2] - wave_factor * columns_diff(0))
    height = wetness * (earlier_sheet[0] - area_factor * (rows_diff(1) + columns_diff(2)) + source)
    return jnp.stack([height, flux_first, flux_second]).reshape(3, CX, NL, CY)


def route(payload):
    tile_data, tile_rows = payload
    width = tile_data.shape[-1]
    received_data, received_rows = (
        lax.all_to_all(tile_data, ("gx", "gy"), split_axis=0, concat_axis=0, tiled=True),
        lax.all_to_all(tile_rows, ("gx", "gy"), split_axis=0, concat_axis=0, tiled=True),
    )
    return (received_data.reshape(-1, width), received_rows.reshape(-1))


def deliver(outgoing, send_rows):
    crossed = from_partner((outgoing, send_rows), "sec", 0)
    return route(crossed)


def general_on_device(state, previous, coeff, wet_mask, link_dest, link_rows, link_weight):
    section = lax.axis_index("sec")
    owners = lax.axis_size("gx") * lax.axis_size("gy")
    fine_rows = REFINE * CX
    fine_cols = REFINE * CY
    current = state[0, :, 0, 0].reshape(3, CX, NL, CY)
    earlier = previous[0, :, 0, 0].reshape(3, CX, NL, CY)
    first_factor = coeff[0, 0, 0, 0]
    second_factor = coeff[0, 1, 0, 0]
    wetness = wet_mask[0, 0].reshape(fine_rows, fine_cols).astype(jnp.float32)
    targets = link_dest.reshape(-1)
    pairs = link_rows.reshape(-1, 2)
    source_rows = pairs[:, 0]
    landing = pairs[:, 1]
    weights = link_weight.reshape(-1)
    one_hot = (targets[:, None] == jnp.arange(owners, dtype=jnp.int32)[None, :]).astype(jnp.int32)
    before = jnp.cumsum(one_hot, axis=0) - one_hot
    slot_index = jnp.sum(before * one_hot, axis=1)
    position = targets * CAP + slot_index
    send_rows = jnp.zeros((owners * CAP,), jnp.int32).at[position].set(landing).reshape(owners, CAP)
    for step_index in range(STEPS):
        padded = with_halo(current, (("gx", 1), ("gy", 3)), 1)

        def elastic_rows():
            return current[2, :, 0, :][source_rows]

        def shallow_rows():
            picked_fine = current[0].reshape(fine_rows, fine_cols)[source_rows]
            return jnp.sum(picked_fine.reshape(-1, CY, REFINE), axis=-1) / REFINE

        picked = lax.cond(section == 0, elastic_rows, shallow_rows)
        outgoing = (
            jnp.zeros((owners * CAP, CY), jnp.float32).at[position].set(picked * weights[:, None])
        )
        outgoing = outgoing.reshape(owners, CAP, CY)
        arrived, arrived_rows = deliver(outgoing, send_rows)

        def elastic_branch():
            surface_force = jnp.zeros((CX, CY), jnp.float32).at[arrived_rows].add(arrived)
            return elastic_update(
                padded,
                current,
                earlier,
                first_factor.reshape(CX, NL, CY),
                second_factor.reshape(CX, NL, CY),
                surface_force,
            )

        def shallow_branch():
            coarse_source = jnp.zeros((fine_rows, CY), jnp.float32).at[arrived_rows].add(arrived)
            source = jnp.repeat(coarse_source, REFINE, axis=1)
            return shallow_update(
                padded,
                current,
                earlier,
                first_factor.reshape(fine_rows, fine_cols),
                second_factor.reshape(fine_rows, fine_cols),
                wetness,
                source,
            )

        updated = lax.cond(section == 0, elastic_branch, shallow_branch)
        earlier, current = (current, updated)
    return current.reshape(1, 3, 1, 1, -1)


def solution(mesh):
    placed = (
        P("sec", None, "gx", "gy", None),
        P("sec", None, "gx", "gy", None),
        P("sec", None, "gx", "gy", None),
        P("gx", "gy", None),
        P("sec", "gx", "gy", None, None),
        P("sec", "gx", "gy", None, None),
        P("sec", "gx", "gy", None),
    )
    n_gx, n_gy = mesh.shape["gx"], mesh.shape["gy"]
    owners = n_gx * n_gy
    device_program = general_on_device
    if n_gx == 2 and n_gy & (n_gy - 1) == 0 and owners * SLOTS == CY:
        device_program = functools.partial(on_device, n_gy, owners)
    return jax.shard_map(
        device_program,
        mesh=mesh,
        in_specs=placed,
        out_specs=P("sec", None, "gx", "gy", None),
        check_vma=False,
    )
```
